32 devices in a mesh: dp: 4 (over y, x), tile: 8 (over z, core).
Axes of the slice: x: 2, y: 2, z: 4, core: 2. Of those that a mesh axis runs over, the one named last changes fastest.
Arguments:
- features: bfloat16 [4, 8, 8, 16, 1024], P('dp', 'tile'), may hold values from -6 to 6
- cotangent: bfloat16 [4, 8, 8, 16, 1024], P('dp', 'tile'), may hold values from -6 to 6
- in_weight: bfloat16 [3072, 1024], P(('dp', 'tile')), may hold values from -0.1875 to 0.1875
- out_weight: bfloat16 [3072, 1024], P(('dp', 'tile')), may hold values from -0.109375 to 0.109375
- hidden_bias: bfloat16 [3072], P(('dp', 'tile')), may hold values from -3 to 3
- kernel: float32 [49, 1024], P(None, 'dp'), may hold values from -0.875 to 0.875
- conv_bias: float32 [1024], P('dp'), may hold values from -3 to 3
- norm_gain: float32 [1024], P('dp'), may hold values from 0.5 to 1.5
- norm_bias: float32 [1024], P('dp'), may hold values from -3 to 3
- layer_scale: float32 [1024], P('dp'), may hold values from 0.5 to 1.5
- out_bias: float32 [1024], P('dp'), may hold values from -3 to 3
Outputs:
- block_out: bfloat16 [4, 8, 8, 16, 1024], P('dp', 'tile')
- grad_input: bfloat16 [4, 8, 8, 16, 1024], P('dp', 'tile')
- grad_kernel: float32 [49, 1024], P(None, 'dp')
- grad_conv_bias: float32 [1024], P('dp')
- grad_norm_gain: float32 [1024], P('dp')
- grad_norm_bias: float32 [1024], P('dp')
- grad_layer_scale: float32 [1024], P('dp')
The draws below stay inside these ranges and needn't reach their ends.
All inputs are finite; a program needn't handle non-finite values.
Results may differ from the reference program's by a relative error of at most 0.0061.
Values may be sent and summed in bfloat16 or wider, within the bound.
No kernel may reach another device: no remote copies, remote signals or barrier semaphores. Data moves between devices by JAX's collectives and lax.ppermute only.
A program may use at most 128 MiB of HBM per device.

```python
import math
import jax
import jax.numpy as jnp
from jax import lax

D = 1024
FF = 3072
KS = 7
GX = 4
TH = 8
TW = 16
KK = 49
IMAGES = 4
TILES = 8
PIXELS = 4096


def raised(entries, rng, source, target, blocks, factor):
    owner, partner = [(jnp.arange(entries.shape[dim]) // (entries.shape[dim] // blocks)).reshape([-1 if axis == dim else 1 for axis in range(entries.ndim)]) for dim in (source, target)]
    chosen = jax.random.permutation(rng, blocks)[partner]
    strong = (owner == chosen) | (owner == (partner + blocks // 2) % blocks)
    return jnp.where(strong, factor * entries, entries)


def block_scale(stream_key, dims, cuts, low, top_value):
    def one(position, parts):
        steps = jax.random.uniform(jax.random.fold_in(jax.random.fold_in(stream_key, 6), position), (parts,), jnp.float32, low / len(cuts), top_value / len(cuts))
        return jnp.repeat(jnp.exp(steps), dims[position] // parts).reshape((-1,) + (1,) * (len(dims) - position - 1))

    loudness = one(*cuts[0])
    for cut in cuts[1:]:
        loudness = loudness * one(*cut)
    return loudness


def noise(stream_key, extent, deviation, limit, pieces=(), kind=jnp.bfloat16):
    entries = deviation * jax.random.normal(stream_key, extent, jnp.float32)
    if pieces:
        entries = entries * block_scale(stream_key, extent, pieces, -0.22, 0.18)
    return jnp.clip(entries, -limit, limit).astype(kind)


def noise_with(key, shape, deviation, bound, cuts, heavy, dtype=jnp.bfloat16):
    entries = deviation * jax.random.normal(key, shape, jnp.float32)
    if cuts:
        entries = entries * block_scale(key, shape, cuts, -0.22, 0.18)
    return jnp.clip(raised(entries, jax.random.fold_in(key, 3), *heavy), -bound, bound).astype(dtype)


def setup_inputs(seed: int = 0) -> dict:
    seeds = jax.random.split(jax.random.key(seed), 12)
    return {
        "features": noise(seeds[0], (IMAGES, TILES, TH, TW, D), 1.0, 6.0, ((0, 4), (1, 8))),
        "cotangent": noise_with(seeds[1], (IMAGES, TILES, TH, TW, D), 1.0, 6.0, ((0, 4), (1, 8)), (1, 4, 8, 2.0)),
        "in_weight": noise(seeds[2], (FF, D), D ** -0.5, 0.1875, ((0, 32),)),
        "out_weight": noise(seeds[3], (FF, D), FF ** -0.5, 0.109375, ((0, 32),)),
        "hidden_bias": noise(seeds[4], (FF,), 0.5, 3.0, ((0, 32),)),
        "kernel": noise(seeds[5], (KK, D), KK ** -0.5, 0.875, ((1, 4),), jnp.float32),
        "conv_bias": noise(seeds[6], (D,), 0.5, 3.0, ((0, 4),), jnp.float32),
        "norm_gain": jnp.clip(0.5 + 1.0 * jax.random.uniform(seeds[7], (D,), jnp.float32) ** block_scale(seeds[7], (D,), ((0, 4),), -0.2, 0.2), 0.5, 1.5),
        "norm_bias": noise(seeds[8], (D,), 0.5, 3.0, ((0, 4),), jnp.float32),
        "layer_scale": jnp.clip(0.5 + 1.0 * jax.random.uniform(seeds[9], (D,), jnp.float32) ** block_scale(seeds[9], (D,), ((0, 4),), -0.2, 0.2), 0.5, 1.5),
        "out_bias": noise(seeds[10], (D,), 0.5, 3.0, ((0, 4),), jnp.float32),
    }


def gelu_exact(values):
    return 0.5 * values * (1.0 + jax.scipy.special.erf(values * 0.7071067811865476))

def gelu_slope(values):
    return 0.5 * (1.0 + jax.scipy.special.erf(values * 0.7071067811865476)) + values * jnp.exp(-0.5 * values * values) * 0.3989422804014327

def reference(features, cotangent, in_weight, out_weight, hidden_bias, kernel, conv_bias, norm_gain, norm_bias, layer_scale, out_bias):
    grid_rows = TILES // GX
    margin = KS // 2
    height = grid_rows * TH
    breadth = GX * TW

    def to_image(tiled):
        shaped = tiled.reshape(IMAGES, grid_rows, GX, TH, TW, D)
        return shaped.transpose(0, 1, 3, 2, 4, 5).reshape(IMAGES, height, breadth, D)

    def to_tiles(whole):
        shaped = whole.reshape(IMAGES, grid_rows, TH, GX, TW, D)
        return shaped.transpose(0, 1, 3, 2, 4, 5).reshape(IMAGES, TILES, TH, TW, D)

    def one_image(pair):
        picture, upper = pair
        source = picture.astype(jnp.float32)
        padded = jnp.pad(source, ((margin, margin), (margin, margin), (0, 0)))
        convolved = jnp.zeros((height, breadth, D), jnp.float32) + conv_bias
        for tap_row in range(KS):
            for tap_col in range(KS):
                convolved = convolved + kernel[tap_row * KS + tap_col] * padded[tap_row:tap_row + height, tap_col:tap_col + breadth]
        average = lax.optimization_barrier(jnp.mean(convolved, axis=-1, keepdims=True))
        centered = convolved - average
        variance = lax.optimization_barrier(jnp.mean(centered * centered, axis=-1, keepdims=True))
        inverse = lax.rsqrt(variance + 1e-06)
        standard = (centered * inverse).reshape(height * breadth, D)
        inverse = inverse.reshape(height * breadth, 1)
        normed = (standard * norm_gain + norm_bias).astype(jnp.bfloat16)
        pre = jnp.dot(normed, in_weight.T, preferred_element_type=jnp.float32) + hidden_bias.astype(jnp.float32)
        hidden = gelu_exact(pre).astype(jnp.bfloat16)
        projected = jnp.dot(hidden, out_weight, preferred_element_type=jnp.float32) + out_bias
        flat_source = source.reshape(height * breadth, D)
        block = (flat_source + layer_scale * projected).astype(jnp.bfloat16)
        upstream = upper.astype(jnp.float32).reshape(height * breadth, D)
        scale_part = lax.optimization_barrier(jnp.sum(upstream * projected, axis=0))
        back_out = (upstream * layer_scale).astype(jnp.bfloat16)
        back_hidden = jnp.dot(back_out, out_weight.T, preferred_element_type=jnp.float32)
        back_pre = (back_hidden * gelu_slope(pre)).astype(jnp.bfloat16)
        back_normed = jnp.dot(back_pre, in_weight, preferred_element_type=jnp.float32)
        gain_part = lax.optimization_barrier(jnp.sum(back_normed * standard, axis=0))
        nbias_part = lax.optimization_barrier(jnp.sum(back_normed, axis=0))
        scaled = back_normed * norm_gain
        back_conv = inverse * (scaled - lax.optimization_barrier(jnp.mean(scaled, axis=-1, keepdims=True)) - standard * lax.optimization_barrier(jnp.mean(scaled * standard, axis=-1, keepdims=True)))
        cbias_part = lax.optimization_barrier(jnp.sum(back_conv, axis=0))
        back_grid = back_conv.reshape(height, breadth, D)
        back_wire = lax.optimization_barrier(back_grid.astype(jnp.bfloat16)).astype(jnp.float32)
        back_padded = jnp.pad(back_wire, ((margin, margin), (margin, margin), (0, 0)))
        grad_grid = upstream.reshape(height, breadth, D)
        kernel_rows = []
        for tap_row in range(KS):
            for tap_col in range(KS):
                tap = kernel[tap_row * KS + tap_col]
                grad_grid = grad_grid + tap * back_padded[2 * margin - tap_row:2 * margin - tap_row + height, 2 * margin - tap_col:2 * margin - tap_col + breadth]
                kernel_rows.append(lax.optimization_barrier(jnp.sum(back_grid * padded[tap_row:tap_row + height, tap_col:tap_col + breadth], axis=(0, 1))))
        vectors = jnp.stack([cbias_part, gain_part, nbias_part, scale_part])
        return (block.reshape(height, breadth, D), grad_grid.astype(jnp.bfloat16), jnp.stack(kernel_rows), vectors)
    blocks, grads, kernel_parts, vector_parts = lax.map(one_image, (to_image(features), to_image(cotangent)))
    factor = 1.0 / math.sqrt(PIXELS)
    kernel_total = lax.optimization_barrier(jnp.sum(kernel_parts, axis=0)) * factor
    vector_total = lax.optimization_barrier(jnp.sum(vector_parts, axis=0)) * factor
    return (to_tiles(blocks), to_tiles(grads), kernel_total, vector_total[0], vector_total[1], vector_total[2], vector_total[3])
```

```python
import math

import jax
import jax.numpy as jnp
from jax import lax
from jax.experimental import pallas as pl
from jax.experimental.pallas import tpu as pltpu
from jax.sharding import PartitionSpec as P

KS = 7
GX = 4
MARGIN = KS // 2
LANES = 128
PITCH = 32
INSET = 8
TAP_ROWS = 56
BIAS_ROWS = 8
F32 = jnp.float32
BF16 = jnp.bfloat16

VMEM = pl.BlockSpec(memory_space=pltpu.VMEM)


def call(body, outs, scratch, args, flops=0, size=0, aliases=None, limit=32):
    return pl.pallas_call(
        body,
        out_shape=outs,
        in_specs=[VMEM] * len(args),
        out_specs=[VMEM] * len(outs),
        scratch_shapes=scratch,
        input_output_aliases=aliases or {},
        compiler_params=pltpu.CompilerParams(vmem_limit_bytes=limit * 1024 * 1024),
        cost_estimate=pl.CostEstimate(flops=flops, bytes_accessed=size, transcendentals=0),
    )(*args)


def shape(dims, kind):
    return jax.ShapeDtypeStruct(dims, kind)


def lane_tile(tile):
    return slice(tile * LANES, (tile + 1) * LANES)


def grid_place():
    place = lax.axis_index("tile")
    return place // GX, place % GX


def swap_rows(sends):
    count = lax.axis_size("tile")
    grid_rows = count // GX
    moved = []
    for first, block in enumerate(sends):
        route = []
        for place in range(count):
            row = place // GX
            if row % 2 == first and row + 1 < grid_rows:
                route += [(place, place + GX), (place + GX, place)]
        moved.append(lax.ppermute(block, "tile", route))
    return moved


def swap_cols(sends):
    count = lax.axis_size("tile")
    moved = []
    for first, block in enumerate(sends):
        route = []
        for place in range(count):
            col = place % GX
            if col % 2 == first and col + 1 < GX:
                route += [(place, place + 1), (place + 1, place)]
        moved.append(lax.ppermute(block, "tile", route))
    return moved


def row_pairings():
    return 1 if lax.axis_size("tile") // GX == 2 else 2


def above_below(bands, tile):
    row, _ = grid_place()
    even = row % 2 == 0
    first = bands[0][:, lane_tile(tile)].astype(F32)
    second = bands[1][:, lane_tile(tile)].astype(F32) if len(bands) > 1 else jnp.zeros_like(first)
    return jnp.where(even, second, first), jnp.where(even, first, second)


def border_columns(field, bands, rows, cols):
    width = field.shape[1]
    tall = rows + 2 * MARGIN
    packed = -(-tall * MARGIN // 16) * 16

    def body(field_ref, *refs):
        band_refs = refs[: len(bands)]
        outs, full, left, right = refs[len(bands) : -3], refs[-3], refs[-2], refs[-1]
        _, col = grid_place()
        even = col % 2 == 0
        left[...] = jnp.zeros_like(left)
        right[...] = jnp.zeros_like(right)
        for tile in range(width // LANES):
            above, below = above_below(band_refs, tile)
            full[: MARGIN * cols] = above
            full[MARGIN * cols : (MARGIN + rows) * cols] = field_ref[:, lane_tile(tile)].astype(F32)
            full[(MARGIN + rows) * cols :] = below
            for row in range(tall):
                here = pl.ds(row * MARGIN, MARGIN)
                left[here] = full[pl.ds(row * cols, MARGIN)]
                right[here] = full[pl.ds(row * cols + cols - MARGIN, MARGIN)]
            toward_left, toward_right = left[...], right[...]
            outs[0][:, lane_tile(tile)] = jnp.where(even, toward_right, toward_left).astype(BF16)
            outs[1][:, lane_tile(tile)] = jnp.where(even, toward_left, toward_right).astype(BF16)

    return call(
        body,
        [shape((packed, width), BF16)] * 2,
        [pltpu.VMEM((tall * cols, LANES), F32)] + [pltpu.VMEM((packed, LANES), F32)] * 2,
        [field, *bands],
        flops=200000,
        size=600000,
        limit=8,
    )


def fill_padded(padded, edge, field_ref, band_refs, side_refs, rows, cols):
    width = field_ref.shape[1]
    tall = rows + 2 * MARGIN
    _, col = grid_place()
    even = col % 2 == 0
    for tile in range(width // LANES):
        above, below = above_below(band_refs, tile)
        for row in range(MARGIN):
            source = slice(row * cols, (row + 1) * cols)
            padded[tile, pl.ds(row * PITCH + INSET, cols)] = above[source]
            padded[tile, pl.ds((MARGIN + rows + row) * PITCH + INSET, cols)] = below[source]
        for row in range(rows):
            padded[tile, pl.ds((MARGIN + row) * PITCH + INSET, cols)] = field_ref[
                row * cols : (row + 1) * cols, lane_tile(tile)
            ].astype(F32)
        first = side_refs[0][:, lane_tile(tile)].astype(F32)
        second = side_refs[1][:, lane_tile(tile)].astype(F32)
        edge[0] = jnp.where(even, second, first)
        edge[1] = jnp.where(even, first, second)
        for row in range(tall):
            padded[tile, pl.ds(row * PITCH + INSET - MARGIN, MARGIN)] = edge[0, pl.ds(row * MARGIN, MARGIN)]
            padded[tile, pl.ds(row * PITCH + INSET + cols, MARGIN)] = edge[1, pl.ds(row * MARGIN, MARGIN)]


def window(padded, tile, row, shift, cols):
    return padded[tile, pl.ds(row * PITCH + INSET - MARGIN + shift, cols), :]


def tap_sums(padded, tile, taps, sums, rows, cols, flipped):
    for b in range(KS):
        for r in range(rows + 2 * MARGIN):
            pixels = window(padded, tile, r, b, cols)
            for a in range(KS):
                if 0 <= r - a < rows:
                    index = (KS - 1 - a) * KS + KS - 1 - b if flipped else a * KS + b
                    sums[r - a] = sums[r - a] + taps[index] * pixels
    return sums


def forward(field, bands, sides, params, upstream, rows, cols):
    pixels, width = field.shape
    tiles = width // LANES
    span = (rows + 2 * MARGIN) * PITCH

    def body(*refs):
        field_ref = refs[0]
        band_refs = refs[1 : 1 + len(bands)]
        side_refs = refs[1 + len(bands) : 3 + len(bands)]
        params_ref, up_ref, acts, standard, inverse, padded, edge = refs[3 + len(bands) :]
        fill_padded(padded, edge, field_ref, band_refs, side_refs, rows, cols)

        @pl.loop(0, tiles)
        def _(tile):
            taps = [params_ref[tile, pl.ds(t, 1), :] for t in range(KS * KS)]
            start = jnp.broadcast_to(params_ref[tile, pl.ds(KS * KS, 1), :], (cols, LANES))
            sums = tap_sums(padded, tile, taps, [start] * rows, rows, cols, False)
            for row in range(rows):
                standard[tile, pl.ds(row * cols, cols), :] = sums[row]

        total = standard[0]
        for tile in range(1, tiles):
            total = total + standard[tile]
        average = jnp.sum(total, axis=1, keepdims=True) * (1.0 / width)
        total = jnp.zeros((pixels, LANES), F32)
        for tile in range(tiles):
            centered = standard[tile] - average
            total = total + centered * centered
        scale = lax.rsqrt(jnp.sum(total, axis=1, keepdims=True) * (1.0 / width) + 1e-06)
        inverse[...] = jnp.broadcast_to(scale, (pixels, LANES))
        for tile in range(tiles):
            value = (standard[tile] - average) * scale
            standard[tile] = value
            gain = params_ref[tile, KS * KS + 1 : KS * KS + 2, :]
            shift = params_ref[tile, KS * KS + 2 : KS * KS + 3, :]
            layer = params_ref[tile, KS * KS + 3 : KS * KS + 4, :]
            acts[:pixels, lane_tile(tile)] = (value * gain + shift).astype(BF16)
            acts[pixels:, lane_tile(tile)] = (up_ref[:, lane_tile(tile)].astype(F32) * layer).astype(BF16)

    return call(
        body,
        [
            shape((2 * pixels, width), BF16),
            shape((tiles, pixels, LANES), F32),
            shape((pixels, LANES), F32),
            shape((tiles, span, LANES), F32),
        ],
        [pltpu.VMEM((2, sides[0].shape[0], LANES), F32)],
        [field, *bands, *sides, params, upstream],
        flops=30000000,
        size=4000000,
        limit=16,
    )


def mlp_part(own, peer, in_parts, out_parts, biases, before, last):
    twice, width = own.shape
    pixels = twice // 2
    units = sum(part[2] for part in in_parts)
    arrays = []

    def slot(array):
        for index, known in enumerate(arrays):
            if known is array:
                return index
        arrays.append(array)
        return len(arrays) - 1

    in_slots = [(slot(a), first, count) for a, first, count in in_parts]
    out_slots = [(slot(a), first, count) for a, first, count in out_parts]
    bias_slots = [(slot(a), row, count) for a, row, count in biases]
    step = 32

    def body(*refs):
        own_ref, peer_ref = refs[:2]
        parts = refs[2 : 2 + len(arrays)]
        rest = refs[2 + len(arrays) :]
        if before is not None:
            sums_in, rest = rest[:2], rest[2:]
        outs, (norm, back, win, wout, pre, slope, hid, bpre) = rest[:-8], rest[-8:]
        norm[:pixels] = own_ref[:pixels]
        norm[pixels:] = peer_ref[:pixels]
        back[:pixels] = own_ref[pixels:]
        back[pixels:] = peer_ref[pixels:]
        for target, slots in ((win, in_slots), (wout, out_slots)):
            at = 0
            for index, first, count in slots:
                target[at : at + count] = parts[index][first : first + count]
                at += count
        row = jnp.concatenate(
            [parts[i][r : r + 1, :count].astype(F32) for i, r, count in bias_slots], axis=1
        )
        across = (((1,), (1,)), ((), ()))
        pre[...] = lax.dot_general(norm[...], win[...], across, preferred_element_type=F32) + row
        slope[...] = lax.dot_general(back[...], wout[...], across, preferred_element_type=F32)

        @pl.loop(0, twice // step)
        def _(part):
            here = pl.ds(pl.multiple_of(part * step, step), step)
            value = pre[here, :]
            half = 0.5 * (1.0 + lax.erf(value * 0.7071067811865476))
            hid[here, :] = (value * half).astype(BF16)
            bell = jnp.exp(-0.5 * value * value) * 0.3989422804014327
            bpre[here, :] = (slope[here, :] * (half + value * bell)).astype(BF16)

        projected = jnp.dot(hid[...], wout[...], preferred_element_type=F32)
        if before is not None:
            projected = projected + sums_in[0][...]
        if last:
            outs[0][:pixels] = projected[:pixels]
            outs[1][:pixels] = projected[pixels:].astype(BF16)
        else:
            outs[0][...] = projected
        normed = jnp.dot(bpre[...], win[...], preferred_element_type=F32)
        if before is not None:
            normed = normed + sums_in[1][...]
        if last:
            outs[0][pixels:] = normed[:pixels]
            outs[1][pixels:] = normed[pixels:].astype(BF16)
        else:
            outs[1][...] = normed

    args = [own, peer, *arrays] + (list(before) if before is not None else [])
    return call(
        body,
        [shape((twice, width), F32), shape((twice, width), BF16 if last else F32)],
        [
            pltpu.VMEM((twice, width), BF16),
            pltpu.VMEM((twice, width), BF16),
            pltpu.VMEM((units, width), BF16),
            pltpu.VMEM((units, width), BF16),
            pltpu.VMEM((twice, units), F32),
            pltpu.VMEM((twice, units), F32),
            pltpu.VMEM((twice, units), BF16),
            pltpu.VMEM((twice, units), BF16),
        ],
        args,
        flops=8 * twice * units * width,
        size=4 * units * width + 16 * twice * width,
        limit=24,
    )


def norm_backward(own, peer, standard, inverse, params, field, upstream, rows, cols):
    pixels, width = field.shape
    tiles = width // LANES
    strip = MARGIN * cols

    def body(own_ref, peer_ref, std, inv, params_ref, field_ref, up_ref, conv, wire, block, vectors, *sends):
        zero = jnp.zeros((pixels, LANES), F32)
        plain, mixed = zero, zero
        for tile in range(tiles):
            lanes = lane_tile(tile)
            normed = own_ref[pixels:, lanes] + peer_ref[pixels:, lanes].astype(F32)
            gain = params_ref[tile, KS * KS + 1 : KS * KS + 2, :]
            scaled = normed * gain
            product = normed * std[tile]
            conv[tile] = scaled
            plain = plain + scaled
            mixed = mixed + product * gain
            vectors[tile] = jnp.zeros((8, LANES), F32)
            vectors[tile, 1:2, :] = jnp.sum(product, axis=0, keepdims=True)
            vectors[tile, 2:3, :] = jnp.sum(normed, axis=0, keepdims=True)
        plain = jnp.sum(plain, axis=1, keepdims=True) * (1.0 / width)
        mixed = jnp.sum(mixed, axis=1, keepdims=True) * (1.0 / width)
        for tile in range(tiles):
            value = inv[...] * (conv[tile] - plain - std[tile] * mixed)
            conv[tile] = value
            wire[:, lane_tile(tile)] = value.astype(BF16)
            vectors[tile, 0:1, :] = jnp.sum(value, axis=0, keepdims=True)
        row, _ = grid_place()
        even = row % 2 == 0
        top, bottom = wire[:strip, :], wire[pixels - strip :, :]
        sends[0][...] = jnp.where(even, bottom, top)
        if len(sends) > 1:
            sends[1][...] = jnp.where(even, top, bottom)
        for tile in range(tiles):
            lanes = lane_tile(tile)
            out_bias = params_ref[tile, KS * KS + 4 : KS * KS + 5, :]
            layer = params_ref[tile, KS * KS + 3 : KS * KS + 4, :]
            projected = own_ref[:pixels, lanes] + peer_ref[:pixels, lanes].astype(F32) + out_bias
            block[:, lanes] = (field_ref[:, lanes].astype(F32) + layer * projected).astype(BF16)
            vectors[tile, 3:4, :] = jnp.sum(up_ref[:, lanes].astype(F32) * projected, axis=0, keepdims=True)

    return call(
        body,
        [
            shape((tiles, pixels, LANES), F32),
            shape((pixels, width), BF16),
            shape((pixels, width), BF16),
            shape((tiles, 8, LANES), F32),
        ]
        + [shape((strip, width), BF16)] * row_pairings(),
        [],
        [own, peer, standard, inverse, params, field, upstream],
        flops=3000000,
        size=5000000,
        limit=16,
    )


def kernel_gradient(padded, back_conv, vectors, rows, cols):
    tiles = back_conv.shape[0]

    def body(padded_ref, conv, vectors_ref, out):
        @pl.loop(0, tiles)
        def _(tile):
            grads = [conv[tile, pl.ds(row * cols, cols), :] for row in range(rows)]
            for b in range(KS):
                sums = [None] * KS
                for r in range(rows + 2 * MARGIN):
                    pixels = window(padded_ref, tile, r, b, cols)
                    for a in range(KS):
                        if 0 <= r - a < rows:
                            term = pixels * grads[r - a]
                            sums[a] = term if sums[a] is None else sums[a] + term
                for a in range(KS):
                    out[tile, pl.ds(a * KS + b, 1), :] = jnp.sum(sums[a], axis=0, keepdims=True)
            out[tile, pl.ds(KS * KS, TAP_ROWS - KS * KS), :] = vectors_ref[tile, : TAP_ROWS - KS * KS, :]

    return call(
        body,
        [shape((tiles, TAP_ROWS, LANES), F32)],
        [],
        [padded, back_conv, vectors],
        flops=15000000,
        size=3000000,
        limit=8,
    )[0]


def input_gradient(wire, bands, sides, params, upstream, rows, cols):
    pixels, width = wire.shape
    tiles = width // LANES
    span = (rows + 2 * MARGIN) * PITCH

    def body(*refs):
        wire_ref = refs[0]
        band_refs = refs[1 : 1 + len(bands)]
        side_refs = refs[1 + len(bands) : 3 + len(bands)]
        params_ref, up_ref, out, padded, edge = refs[3 + len(bands) :]
        fill_padded(padded, edge, wire_ref, band_refs, side_refs, rows, cols)

        @pl.loop(0, tiles)
        def _(tile):
            lanes = pl.ds(pl.multiple_of(tile * LANES, LANES), LANES)
            taps = [params_ref[tile, pl.ds(t, 1), :] for t in range(KS * KS)]
            start = [up_ref[pl.ds(row * cols, cols), lanes].astype(F32) for row in range(rows)]
            sums = tap_sums(padded, tile, taps, start, rows, cols, True)
            for row in range(rows):
                out[pl.ds(row * cols, cols), lanes] = sums[row].astype(BF16)

    return call(
        body,
        [shape((pixels, width), BF16)],
        [pltpu.VMEM((tiles, span, LANES), F32), pltpu.VMEM((2, sides[0].shape[0], LANES), F32)],
        [wire, *bands, *sides, params, upstream],
        flops=15000000,
        size=1500000,
        limit=16,
    )[0]


def across(block, bits):
    groups = lax.axis_size("dp")
    return lax.ppermute(block, "dp", [(i, i ^ bits) for i in range(groups)])


def ring(block):
    count = lax.axis_size("tile")
    chips = count // 2
    return lax.ppermute(
        block, "tile", [(i, (i // 2 + 1) % chips * 2 + i % 2) for i in range(count)]
    )


def tile_swap(block, bits):
    return lax.ppermute(block, "tile", [(i, i ^ bits) for i in range(lax.axis_size("tile"))])


def gather_params(pack):
    groups = lax.axis_size("dp")
    rows, own = pack.shape
    if own % LANES or groups & (groups - 1):
        whole = lax.all_gather(pack, "dp", axis=1, tiled=True)
        return whole.reshape(rows, -1, LANES).transpose(1, 0, 2)
    here = pack.reshape(rows, own // LANES, LANES).transpose(1, 0, 2)
    me = lax.axis_index("dp")
    pieces = jnp.stack([here] + [across(here, bits) for bits in range(1, groups)])
    return jnp.concatenate(
        [lax.dynamic_index_in_dim(pieces, me ^ source, 0, keepdims=False) for source in range(groups)]
    )


def sum_params(parts, own):
    groups = lax.axis_size("dp")
    tiles, rows, _ = parts.shape
    if own % LANES or groups & (groups - 1):
        flat = parts.transpose(1, 0, 2).reshape(rows, -1)
        return lax.psum(lax.psum_scatter(flat, "dp", scatter_dimension=1, tiled=True), "tile")
    me = lax.axis_index("dp")
    count = own // LANES
    total = lax.dynamic_slice_in_dim(parts, me * count, count, 0)
    moved = [
        across(lax.dynamic_slice_in_dim(parts, (me ^ bits) * count, count, 0), bits)
        for bits in range(1, groups)
    ]
    for block in moved:
        total = total + block
    bits = 1
    while bits < lax.axis_size("tile"):
        total = total + tile_swap(total, bits)
        bits *= 2
    return total.transpose(1, 0, 2).reshape(rows, own)


def weight_shares(in_weight, out_weight, hidden_bias):
    units, width = in_weight.shape
    groups, count = lax.axis_size("dp"), lax.axis_size("tile")
    if units % 16 or groups != 4 or units > width:
        core = lax.axis_index("tile") % 2

        def mine(array):
            whole = lax.all_gather(array, ("dp", "tile"), axis=0, tiled=True)
            whole = whole.reshape((groups * count // 2, 2, units) + array.shape[1:])
            return lax.dynamic_index_in_dim(whole, core, 1, keepdims=False).reshape(
                (-1,) + array.shape[1:]
            )

        rows_in, rows_out, bias = mine(in_weight), mine(out_weight), mine(hidden_bias)
        part = rows_in.shape[0] // 4
        shares = []
        for at in range(0, 4 * part, part):
            shares.append(
                (
                    [(rows_in[at : at + part], 0, part)],
                    [(rows_out[at : at + part], 0, part)],
                    [(bias[at : at + part].reshape(1, part), 0, part)],
                )
            )
        return shares
    row = jnp.pad(hidden_bias.reshape(1, units), ((0, BIAS_ROWS - 1), (0, width - units)))
    held = jnp.concatenate([in_weight, out_weight, row])
    shares = []
    for step in range(count // 2):
        onward = ring(held) if step + 1 < count // 2 else None
        first, second = across(held, 1), across(held, 2)
        far_in = across(first[:units], 2)
        far_out = across(second[units:], 1)
        shares.append(
            (
                [(held, 0, units), (first, 0, units), (second, 0, units), (far_in, 0, units)],
                [(held, units, units), (first, units, units), (second, units, units), (far_out, 0, units)],
                [(held, 2 * units, units), (first, 2 * units, units), (second, 2 * units, units), (far_out, units, units)],
            )
        )
        held = onward
    return shares


def per_device(
    features,
    cotangent,
    in_weight,
    out_weight,
    hidden_bias,
    kernel,
    conv_bias,
    norm_gain,
    norm_bias,
    layer_scale,
    out_bias,
):
    image_count, _, rows, cols, width = features.shape
    groups, count = lax.axis_size("dp"), lax.axis_size("tile")
    pixels = rows * cols
    own = kernel.shape[1]
    strip = MARGIN * cols
    shares = weight_shares(in_weight, out_weight, hidden_bias)

    vectors = [v.reshape(1, own) for v in (conv_bias, norm_gain, norm_bias, layer_scale, out_bias)]
    pack = jnp.concatenate([kernel, *vectors, jnp.zeros((TAP_ROWS - KS * KS - 5, own), F32)])
    params = gather_params(pack)

    field = features.reshape(pixels, width)
    upstream = cotangent.reshape(pixels, width)
    row, _ = grid_place()
    sends = [
        lax.dynamic_slice_in_dim(field, (1 - (row + first) % 2) * (pixels - strip), strip, 0)
        for first in range(row_pairings())
    ]
    bands = swap_rows(sends)
    sides = swap_cols(border_columns(field, bands, rows, cols))
    acts, standard, inverse, padded = forward(field, bands, sides, params, upstream, rows, cols)
    peer_acts = tile_swap(acts, 1)

    sums = None
    for index, share in enumerate(shares):
        sums = mlp_part(acts, peer_acts, *share, sums, index + 1 == len(shares))
    mine, theirs = sums
    back_conv, wire, block, vector_parts, *back_sends = norm_backward(
        mine, tile_swap(theirs, 1), standard, inverse, params, field, upstream, rows, cols
    )
    back_bands = swap_rows(back_sends)
    parts = kernel_gradient(padded, back_conv, vector_parts, rows, cols)
    back_sides = swap_cols(border_columns(wire, back_bands, rows, cols))
    grad = input_gradient(wire, back_bands, back_sides, params, upstream, rows, cols)
    factor = 1.0 / math.sqrt(image_count * groups * count * pixels)
    sums = sum_params(parts, own) * factor
    taps = KS * KS
    return (
        block.reshape(features.shape),
        grad.reshape(features.shape),
        sums[:taps],
        sums[taps],
        sums[taps + 1],
        sums[taps + 2],
        sums[taps + 3],
    )


def solution(mesh):
    placed = (
        P("dp", "tile", None, None, None),
        P("dp", "tile", None, None, None),
        P(("dp", "tile"), None),
        P(("dp", "tile"), None),
        P(("dp", "tile")),
        P(None, "dp"),
        P("dp"),
        P("dp"),
        P("dp"),
        P("dp"),
        P("dp"),
    )
    return jax.shard_map(
        per_device,
        mesh=mesh,
        in_specs=placed,
        out_specs=(
            P("dp", "tile", None, None, None),
            P("dp", "tile", None, None, None),
            P(None, "dp"),
            P("dp"),
            P("dp"),
            P("dp"),
            P("dp"),
        ),
        check_vma=False,
    )
```

```python
import math

import jax
import jax.numpy as jnp
from jax import lax
from jax.experimental import pallas as pl
from jax.experimental.pallas import tpu as pltpu
from jax.sharding import PartitionSpec as P

KS = 7
GX = 4
MARGIN = KS // 2
LANES = 128
PITCH = 32
INSET = 8
TAP_ROWS = 56
BIAS_ROWS = 8
PARAM_ROWS = 32
F32 = jnp.float32
BF16 = jnp.bfloat16

VMEM = pl.BlockSpec(memory_space=pltpu.VMEM)


def call(body, outs, scratch, args, flops=0, size=0, aliases=None, limit=32):
    return pl.pallas_call(
        body,
        out_shape=outs,
        in_specs=[VMEM] * len(args),
        out_specs=[VMEM] * len(outs),
        scratch_shapes=scratch,
        input_output_aliases=aliases or {},
        compiler_params=pltpu.CompilerParams(vmem_limit_bytes=limit * 1024 * 1024),
        cost_estimate=pl.CostEstimate(flops=flops, bytes_accessed=size, transcendentals=0),
    )(*args)


def shape(dims, kind):
    return jax.ShapeDtypeStruct(dims, kind)


def lane_tile(tile):
    return slice(tile * LANES, (tile + 1) * LANES)


def grid_place():
    place = lax.axis_index("tile")
    return place // GX, place % GX


def swap_rows(sends):
    count = lax.axis_size("tile")
    grid_rows = count // GX
    moved = []
    for first, block in enumerate(sends):
        route = []
        for place in range(count):
            row = place // GX
            if row % 2 == first and row + 1 < grid_rows:
                route += [(place, place + GX), (place + GX, place)]
        moved.append(lax.ppermute(block, "tile", route))
    return moved


def swap_cols(sends):
    count = lax.axis_size("tile")
    moved = []
    for first, block in enumerate(sends):
        route = []
        for place in range(count):
            col = place % GX
            if col % 2 == first and col + 1 < GX:
                route += [(place, place + 1), (place + 1, place)]
        moved.append(lax.ppermute(block, "tile", route))
    return moved


def row_pairings():
    return 1 if lax.axis_size("tile") // GX == 2 else 2


def above_below(bands, tile):
    row, _ = grid_place()
    even = row % 2 == 0
    first = bands[0][:, lane_tile(tile)].astype(F32)
    second = bands[1][:, lane_tile(tile)].astype(F32) if len(bands) > 1 else jnp.zeros_like(first)
    return jnp.where(even, second, first), jnp.where(even, first, second)


def border_columns(field, bands, rows, cols):
    width = field.shape[1]
    tall = rows + 2 * MARGIN
    packed = -(-tall * MARGIN // 16) * 16

    def body(field_ref, *refs):
        band_refs = refs[: len(bands)]
        outs, full, left, right = refs[len(bands) : -3], refs[-3], refs[-2], refs[-1]
        _, col = grid_place()
        even = col % 2 == 0
        left[...] = jnp.zeros_like(left)
        right[...] = jnp.zeros_like(right)
        for tile in range(width // LANES):
            above, below = above_below(band_refs, tile)
            full[: MARGIN * cols] = above
            full[MARGIN * cols : (MARGIN + rows) * cols] = field_ref[:, lane_tile(tile)].astype(F32)
            full[(MARGIN + rows) * cols :] = below
            for row in range(tall):
                here = pl.ds(row * MARGIN, MARGIN)
                left[here] = full[pl.ds(row * cols, MARGIN)]
                right[here] = full[pl.ds(row * cols + cols - MARGIN, MARGIN)]
            toward_left, toward_right = left[...], right[...]
            outs[0][:, lane_tile(tile)] = jnp.where(even, toward_right, toward_left).astype(BF16)
            outs[1][:, lane_tile(tile)] = jnp.where(even, toward_left, toward_right).astype(BF16)

    return call(
        body,
        [shape((packed, width), BF16)] * 2,
        [pltpu.VMEM((tall * cols, LANES), F32)] + [pltpu.VMEM((packed, LANES), F32)] * 2,
        [field, *bands],
        size=1107000,
        limit=8,
    )


def fill_padded(padded, edge, field_ref, band_refs, side_refs, rows, cols):
    width = field_ref.shape[1]
    tall = rows + 2 * MARGIN
    _, col = grid_place()
    even = col % 2 == 0
    for tile in range(width // LANES):
        above, below = above_below(band_refs, tile)
        for row in range(MARGIN):
            source = slice(row * cols, (row + 1) * cols)
            padded[tile, pl.ds(row * PITCH + INSET, cols)] = above[source]
            padded[tile, pl.ds((MARGIN + rows + row) * PITCH + INSET, cols)] = below[source]
        for row in range(rows):
            padded[tile, pl.ds((MARGIN + row) * PITCH + INSET, cols)] = field_ref[
                row * cols : (row + 1) * cols, lane_tile(tile)
            ].astype(F32)
        first = side_refs[0][:, lane_tile(tile)].astype(F32)
        second = side_refs[1][:, lane_tile(tile)].astype(F32)
        edge[0] = jnp.where(even, second, first)
        edge[1] = jnp.where(even, first, second)
        for row in range(tall):
            padded[tile, pl.ds(row * PITCH + INSET - MARGIN, MARGIN)] = edge[0, pl.ds(row * MARGIN, MARGIN)]
            padded[tile, pl.ds(row * PITCH + INSET + cols, MARGIN)] = edge[1, pl.ds(row * MARGIN, MARGIN)]


def window(padded, tile, row, shift, cols):
    return padded[tile, pl.ds(row * PITCH + INSET - MARGIN + shift, cols), :]


def tap_sums(padded, tile, taps, sums, rows, cols, flipped):
    for b in range(KS):
        for r in range(rows + 2 * MARGIN):
            pixels = window(padded, tile, r, b, cols)
            for a in range(KS):
                if 0 <= r - a < rows:
                    index = (KS - 1 - a) * KS + KS - 1 - b if flipped else a * KS + b
                    sums[r - a] = sums[r - a] + taps[index] * pixels
    return sums


def forward(field, bands, sides, params, rows, cols):
    pixels, width = field.shape
    tiles = width // LANES
    span = (rows + 2 * MARGIN) * PITCH

    def body(*refs):
        field_ref = refs[0]
        band_refs = refs[1 : 1 + len(bands)]
        side_refs = refs[1 + len(bands) : 3 + len(bands)]
        params_ref, acts, standard, inverse, padded, edge = refs[3 + len(bands) :]
        fill_padded(padded, edge, field_ref, band_refs, side_refs, rows, cols)

        @pl.loop(0, tiles)
        def _(tile):
            taps = [params_ref[tile, pl.ds(t, 1), :] for t in range(KS * KS)]
            start = jnp.broadcast_to(params_ref[tile, pl.ds(KS * KS, 1), :], (cols, LANES))
            sums = tap_sums(padded, tile, taps, [start] * rows, rows, cols, False)
            for row in range(rows):
                standard[tile, pl.ds(row * cols, cols), :] = sums[row]

        total = standard[0]
        for tile in range(1, tiles):
            total = total + standard[tile]
        average = jnp.sum(total, axis=1, keepdims=True) * (1.0 / width)
        total = jnp.zeros((pixels, LANES), F32)
        for tile in range(tiles):
            centered = standard[tile] - average
            total = total + centered * centered
        scale = lax.rsqrt(jnp.sum(total, axis=1, keepdims=True) * (1.0 / width) + 1e-06)
        inverse[...] = jnp.broadcast_to(scale, (pixels, LANES))
        for tile in range(tiles):
            value = (standard[tile] - average) * scale
            standard[tile] = value
            gain = params_ref[tile, KS * KS + 1 : KS * KS + 2, :]
            shift = params_ref[tile, KS * KS + 2 : KS * KS + 3, :]
            acts[:, lane_tile(tile)] = (value * gain + shift).astype(BF16)

    return call(
        body,
        [
            shape((pixels, width), BF16),
            shape((tiles, pixels, LANES), F32),
            shape((pixels, LANES), F32),
            shape((tiles, span, LANES), F32),
        ],
        [pltpu.VMEM((2, sides[0].shape[0], LANES), F32)],
        [field, *bands, *sides, params],
        size=10701000,
        limit=16,
    )


def hidden_values(normed, upstream, params, shards, units):
    pixels, width = normed[0].shape
    members, count = len(normed), len(shards)
    total, kept = members * pixels, members * pixels // 2
    tiles = width // LANES
    every = count * units
    step = 32

    def body(*refs):
        normed_refs, up_refs, params_ref = refs[:members], refs[members : 2 * members], refs[2 * members]
        shard_refs, rest = refs[2 * members + 1 : 2 * members + 1 + count], refs[2 * members + 1 + count :]
        hid, stay, send, norm, back, win, wout, pre, slope, bpre = rest
        for index in range(members):
            here = slice(index * pixels, (index + 1) * pixels)
            norm[here] = normed_refs[index][...]
            for tile in range(tiles):
                lanes = lane_tile(tile)
                layer = params_ref[tile, KS * KS + 3 : KS * KS + 4, :]
                back[here, lanes] = (up_refs[index][:, lanes].astype(F32) * layer).astype(BF16)
        for index, shard in enumerate(shard_refs):
            here = slice(index * units, (index + 1) * units)
            win[here] = shard[:units]
            wout[here] = shard[units : 2 * units]
        row = jnp.concatenate(
            [shard[2 * units : 2 * units + 1, :units].astype(F32) for shard in shard_refs], axis=1
        )
        across = (((1,), (1,)), ((), ()))
        pre[...] = lax.dot_general(norm[...], win[...], across, preferred_element_type=F32) + row
        slope[...] = lax.dot_general(back[...], wout[...], across, preferred_element_type=F32)

        @pl.loop(0, total // step)
        def _(part):
            here = pl.ds(pl.multiple_of(part * step, step), step)
            value = pre[here, :]
            half = 0.5 * (1.0 + lax.erf(value * 0.7071067811865476))
            hid[here, :] = (value * half).astype(BF16)
            bell = jnp.exp(-0.5 * value * value) * 0.3989422804014327
            bpre[here, :] = (slope[here, :] * (half + value * bell)).astype(BF16)

        back_normed = jnp.dot(bpre[...], win[...], preferred_element_type=F32)
        stay[...] = back_normed[:kept]
        send[...] = back_normed[kept:].astype(BF16)

    return call(
        body,
        [shape((total, every), BF16), shape((kept, width), F32), shape((kept, width), BF16)],
        [
            pltpu.VMEM((total, width), BF16),
            pltpu.VMEM((total, width), BF16),
            pltpu.VMEM((every, width), BF16),
            pltpu.VMEM((every, width), BF16),
            pltpu.VMEM((total, every), F32),
            pltpu.VMEM((total, every), F32),
            pltpu.VMEM((total, every), BF16),
        ],
        [*normed, *upstream, params, *shards],
        size=13653000,
        limit=28,
    )


def project(hidden, upstream, shards, units):
    pixels, width = upstream[0].shape
    members, count = len(upstream), len(shards)
    total, kept = members * pixels, members * pixels // 2
    tiles = width // LANES

    def body(*refs):
        hidden_ref, up_refs, shard_refs = refs[0], refs[1 : 1 + members], refs[1 + members : 1 + members + count]
        stay, send, scale, wout = refs[1 + members + count :]
        for index, shard in enumerate(shard_refs):
            wout[index * units : (index + 1) * units] = shard[units : 2 * units]
        projected = jnp.dot(hidden_ref[...], wout[...], preferred_element_type=F32)
        stay[...] = projected[:kept]
        send[...] = projected[kept:].astype(BF16)
        for tile in range(tiles):
            lanes = lane_tile(tile)
            sums = jnp.zeros((pixels, LANES), F32)
            for index in range(members):
                rows = projected[index * pixels : (index + 1) * pixels, lanes]
                sums = sums + up_refs[index][:, lanes].astype(F32) * rows
            scale[tile] = jnp.broadcast_to(jnp.sum(sums, axis=0, keepdims=True), (8, LANES))

    return call(
        body,
        [shape((kept, width), F32), shape((kept, width), BF16), shape((tiles, 8, LANES), F32)],
        [pltpu.VMEM((count * units, width), BF16)],
        [hidden, *upstream, *shards],
        size=3911400,
        limit=20,
    )


def pair_sum(mine, peer):
    rows, width = mine.shape
    half = rows // 2

    def body(mine_ref, peer_ref, out):
        out[...] = (mine_ref[half:, :] + peer_ref[half:, :].astype(F32)).astype(BF16)

    return call(body, [shape((half, width), BF16)], [], [mine, peer], size=738000, limit=4)[0]


def norm_backward(own, peer, far, standard, inverse, params, upstream, rows, cols):
    pixels, width = upstream.shape
    tiles = width // LANES
    strip = MARGIN * cols

    def body(own_ref, peer_ref, far_ref, std, inv, params_ref, up_ref, conv, wire, vectors, *sends):
        zero = jnp.zeros((pixels, LANES), F32)
        plain, mixed = zero, zero
        for tile in range(tiles):
            lanes = lane_tile(tile)
            normed = own_ref[:pixels, lanes] + peer_ref[:pixels, lanes].astype(F32) + far_ref[:, lanes].astype(F32)
            gain = params_ref[tile, KS * KS + 1 : KS * KS + 2, :]
            scaled = normed * gain
            product = normed * std[tile]
            conv[tile] = scaled
            plain = plain + scaled
            mixed = mixed + product * gain
            vectors[tile] = jnp.zeros((8, LANES), F32)
            vectors[tile, 1:2, :] = jnp.sum(product, axis=0, keepdims=True)
            vectors[tile, 2:3, :] = jnp.sum(normed, axis=0, keepdims=True)
            out_bias = params_ref[tile, KS * KS + 4 : KS * KS + 5, :]
            vectors[tile, 3:4, :] = jnp.sum(up_ref[:, lanes].astype(F32), axis=0, keepdims=True) * out_bias
        plain = jnp.sum(plain, axis=1, keepdims=True) * (1.0 / width)
        mixed = jnp.sum(mixed, axis=1, keepdims=True) * (1.0 / width)
        for tile in range(tiles):
            value = inv[...] * (conv[tile] - plain - std[tile] * mixed)
            conv[tile] = value
            wire[:, lane_tile(tile)] = value.astype(BF16)
            vectors[tile, 0:1, :] = jnp.sum(value, axis=0, keepdims=True)
        row, _ = grid_place()
        even = row % 2 == 0
        top, bottom = wire[:strip, :], wire[pixels - strip :, :]
        sends[0][...] = jnp.where(even, bottom, top)
        if len(sends) > 1:
            sends[1][...] = jnp.where(even, top, bottom)

    return call(
        body,
        [
            shape((tiles, pixels, LANES), F32),
            shape((pixels, width), BF16),
            shape((tiles, 8, LANES), F32),
        ]
        + [shape((strip, width), BF16)] * row_pairings(),
        [],
        [own, peer, far, standard, inverse, params, upstream],
        size=1845000,
        limit=16,
    )


def block_output(own, peer, far, params, field):
    pixels, width = field.shape

    def body(own_ref, peer_ref, far_ref, params_ref, field_ref, block):
        for tile in range(width // LANES):
            lanes = lane_tile(tile)
            out_bias = params_ref[tile, KS * KS + 4 : KS * KS + 5, :]
            layer = params_ref[tile, KS * KS + 3 : KS * KS + 4, :]
            projected = own_ref[:pixels, lanes] + peer_ref[:pixels, lanes].astype(F32) + far_ref[:, lanes].astype(F32)
            block[:, lanes] = (field_ref[:, lanes].astype(F32) + layer * (projected + out_bias)).astype(BF16)

    return call(
        body,
        [shape((pixels, width), BF16)],
        [],
        [own, peer, far, params, field],
        size=3210300,
        limit=8,
    )[0]


def kernel_gradient(padded, back_conv, vectors, scale_part, rows, cols, groups):
    tiles = back_conv.shape[0]
    share = tiles // groups

    def body(padded_ref, conv, vectors_ref, scale_ref, *refs):
        outs, out = refs[:-1], refs[-1]

        @pl.loop(0, tiles)
        def _(tile):
            grads = [conv[tile, pl.ds(row * cols, cols), :] for row in range(rows)]
            for b in range(KS):
                sums = [None] * KS
                for r in range(rows + 2 * MARGIN):
                    pixels = window(padded_ref, tile, r, b, cols)
                    for a in range(KS):
                        if 0 <= r - a < rows:
                            term = pixels * grads[r - a]
                            sums[a] = term if sums[a] is None else sums[a] + term
                for a in range(KS):
                    out[tile, pl.ds(a * KS + b, 1), :] = jnp.sum(sums[a], axis=0, keepdims=True)
            out[tile, pl.ds(KS * KS, TAP_ROWS - KS * KS), :] = vectors_ref[tile, : TAP_ROWS - KS * KS, :]
            out[tile, pl.ds(KS * KS + 3, 1), :] += scale_ref[tile, :1, :]

        if groups == 1:
            outs[0][...] = out[...]
        else:
            me = lax.axis_index("dp")
            for bits in range(groups):
                for part in range(share):
                    outs[bits][part] = out[(me ^ bits) * share + part]

    return call(
        body,
        [shape((share, TAP_ROWS, LANES), F32)] * groups,
        [pltpu.VMEM((tiles, TAP_ROWS, LANES), F32)],
        [padded, back_conv, vectors, scale_part],
        size=7380000,
        limit=8,
    )


def input_gradient(wire, bands, sides, params, upstream, rows, cols):
    pixels, width = wire.shape
    tiles = width // LANES
    span = (rows + 2 * MARGIN) * PITCH

    def body(*refs):
        wire_ref = refs[0]
        band_refs = refs[1 : 1 + len(bands)]
        side_refs = refs[1 + len(bands) : 3 + len(bands)]
        params_ref, up_ref, out, padded, edge = refs[3 + len(bands) :]
        fill_padded(padded, edge, wire_ref, band_refs, side_refs, rows, cols)

        @pl.loop(0, tiles)
        def _(tile):
            lanes = pl.ds(pl.multiple_of(tile * LANES, LANES), LANES)
            taps = [params_ref[tile, pl.ds(t, 1), :] for t in range(KS * KS)]
            start = [up_ref[pl.ds(row * cols, cols), lanes].astype(F32) for row in range(rows)]
            sums = tap_sums(padded, tile, taps, start, rows, cols, True)
            for row in range(rows):
                out[pl.ds(row * cols, cols), lanes] = sums[row].astype(BF16)

    return call(
        body,
        [shape((pixels, width), BF16)],
        [pltpu.VMEM((tiles, span, LANES), F32), pltpu.VMEM((2, sides[0].shape[0], LANES), F32)],
        [wire, *bands, *sides, params, upstream],
        size=12177000,
        limit=16,
    )[0]


def across(block, bits):
    groups = lax.axis_size("dp")
    return lax.ppermute(block, "dp", [(i, i ^ bits) for i in range(groups)])


def tile_swap(block, bits):
    return lax.ppermute(block, "tile", [(i, i ^ bits) for i in range(lax.axis_size("tile"))])


def place_params(own, joints, last):
    share, rows, _ = own.shape
    half = rows // 2

    def body(own_ref, one_ref, two_ref, last_ref, out):
        me = lax.axis_index("dp")
        for part in range(share):
            out[me * share + part] = own_ref[part]
            out[(me ^ 3) * share + part] = last_ref[part]
        for bits, ref in ((1, one_ref), (2, two_ref)):
            start = ref.shape[0] - PARAM_ROWS
            for part in range(2 * share):
                high = ref[start:, lane_tile(2 * part)].astype(F32)
                value = high + ref[start:, lane_tile(2 * part + 1)].astype(F32)
                out[(me ^ bits) * share + part // 2, pl.ds(part % 2 * half, half), :] = value[:half]

    return call(
        body,
        [shape((4 * share, rows, LANES), F32)],
        [],
        [own, *joints, last],
        size=738000,
        limit=4,
    )[0]


def gather_params(kernel, vectors):
    own = kernel.shape[1]
    pack = jnp.concatenate([kernel, *vectors, jnp.zeros((TAP_ROWS - KS * KS - len(vectors), own), F32)])
    whole = lax.all_gather(pack, "dp", axis=1, tiled=True)
    return whole.reshape(TAP_ROWS, -1, LANES).transpose(1, 0, 2)


def sum_params(parts, factor):
    flat = parts.transpose(1, 0, 2).reshape(TAP_ROWS, -1)
    sums = lax.psum(lax.psum_scatter(flat, "dp", scatter_dimension=1, tiled=True), "tile") * factor
    taps = KS * KS
    return [sums[:taps]] + [sums[taps + index] for index in range(4)]


def add_blocks(blocks):
    def body(*refs):
        value = refs[0][...]
        for ref in refs[1:-1]:
            value = value + ref[...]
        refs[-1][...] = value

    return call(body, [shape(blocks[0].shape, F32)], [], blocks, size=738000, limit=4)[0]


def finish(total, moved, factor):
    tiles, rows, _ = total.shape
    taps = KS * KS

    def body(*refs):
        outs = refs[1 + len(moved) :]
        for tile in range(tiles):
            value = refs[0][tile]
            for other in refs[1 : 1 + len(moved)]:
                value = value + other[tile]
            value = value * factor
            outs[0][:, lane_tile(tile)] = value[:taps]
            for index in range(4):
                outs[1 + index][:, lane_tile(tile)] = value[taps + index : taps + index + 1]

    taps_sum, *vectors = call(
        body,
        [shape((taps, tiles * LANES), F32)] + [shape((1, tiles * LANES), F32)] * 4,
        [],
        [total, *moved],
        size=2214000,
        limit=4,
    )
    return [taps_sum] + [v.reshape(-1) for v in vectors]


def after(block, *others):
    return lax.optimization_barrier((block, *others))[0]


def pack_shard(rows_in, rows_out, bias):
    units, width = rows_in.shape
    row = jnp.pad(bias.reshape(1, units), ((0, BIAS_ROWS - 1), (0, width - units)))
    return jnp.concatenate([rows_in, rows_out, row])


def first_sends(field, rows_in, rows_out, bias, kernel, vectors, strip):
    pixels, width = field.shape
    units = rows_in.shape[0]
    taps, own = kernel.shape
    pairings = row_pairings()
    shard_rows = 2 * units + BIAS_ROWS
    half = TAP_ROWS // 2

    def body(bias_ref, field_ref, in_ref, out_ref, kernel_ref, *refs):
        vector_refs, refs = refs[: len(vectors)], refs[len(vectors) :]
        shard, joint, pack, sends = refs[0], refs[1], refs[2], refs[3 : 3 + pairings]
        tap_stage, vector_stage, sems = refs[3 + pairings :]
        row, _ = grid_place()
        copies = [
            pltpu.make_async_copy(in_ref, shard.at[pl.ds(0, units)], sems.at[0]),
            pltpu.make_async_copy(out_ref, shard.at[pl.ds(units, units)], sems.at[1]),
            pltpu.make_async_copy(kernel_ref, tap_stage, sems.at[2]),
        ]
        for index in range(pairings):
            start = pl.multiple_of((1 - (row + index) % 2) * (pixels - strip), 16)
            copies.append(
                pltpu.make_async_copy(field_ref.at[pl.ds(start, strip)], sends[index], sems.at[3 + index])
            )
        for index, ref in enumerate(vector_refs):
            copies.append(
                pltpu.make_async_copy(ref, vector_stage.at[index], sems.at[3 + pairings + index])
            )
        for copy in copies:
            copy.start()
        line = jnp.concatenate([bias_ref[...].astype(F32), jnp.zeros((1, width - units), F32)], axis=1)
        first = lax.broadcasted_iota(jnp.int32, (BIAS_ROWS, width), 0) == 0
        shard[2 * units :] = jnp.where(first, jnp.broadcast_to(line, (BIAS_ROWS, width)), 0.0).astype(BF16)
        for copy in copies:
            copy.wait()
        for tile in range(own // LANES):
            pack[tile, TAP_ROWS - 8 :, :] = jnp.zeros((8, LANES), F32)
            pack[tile, :taps, :] = tap_stage[:, lane_tile(tile)]
            for index in range(len(vectors)):
                pack[tile, taps + index : taps + index + 1, :] = vector_stage[index, :, lane_tile(tile)]
        joint[:shard_rows] = shard[...]
        for part in range(2 * own // LANES):
            value = pack[part // 2, part % 2 * half : (part % 2 + 1) * half, :]
            value = jnp.concatenate([value, jnp.zeros((PARAM_ROWS - half, LANES), F32)])
            high = value.astype(BF16)
            joint[shard_rows:, lane_tile(2 * part)] = high
            joint[shard_rows:, lane_tile(2 * part + 1)] = (value - high.astype(F32)).astype(BF16)

    outs = [
        shape((shard_rows, width), BF16),
        shape((shard_rows + PARAM_ROWS, width), BF16),
        shape((own // LANES, TAP_ROWS, LANES), F32),
    ]
    outs += [shape((strip, width), BF16)] * pairings
    args = [bias.reshape(1, units), field, rows_in, rows_out, kernel, *vectors]
    return pl.pallas_call(
        body,
        out_shape=outs,
        in_specs=[VMEM] + [pl.BlockSpec(memory_space=pltpu.HBM)] * (len(args) - 1),
        out_specs=[VMEM] * len(outs),
        scratch_shapes=[
            pltpu.VMEM((taps, own), F32),
            pltpu.VMEM((len(vectors), 1, own), F32),
            pltpu.SemaphoreType.DMA((3 + pairings + len(vectors),)),
        ],
        compiler_params=pltpu.CompilerParams(vmem_limit_bytes=62 * 1024 * 1024),
        cost_estimate=pl.CostEstimate(flops=10000, bytes_accessed=1000000, transcendentals=0),
    )(*args)


def row_sends(field, strip):
    row, _ = grid_place()
    starts = [(1 - (row + first) % 2) * (field.shape[0] - strip) for first in range(row_pairings())]
    return [lax.dynamic_slice_in_dim(field, start, strip, 0) for start in starts]


def gathered_shard(in_weight, out_weight, hidden_bias):
    units = in_weight.shape[0]
    groups, count = lax.axis_size("dp"), lax.axis_size("tile")
    place = lax.axis_index("tile")
    member = place // 4 % 2 * 2 + place % 2

    def mine(array):
        whole = lax.all_gather(array, ("dp", "tile"), axis=0, tiled=True)
        whole = whole.reshape((4, groups * count // 4 * units) + array.shape[1:])
        return lax.dynamic_index_in_dim(whole, member, 0, keepdims=False)

    rows_in, rows_out, bias = mine(in_weight), mine(out_weight), mine(hidden_bias)
    return pack_shard(rows_in, rows_out, bias)


def per_device(
    features,
    cotangent,
    in_weight,
    out_weight,
    hidden_bias,
    kernel,
    conv_bias,
    norm_gain,
    norm_bias,
    layer_scale,
    out_bias,
):
    image_count, _, rows, cols, width = features.shape
    groups, count = lax.axis_size("dp"), lax.axis_size("tile")
    units = in_weight.shape[0]
    pixels = rows * cols
    own = kernel.shape[1]
    strip = MARGIN * cols
    field = features.reshape(pixels, width)
    upstream = cotangent.reshape(pixels, width)

    by_permutes = units % 16 == 0 and groups == 4 and count == 8 and units < width and 4 * own == width
    vectors = [v.reshape(1, own) for v in (conv_bias, norm_gain, norm_bias, layer_scale, out_bias)]
    if by_permutes:
        held, joint, piece, *sends = first_sends(
            field, in_weight, out_weight, hidden_bias, kernel, vectors, strip
        )
        first, second, other = across(joint, 1), across(joint, 2), tile_swap(held, 2)
        last = across(piece, 3)
        bands = swap_rows(sends)
        first, second, other, last, bands = lax.optimization_barrier((first, second, other, last, bands))
        params = place_params(piece, [first, second], last)
        other_first = across(after(other, first, second), 1)
        other_second = across(after(other, first, second), 2)
        far = across(after(first, other_first, other_second), 2)
        other_far = across(after(other_second, other_first), 1)
        shards = [held, first, second, far, other, other_first, other_second, other_far]
    else:
        bands = swap_rows(row_sends(field, strip))
        params = gather_params(kernel, vectors)
        shards = [gathered_shard(in_weight, out_weight, hidden_bias)]
        units = shards[0].shape[0] // 2 - BIAS_ROWS // 2
    far_upstream = tile_swap(after(upstream, *bands), 4)
    sides = swap_cols(border_columns(field, bands, rows, cols))
    acts, standard, inverse, padded = forward(field, bands, sides, params, rows, cols)
    far_acts = tile_swap(after(acts, far_upstream), 4)
    normed = [acts, far_acts, tile_swap(acts, 1), tile_swap(far_acts, 1)]
    upstreams = [upstream, far_upstream, tile_swap(upstream, 1), tile_swap(far_upstream, 1)]
    hidden, back_own, back_send = hidden_values(normed, upstreams, params, shards, units)

    def group_sum(mine, theirs, *others):
        peer = tile_swap(theirs, 1)
        return mine, peer, tile_swap(after(pair_sum(mine, peer), *others), 4)

    back_sums = group_sum(back_own, back_send)
    out_own, out_send, scale_part = project(hidden, upstreams, shards, units)
    back_conv, wire, vector_parts, *back_sends = norm_backward(
        *back_sums, standard, inverse, params, upstream, rows, cols
    )
    parts = kernel_gradient(
        padded, back_conv, vector_parts, scale_part, rows, cols, groups if by_permutes else 1
    )
    back_bands = swap_rows(back_sends)
    block = block_output(*group_sum(out_own, out_send, *back_bands), params, field)
    back_sides = swap_cols(border_columns(wire, back_bands, rows, cols))
    grad = input_gradient(wire, back_bands, back_sides, params, upstream, rows, cols)
    factor = 1.0 / math.sqrt(image_count * groups * count * pixels)
    if by_permutes:
        total = add_blocks([parts[0]] + [across(parts[bits], bits) for bits in range(1, groups)])
        total = add_blocks([total, tile_swap(total, 1)])
        moved = [tile_swap(total, bits) for bits in range(2, count, 2)]
        sums = finish(after(total, grad), moved, factor)
    else:
        sums = sum_params(parts[0], factor)
    return (block.reshape(features.shape), grad.reshape(features.shape), *sums)


def solution(mesh):
    placed = (
        P("dp", "tile", None, None, None),
        P("dp", "tile", None, None, None),
        P(("dp", "tile"), None),
        P(("dp", "tile"), None),
        P(("dp", "tile")),
        P(None, "dp"),
        P("dp"),
        P("dp"),
        P("dp"),
        P("dp"),
        P("dp"),
    )
    return jax.shard_map(
        per_device,
        mesh=mesh,
        in_specs=placed,
        out_specs=(
            P("dp", "tile", None, None, None),
            P("dp", "tile", None, None, None),
            P(None, "dp"),
            P("dp"),
            P("dp"),
            P("dp"),
            P("dp"),
        ),
        check_vma=False,
    )
```

```python
import math

import jax
import jax.numpy as jnp
from jax import lax
from jax.experimental import pallas as pl
from jax.experimental.pallas import tpu as pltpu
from jax.sharding import PartitionSpec as P

KS = 7
GX = 4
MARGIN = KS // 2
LANES = 128
PITCH = 32
INSET = 8
TAP_ROWS = 56
BIAS_ROWS = 16
PARAM_ROWS = 32
F32 = jnp.float32
BF16 = jnp.bfloat16

VMEM = pl.BlockSpec(memory_space=pltpu.VMEM)


def call(body, outs, scratch, args, flops=0, size=0, aliases=None, limit=32):
    return pl.pallas_call(
        body,
        out_shape=outs,
        in_specs=[VMEM] * len(args),
        out_specs=[VMEM] * len(outs),
        scratch_shapes=scratch,
        input_output_aliases=aliases or {},
        compiler_params=pltpu.CompilerParams(vmem_limit_bytes=limit * 1024 * 1024),
        cost_estimate=pl.CostEstimate(flops=flops, bytes_accessed=size, transcendentals=0),
    )(*args)


def shape(dims, kind):
    return jax.ShapeDtypeStruct(dims, kind)


def lane_tile(tile):
    return slice(tile * LANES, (tile + 1) * LANES)


def grid_place():
    place = lax.axis_index("tile")
    return place // GX, place % GX


def swap_rows(sends):
    count = lax.axis_size("tile")
    grid_rows = count // GX
    moved = []
    for first, block in enumerate(sends):
        route = []
        for place in range(count):
            row = place // GX
            if row % 2 == first and row + 1 < grid_rows:
                route += [(place, place + GX), (place + GX, place)]
        moved.append(lax.ppermute(block, "tile", route))
    return moved


def swap_cols(sends):
    count = lax.axis_size("tile")
    moved = []
    for first, block in enumerate(sends):
        route = []
        for place in range(count):
            col = place % GX
            if col % 2 == first:
                other = place - col + (col + 1) % GX
                route += [(place, other), (other, place)]
        moved.append(lax.ppermute(block, "tile", route))
    return moved


def row_pairings():
    return 1 if lax.axis_size("tile") // GX == 2 else 2


def above_below(bands, tile):
    row, _ = grid_place()
    even = row % 2 == 0
    first = bands[0][:, lane_tile(tile)].astype(F32)
    second = bands[1][:, lane_tile(tile)].astype(F32) if len(bands) > 1 else jnp.zeros_like(first)
    return jnp.where(even, second, first), jnp.where(even, first, second)


def border_columns(field, bands, rows, cols):
    width = field.shape[1]
    tall = rows + 2 * MARGIN
    packed = -(-tall * MARGIN // 16) * 16

    def body(field_ref, *refs):
        band_refs = refs[: len(bands)]
        outs, full, left, right = refs[len(bands) : -3], refs[-3], refs[-2], refs[-1]
        _, col = grid_place()
        even = col % 2 == 0
        left[...] = jnp.zeros_like(left)
        right[...] = jnp.zeros_like(right)
        for tile in range(width // LANES):
            above, below = above_below(band_refs, tile)
            full[: MARGIN * cols] = above
            full[MARGIN * cols : (MARGIN + rows) * cols] = field_ref[:, lane_tile(tile)].astype(F32)
            full[(MARGIN + rows) * cols :] = below
            for row in range(tall):
                here = pl.ds(row * MARGIN, MARGIN)
                left[here] = full[pl.ds(row * cols, MARGIN)]
                right[here] = full[pl.ds(row * cols + cols - MARGIN, MARGIN)]
            toward_left, toward_right = left[...], right[...]
            outs[0][:, lane_tile(tile)] = jnp.where(even, toward_right, toward_left).astype(BF16)
            outs[1][:, lane_tile(tile)] = jnp.where(even, toward_left, toward_right).astype(BF16)

    return call(
        body,
        [shape((packed, width), BF16)] * 2,
        [pltpu.VMEM((tall * cols, LANES), F32)] + [pltpu.VMEM((packed, LANES), F32)] * 2,
        [field, *bands],
        size=1107000,
        limit=8,
    )


def fill_padded(padded, edge, field_ref, band_refs, side_refs, rows, cols):
    width = field_ref.shape[1]
    tall = rows + 2 * MARGIN
    _, col = grid_place()
    even = col % 2 == 0
    inner = (col > 0) & (col < GX - 1)
    for tile in range(width // LANES):
        above, below = above_below(band_refs, tile)
        for row in range(MARGIN):
            source = slice(row * cols, (row + 1) * cols)
            padded[tile, pl.ds(row * PITCH + INSET, cols)] = above[source]
            padded[tile, pl.ds((MARGIN + rows + row) * PITCH + INSET, cols)] = below[source]
        for row in range(rows):
            padded[tile, pl.ds((MARGIN + row) * PITCH + INSET, cols)] = field_ref[
                row * cols : (row + 1) * cols, lane_tile(tile)
            ].astype(F32)
        first = side_refs[0][:, lane_tile(tile)].astype(F32)
        second = jnp.where(inner, side_refs[1][:, lane_tile(tile)].astype(F32), 0.0)
        edge[0] = jnp.where(even, second, first)
        edge[1] = jnp.where(even, first, second)
        for row in range(tall):
            padded[tile, pl.ds(row * PITCH + INSET - MARGIN, MARGIN)] = edge[0, pl.ds(row * MARGIN, MARGIN)]
            padded[tile, pl.ds(row * PITCH + INSET + cols, MARGIN)] = edge[1, pl.ds(row * MARGIN, MARGIN)]


def window(padded, tile, row, shift, cols):
    return padded[tile, pl.ds(row * PITCH + INSET - MARGIN + shift, cols), :]


def tap_sums(padded, tile, taps, sums, rows, cols, flipped):
    for b in range(KS):
        for r in range(rows + 2 * MARGIN):
            pixels = window(padded, tile, r, b, cols)
            for a in range(KS):
                if 0 <= r - a < rows:
                    index = (KS - 1 - a) * KS + KS - 1 - b if flipped else a * KS + b
                    sums[r - a] = sums[r - a] + taps[index] * pixels
    return sums


def forward(field, bands, sides, params, rows, cols):
    pixels, width = field.shape
    tiles = width // LANES
    span = (rows + 2 * MARGIN) * PITCH

    def body(*refs):
        field_ref = refs[0]
        band_refs = refs[1 : 1 + len(bands)]
        side_refs = refs[1 + len(bands) : 3 + len(bands)]
        params_ref, acts, standard, inverse, padded, edge = refs[3 + len(bands) :]
        fill_padded(padded, edge, field_ref, band_refs, side_refs, rows, cols)

        @pl.loop(0, tiles)
        def _(tile):
            taps = [params_ref[tile, pl.ds(t, 1), :] for t in range(KS * KS)]
            start = jnp.broadcast_to(params_ref[tile, pl.ds(KS * KS, 1), :], (cols, LANES))
            sums = tap_sums(padded, tile, taps, [start] * rows, rows, cols, False)
            for row in range(rows):
                standard[tile, pl.ds(row * cols, cols), :] = sums[row]

        total = standard[0]
        for tile in range(1, tiles):
            total = total + standard[tile]
        average = jnp.sum(total, axis=1, keepdims=True) * (1.0 / width)
        total = jnp.zeros((pixels, LANES), F32)
        for tile in range(tiles):
            centered = standard[tile] - average
            total = total + centered * centered
        scale = lax.rsqrt(jnp.sum(total, axis=1, keepdims=True) * (1.0 / width) + 1e-06)
        inverse[...] = jnp.broadcast_to(scale, (pixels, LANES))
        for tile in range(tiles):
            value = (standard[tile] - average) * scale
            standard[tile] = value
            gain = params_ref[tile, KS * KS + 1 : KS * KS + 2, :]
            shift = params_ref[tile, KS * KS + 2 : KS * KS + 3, :]
            acts[:, lane_tile(tile)] = (value * gain + shift).astype(BF16)

    return call(
        body,
        [
            shape((pixels, width), BF16),
            shape((tiles, pixels, LANES), F32),
            shape((pixels, LANES), F32),
            shape((tiles, span, LANES), F32),
        ],
        [pltpu.VMEM((2, sides[0].shape[0], LANES), F32)],
        [field, *bands, *sides, params],
        size=10701000,
        limit=16,
    )


def arrays_of(shards):
    arrays, slots = [], []
    for shard in shards:
        places = []
        for array, start, _ in shard:
            known = [index for index, other in enumerate(arrays) if other is array]
            if not known:
                arrays.append(array)
            places.append((known[0] if known else len(arrays) - 1, start))
        slots.append(places)
    return arrays, slots


def hidden_values(normed, upstream, params, shards, units):
    pixels, width = normed[0].shape
    arrays, slots = arrays_of(shards)
    members, count = len(normed), len(arrays)
    total, kept = members * pixels, members * pixels // 2
    tiles = width // LANES
    every = len(shards) * units
    step = 32

    def body(*refs):
        normed_refs, up_refs, params_ref = refs[:members], refs[members : 2 * members], refs[2 * members]
        shard_refs, rest = refs[2 * members + 1 : 2 * members + 1 + count], refs[2 * members + 1 + count :]
        hid, stay, send, norm, back, win, wout, pre, slope, bpre = rest
        for index in range(members):
            here = slice(index * pixels, (index + 1) * pixels)
            norm[here] = normed_refs[index][...]
            for tile in range(tiles):
                lanes = lane_tile(tile)
                layer = params_ref[tile, KS * KS + 3 : KS * KS + 4, :]
                back[here, lanes] = (up_refs[index][:, lanes].astype(F32) * layer).astype(BF16)
        for index, (rows_in, rows_out, _) in enumerate(slots):
            here = slice(index * units, (index + 1) * units)
            win[here] = shard_refs[rows_in[0]][rows_in[1] : rows_in[1] + units]
            wout[here] = shard_refs[rows_out[0]][rows_out[1] : rows_out[1] + units]
        row = jnp.concatenate(
            [shard_refs[bias[0]][bias[1] : bias[1] + 1, :units].astype(F32) for *_, bias in slots], axis=1
        )
        across = (((1,), (1,)), ((), ()))
        pre[...] = lax.dot_general(norm[...], win[...], across, preferred_element_type=F32) + row
        slope[...] = lax.dot_general(back[...], wout[...], across, preferred_element_type=F32)

        @pl.loop(0, total // step)
        def _(part):
            here = pl.ds(pl.multiple_of(part * step, step), step)
            value = pre[here, :]
            half = 0.5 * (1.0 + lax.erf(value * 0.7071067811865476))
            hid[here, :] = (value * half).astype(BF16)
            bell = jnp.exp(-0.5 * value * value) * 0.3989422804014327
            bpre[here, :] = (slope[here, :] * (half + value * bell)).astype(BF16)

        back_normed = jnp.dot(bpre[...], win[...], preferred_element_type=F32)
        stay[...] = back_normed[:kept]
        send[...] = back_normed[kept:].astype(BF16)

    return call(
        body,
        [shape((total, every), BF16), shape((kept, width), F32), shape((kept, width), BF16)],
        [
            pltpu.VMEM((total, width), BF16),
            pltpu.VMEM((total, width), BF16),
            pltpu.VMEM((every, width), BF16),
            pltpu.VMEM((every, width), BF16),
            pltpu.VMEM((total, every), F32),
            pltpu.VMEM((total, every), F32),
            pltpu.VMEM((total, every), BF16),
        ],
        [*normed, *upstream, params, *arrays],
        size=13653000,
        limit=28,
    )


def project(hidden, upstream, shards, units):
    pixels, width = upstream[0].shape
    arrays, slots = arrays_of([[rows_out] for _, rows_out, _ in shards])
    members, count = len(upstream), len(arrays)
    total, kept = members * pixels, members * pixels // 2
    tiles = width // LANES

    def body(*refs):
        hidden_ref, up_refs, shard_refs = refs[0], refs[1 : 1 + members], refs[1 + members : 1 + members + count]
        stay, send, scale, wout = refs[1 + members + count :]
        for index, ((slot, start),) in enumerate(slots):
            wout[index * units : (index + 1) * units] = shard_refs[slot][start : start + units]
        projected = jnp.dot(hidden_ref[...], wout[...], preferred_element_type=F32)
        stay[...] = projected[:kept]
        send[...] = projected[kept:].astype(BF16)
        for tile in range(tiles):
            lanes = lane_tile(tile)
            sums = jnp.zeros((pixels, LANES), F32)
            for index in range(members):
                rows = projected[index * pixels : (index + 1) * pixels, lanes]
                sums = sums + up_refs[index][:, lanes].astype(F32) * rows
            scale[tile] = jnp.broadcast_to(jnp.sum(sums, axis=0, keepdims=True), (8, LANES))

    return call(
        body,
        [shape((kept, width), F32), shape((kept, width), BF16), shape((tiles, 8, LANES), F32)],
        [pltpu.VMEM((len(shards) * units, width), BF16)],
        [hidden, *upstream, *arrays],
        size=3911400,
        limit=20,
    )


def pair_sum(mine, peer):
    rows, width = mine.shape
    half = rows // 2

    def body(mine_ref, peer_ref, out):
        out[...] = (mine_ref[half:, :] + peer_ref[half:, :].astype(F32)).astype(BF16)

    return call(body, [shape((half, width), BF16)], [], [mine, peer], size=738000, limit=4)[0]


def norm_backward(own, peer, far, standard, inverse, params, upstream, rows, cols):
    pixels, width = upstream.shape
    tiles = width // LANES
    strip = MARGIN * cols

    def body(own_ref, peer_ref, far_ref, std, inv, params_ref, up_ref, conv, wire, vectors, *sends):
        zero = jnp.zeros((pixels, LANES), F32)
        plain, mixed = zero, zero
        for tile in range(tiles):
            lanes = lane_tile(tile)
            normed = own_ref[:pixels, lanes] + peer_ref[:pixels, lanes].astype(F32) + far_ref[:, lanes].astype(F32)
            gain = params_ref[tile, KS * KS + 1 : KS * KS + 2, :]
            scaled = normed * gain
            product = normed * std[tile]
            conv[tile] = scaled
            plain = plain + scaled
            mixed = mixed + product * gain
            vectors[tile] = jnp.zeros((8, LANES), F32)
            vectors[tile, 1:2, :] = jnp.sum(product, axis=0, keepdims=True)
            vectors[tile, 2:3, :] = jnp.sum(normed, axis=0, keepdims=True)
            out_bias = params_ref[tile, KS * KS + 4 : KS * KS + 5, :]
            vectors[tile, 3:4, :] = jnp.sum(up_ref[:, lanes].astype(F32), axis=0, keepdims=True) * out_bias
        plain = jnp.sum(plain, axis=1, keepdims=True) * (1.0 / width)
        mixed = jnp.sum(mixed, axis=1, keepdims=True) * (1.0 / width)
        for tile in range(tiles):
            value = inv[...] * (conv[tile] - plain - std[tile] * mixed)
            conv[tile] = value
            wire[:, lane_tile(tile)] = value.astype(BF16)
            vectors[tile, 0:1, :] = jnp.sum(value, axis=0, keepdims=True)
        row, _ = grid_place()
        even = row % 2 == 0
        top, bottom = wire[:strip, :], wire[pixels - strip :, :]
        sends[0][...] = jnp.where(even, bottom, top)
        if len(sends) > 1:
            sends[1][...] = jnp.where(even, top, bottom)

    return call(
        body,
        [
            shape((tiles, pixels, LANES), F32),
            shape((pixels, width), BF16),
            shape((tiles, 8, LANES), F32),
        ]
        + [shape((strip, width), BF16)] * row_pairings(),
        [],
        [own, peer, far, standard, inverse, params, upstream],
        size=1845000,
        limit=16,
    )


def block_output(own, peer, far, params, field):
    pixels, width = field.shape

    def body(own_ref, peer_ref, far_ref, params_ref, field_ref, block):
        for tile in range(width // LANES):
            lanes = lane_tile(tile)
            out_bias = params_ref[tile, KS * KS + 4 : KS * KS + 5, :]
            layer = params_ref[tile, KS * KS + 3 : KS * KS + 4, :]
            projected = own_ref[:pixels, lanes] + peer_ref[:pixels, lanes].astype(F32) + far_ref[:, lanes].astype(F32)
            block[:, lanes] = (field_ref[:, lanes].astype(F32) + layer * (projected + out_bias)).astype(BF16)

    return call(
        body,
        [shape((pixels, width), BF16)],
        [],
        [own, peer, far, params, field],
        size=3210300,
        limit=8,
    )[0]


def kernel_gradient(padded, back_conv, vectors, scale_part, rows, cols, groups):
    tiles = back_conv.shape[0]
    share = tiles // groups

    def body(padded_ref, conv, vectors_ref, scale_ref, *refs):
        outs, out = refs[:-1], refs[-1]

        @pl.loop(0, tiles)
        def _(tile):
            grads = [conv[tile, pl.ds(row * cols, cols), :] for row in range(rows)]
            for b in range(KS):
                sums = [None] * KS
                for r in range(rows + 2 * MARGIN):
                    pixels = window(padded_ref, tile, r, b, cols)
                    for a in range(KS):
                        if 0 <= r - a < rows:
                            term = pixels * grads[r - a]
                            sums[a] = term if sums[a] is None else sums[a] + term
                for a in range(KS):
                    out[tile, pl.ds(a * KS + b, 1), :] = jnp.sum(sums[a], axis=0, keepdims=True)
            out[tile, pl.ds(KS * KS, TAP_ROWS - KS * KS), :] = vectors_ref[tile, : TAP_ROWS - KS * KS, :]
            out[tile, pl.ds(KS * KS + 3, 1), :] += scale_ref[tile, :1, :]

        if groups == 1:
            outs[0][...] = out[...]
        else:
            me = lax.axis_index("dp")
            for bits in range(groups):
                for part in range(share):
                    outs[bits][part] = out[(me ^ bits) * share + part]

    return call(
        body,
        [shape((share, TAP_ROWS, LANES), F32)] * groups,
        [pltpu.VMEM((tiles, TAP_ROWS, LANES), F32)],
        [padded, back_conv, vectors, scale_part],
        size=7380000,
        limit=8,
    )


def input_gradient(wire, bands, sides, params, upstream, rows, cols):
    pixels, width = wire.shape
    tiles = width // LANES
    span = (rows + 2 * MARGIN) * PITCH

    def body(*refs):
        wire_ref = refs[0]
        band_refs = refs[1 : 1 + len(bands)]
        side_refs = refs[1 + len(bands) : 3 + len(bands)]
        params_ref, up_ref, out, padded, edge = refs[3 + len(bands) :]
        fill_padded(padded, edge, wire_ref, band_refs, side_refs, rows, cols)

        @pl.loop(0, tiles)
        def _(tile):
            lanes = pl.ds(pl.multiple_of(tile * LANES, LANES), LANES)
            taps = [params_ref[tile, pl.ds(t, 1), :] for t in range(KS * KS)]
            start = [up_ref[pl.ds(row * cols, cols), lanes].astype(F32) for row in range(rows)]
            sums = tap_sums(padded, tile, taps, start, rows, cols, True)
            for row in range(rows):
                out[pl.ds(row * cols, cols), lanes] = sums[row].astype(BF16)

    return call(
        body,
        [shape((pixels, width), BF16)],
        [pltpu.VMEM((tiles, span, LANES), F32), pltpu.VMEM((2, sides[0].shape[0], LANES), F32)],
        [wire, *bands, *sides, params, upstream],
        size=12177000,
        limit=16,
    )[0]


def across(block, bits):
    groups = lax.axis_size("dp")
    return lax.ppermute(block, "dp", [(i, i ^ bits) for i in range(groups)])


def tile_swap(block, bits):
    return lax.ppermute(block, "tile", [(i, i ^ bits) for i in range(lax.axis_size("tile"))])


def place_params(own, joints):
    share, rows, _ = own.shape
    half = rows // 2

    def body(own_ref, *refs):
        joint_refs, out = refs[:-1], refs[-1]
        me = lax.axis_index("dp")
        for part in range(share):
            out[me * share + part] = own_ref[part]
        for bits, ref in enumerate(joint_refs, 1):
            start = ref.shape[0] - PARAM_ROWS
            for part in range(2 * share):
                high = ref[start:, lane_tile(2 * part)].astype(F32)
                value = high + ref[start:, lane_tile(2 * part + 1)].astype(F32)
                out[(me ^ bits) * share + part // 2, pl.ds(part % 2 * half, half), :] = value[:half]

    return call(
        body,
        [shape((4 * share, rows, LANES), F32)],
        [],
        [own, *joints],
        size=738000,
        limit=4,
    )[0]


def gather_params(kernel, vectors):
    own = kernel.shape[1]
    pack = jnp.concatenate([kernel, *vectors, jnp.zeros((TAP_ROWS - KS * KS - len(vectors), own), F32)])
    whole = lax.all_gather(pack, "dp", axis=1, tiled=True)
    return whole.reshape(TAP_ROWS, -1, LANES).transpose(1, 0, 2)


def sum_params(parts, factor):
    flat = parts.transpose(1, 0, 2).reshape(TAP_ROWS, -1)
    sums = lax.psum(lax.psum_scatter(flat, "dp", scatter_dimension=1, tiled=True), "tile") * factor
    taps = KS * KS
    return [sums[:taps]] + [sums[taps + index] for index in range(4)]


def add_blocks(blocks):
    def body(*refs):
        value = refs[0][...]
        for ref in refs[1:-1]:
            value = value + ref[...]
        refs[-1][...] = value

    return call(body, [shape(blocks[0].shape, F32)], [], blocks, size=738000, limit=4)[0]


def finish(total, moved, factor):
    tiles, rows, _ = total.shape
    taps = KS * KS

    def body(*refs):
        outs = refs[1 + len(moved) :]
        for tile in range(tiles):
            value = refs[0][tile]
            for other in refs[1 : 1 + len(moved)]:
                value = value + other[tile]
            value = value * factor
            outs[0][:, lane_tile(tile)] = value[:taps]
            for index in range(4):
                outs[1 + index][:, lane_tile(tile)] = value[taps + index : taps + index + 1]

    taps_sum, *vectors = call(
        body,
        [shape((taps, tiles * LANES), F32)] + [shape((1, tiles * LANES), F32)] * 4,
        [],
        [total, *moved],
        size=2214000,
        limit=4,
    )
    return [taps_sum] + [v.reshape(-1) for v in vectors]


def after(block, *others):
    return lax.optimization_barrier((block, *others))[0]


def pack_shard(rows_in, rows_out, bias):
    units, width = rows_in.shape
    row = jnp.pad(bias.reshape(1, units), ((0, BIAS_ROWS - 1), (0, width - units)))
    return jnp.concatenate([rows_in, rows_out, row])


def first_sends(field, rows_in, rows_out, bias, kernel, vectors, strip):
    pixels, width = field.shape
    units = rows_in.shape[0]
    taps, own = kernel.shape
    half = TAP_ROWS // 2

    def body(bias_ref, field_ref, in_ref, out_ref, kernel_ref, *refs):
        vector_refs, refs = refs[: len(vectors)], refs[len(vectors) :]
        joint, cross, pack, tap_stage, vector_stage, sems = refs
        row, _ = grid_place()
        start = pl.multiple_of((1 - row % 2) * (pixels - strip), 16)
        small = [pltpu.make_async_copy(kernel_ref, tap_stage, sems.at[0])]
        for index, ref in enumerate(vector_refs):
            small.append(pltpu.make_async_copy(ref, vector_stage.at[index], sems.at[1 + index]))
        at = 1 + len(vectors)
        large = [
            pltpu.make_async_copy(field_ref.at[pl.ds(start, strip)], cross.at[pl.ds(0, strip)], sems.at[at]),
            pltpu.make_async_copy(in_ref, joint.at[pl.ds(0, units)], sems.at[at + 1]),
            pltpu.make_async_copy(out_ref, joint.at[pl.ds(units, units)], sems.at[at + 2]),
        ]
        for copy in small + large:
            copy.start()
        line = jnp.concatenate([bias_ref[...].astype(F32), jnp.zeros((1, width - units), F32)], axis=1)
        line = jnp.broadcast_to(line, (BIAS_ROWS, width))
        places = lax.broadcasted_iota(jnp.int32, (BIAS_ROWS, width), 0)
        cross[strip + 2 * units :] = jnp.where(places == 0, line, 0.0).astype(BF16)
        for copy in small:
            copy.wait()
        for tile in range(own // LANES):
            pack[tile, TAP_ROWS - 8 :, :] = jnp.zeros((8, LANES), F32)
            pack[tile, :taps, :] = tap_stage[:, lane_tile(tile)]
            for index in range(len(vectors)):
                pack[tile, taps + index : taps + index + 1, :] = vector_stage[index, :, lane_tile(tile)]
        for part in range(2 * own // LANES):
            value = pack[part // 2, part % 2 * half : (part % 2 + 1) * half, :]
            value = jnp.concatenate([value, jnp.zeros((PARAM_ROWS - half, LANES), F32)])
            high = value.astype(BF16).astype(F32)
            for side, rest in enumerate((high, value - high)):
                lanes = lane_tile(2 * part + side)
                spread = jnp.broadcast_to(line[:1, lanes], (PARAM_ROWS, LANES))
                places = lax.broadcasted_iota(jnp.int32, (PARAM_ROWS, LANES), 0)
                joint[2 * units :, lanes] = jnp.where(places == half, spread, rest).astype(BF16)
        for copy in large:
            copy.wait()
        cross[strip : strip + 2 * units] = joint[: 2 * units]

    outs = [
        shape((2 * units + PARAM_ROWS, width), BF16),
        shape((strip + 2 * units + BIAS_ROWS, width), BF16),
        shape((own // LANES, TAP_ROWS, LANES), F32),
    ]
    args = [bias.reshape(1, units), field, rows_in, rows_out, kernel, *vectors]
    far = pl.BlockSpec(memory_space=pltpu.HBM)
    return pl.pallas_call(
        body,
        out_shape=outs,
        in_specs=[VMEM] + [far] * (len(args) - 1),
        out_specs=[VMEM] * len(outs),
        scratch_shapes=[
            pltpu.VMEM((taps, own), F32),
            pltpu.VMEM((len(vectors), 1, own), F32),
            pltpu.SemaphoreType.DMA((4 + len(vectors),)),
        ],
        compiler_params=pltpu.CompilerParams(vmem_limit_bytes=62 * 1024 * 1024),
        cost_estimate=pl.CostEstimate(flops=10000, bytes_accessed=1000000, transcendentals=0),
    )(*args)


def cut_rows(block, cuts):
    def body(ref, *outs):
        for (start, count), out in zip(cuts, outs):
            out[...] = ref[start : start + count]

    outs = [shape((count, block.shape[1]), block.dtype) for _, count in cuts]
    return call(body, outs, [], [block], size=738000, limit=4)


def row_sends(field, strip):
    row, _ = grid_place()
    starts = [(1 - (row + first) % 2) * (field.shape[0] - strip) for first in range(row_pairings())]
    return [lax.dynamic_slice_in_dim(field, start, strip, 0) for start in starts]


def gathered_shard(in_weight, out_weight, hidden_bias):
    units = in_weight.shape[0]
    groups, count = lax.axis_size("dp"), lax.axis_size("tile")
    place = lax.axis_index("tile")
    member = place % 4

    def mine(array):
        whole = lax.all_gather(array, ("dp", "tile"), axis=0, tiled=True)
        whole = whole.reshape((4, groups * count // 4 * units) + array.shape[1:])
        return lax.dynamic_index_in_dim(whole, member, 0, keepdims=False)

    rows_in, rows_out, bias = mine(in_weight), mine(out_weight), mine(hidden_bias)
    return pack_shard(rows_in, rows_out, bias)


def per_device(
    features,
    cotangent,
    in_weight,
    out_weight,
    hidden_bias,
    kernel,
    conv_bias,
    norm_gain,
    norm_bias,
    layer_scale,
    out_bias,
):
    image_count, _, rows, cols, width = features.shape
    groups, count = lax.axis_size("dp"), lax.axis_size("tile")
    units = in_weight.shape[0]
    pixels = rows * cols
    own = kernel.shape[1]
    strip = MARGIN * cols
    field = features.reshape(pixels, width)
    upstream = cotangent.reshape(pixels, width)

    by_permutes = units % 16 == 0 and groups == 4 and count == 8 and units < width and 4 * own == width
    vectors = [v.reshape(1, own) for v in (conv_bias, norm_gain, norm_bias, layer_scale, out_bias)]
    if by_permutes:
        held, cross, piece = first_sends(field, in_weight, out_weight, hidden_bias, kernel, vectors, strip)
        cross, far_upstream = tile_swap(cross, 4), tile_swap(upstream, 2)
        first, second, far = [across(held, bits) for bits in (1, 2, 3)]
        cross, far_upstream, first, second, far = lax.optimization_barrier(
            (cross, far_upstream, first, second, far)
        )
        params = place_params(piece, [first, second, far])
        bands = cut_rows(cross, [(0, strip)])
        (other,) = cut_rows(cross, [(strip, 2 * units + BIAS_ROWS)])
        other_first, other_second = across(other, 1), across(other, 2)
        (part_in,) = cut_rows(other_first, [(0, units)])
        (part_out,) = cut_rows(other_second, [(units, units + BIAS_ROWS)])
        far_in, far_out = across(part_in, 2), across(part_out, 1)
        after_params = 2 * units + TAP_ROWS // 2
        shards = [
            [(shard, 0, units), (shard, units, units), (shard, after_params, 1)]
            for shard in (held, first, second, far)
        ]
        whole = [(0, units), (units, units), (2 * units, BIAS_ROWS)]
        shards += [[(shard, *rows) for rows in whole] for shard in (other, other_first, other_second)]
        shards.append([(far_in, 0, units), (far_out, 0, units), (far_out, units, BIAS_ROWS)])
    else:
        bands = swap_rows(row_sends(field, strip))
        params = gather_params(kernel, vectors)
        far_upstream = tile_swap(upstream, 2)
        shards = [gathered_shard(in_weight, out_weight, hidden_bias)]
        units = shards[0].shape[0] // 2 - BIAS_ROWS // 2
        shards = [[(shards[0], 0, units), (shards[0], units, units), (shards[0], 2 * units, BIAS_ROWS)]]
    sides = swap_cols(border_columns(field, bands, rows, cols))
    acts, standard, inverse, padded = forward(field, bands, sides, params, rows, cols)
    far_acts = tile_swap(acts, 2)
    if by_permutes:
        far_acts = after(far_acts, far_in, far_out)
    normed = [acts, far_acts, tile_swap(acts, 1), tile_swap(far_acts, 1)]
    upstreams = [upstream, far_upstream, tile_swap(upstream, 1), tile_swap(far_upstream, 1)]
    hidden, back_own, back_send = hidden_values(normed, upstreams, params, shards, units)

    def group_sum(mine, theirs, *others):
        peer = tile_swap(theirs, 1)
        return mine, peer, tile_swap(after(pair_sum(mine, peer), *others), 2)

    back_sums = group_sum(back_own, back_send)
    out_own, out_send, scale_part = project(hidden, upstreams, shards, units)
    back_conv, wire, vector_parts, *back_sends = norm_backward(
        *back_sums, standard, inverse, params, upstream, rows, cols
    )
    parts = kernel_gradient(
        padded, back_conv, vector_parts, scale_part, rows, cols, groups if by_permutes else 1
    )
    back_bands = swap_rows(back_sends)
    back_bands[0] = after(back_bands[0], parts[0])
    back_sides = swap_cols(border_columns(wire, back_bands, rows, cols))
    grad = input_gradient(wire, back_bands, back_sides, params, upstream, rows, cols)
    factor = 1.0 / math.sqrt(image_count * groups * count * pixels)
    if by_permutes:
        total = add_blocks([parts[0]] + [across(parts[bits], bits) for bits in range(1, groups)])
        block = block_output(*group_sum(out_own, out_send, total), params, field)
        total = after(total, *back_sides)
        total = add_blocks([total, tile_swap(total, 1)])
        total = after(add_blocks([total, tile_swap(total, 4)]), grad)
        sums = finish(after(total, block), [tile_swap(total, 2)], factor)
    else:
        block = block_output(*group_sum(out_own, out_send), params, field)
        sums = sum_params(parts[0], factor)
    return (block.reshape(features.shape), grad.reshape(features.shape), *sums)


def solution(mesh):
    placed = (
        P("dp", "tile", None, None, None),
        P("dp", "tile", None, None, None),
        P(("dp", "tile"), None),
        P(("dp", "tile"), None),
        P(("dp", "tile")),
        P(None, "dp"),
        P("dp"),
        P("dp"),
        P("dp"),
        P("dp"),
        P("dp"),
    )
    return jax.shard_map(
        per_device,
        mesh=mesh,
        in_specs=placed,
        out_specs=(
            P("dp", "tile", None, None, None),
            P("dp", "tile", None, None, None),
            P(None, "dp"),
            P("dp"),
            P("dp"),
            P("dp"),
            P("dp"),
        ),
        check_vma=False,
    )
```

```python
import math

import jax
import jax.numpy as jnp
from jax import lax
from jax.experimental import pallas as pl
from jax.experimental.pallas import tpu as pltpu
from jax.sharding import PartitionSpec as P

KS = 7
GX = 4
MARGIN = KS // 2
LANES = 128
PITCH = 32
INSET = 8
TAP_ROWS = 56
BIAS_ROWS = 16
PARAM_ROWS = 32
F32 = jnp.float32
BF16 = jnp.bfloat16

VMEM = pl.BlockSpec(memory_space=pltpu.VMEM)


def call(body, outs, scratch, args, flops=0, size=0, aliases=None, limit=32):
    return pl.pallas_call(
        body,
        out_shape=outs,
        in_specs=[VMEM] * len(args),
        out_specs=[VMEM] * len(outs),
        scratch_shapes=scratch,
        input_output_aliases=aliases or {},
        compiler_params=pltpu.CompilerParams(vmem_limit_bytes=limit * 1024 * 1024),
        cost_estimate=pl.CostEstimate(flops=flops, bytes_accessed=size, transcendentals=0),
    )(*args)


def shape(dims, kind):
    return jax.ShapeDtypeStruct(dims, kind)


def lane_tile(tile):
    return slice(tile * LANES, (tile + 1) * LANES)


def grid_place():
    place = lax.axis_index("tile")
    return place // GX, place % GX


def swap_rows(sends):
    count = lax.axis_size("tile")
    grid_rows = count // GX
    moved = []
    for first, block in enumerate(sends):
        route = []
        for place in range(count):
            row = place // GX
            if row % 2 == first and row + 1 < grid_rows:
                route += [(place, place + GX), (place + GX, place)]
        moved.append(lax.ppermute(block, "tile", route))
    return moved


def swap_cols(sends):
    count = lax.axis_size("tile")
    moved = []
    for first, block in enumerate(sends):
        route = []
        for place in range(count):
            col = place % GX
            if col % 2 == first:
                other = place - col + (col + 1) % GX
                route += [(place, other), (other, place)]
        moved.append(lax.ppermute(block, "tile", route))
    return moved


def row_pairings():
    return 1 if lax.axis_size("tile") // GX == 2 else 2


def above_below(bands, tile):
    row, _ = grid_place()
    even = row % 2 == 0
    first = bands[0][:, lane_tile(tile)].astype(F32)
    second = bands[1][:, lane_tile(tile)].astype(F32) if len(bands) > 1 else jnp.zeros_like(first)
    return jnp.where(even, second, first), jnp.where(even, first, second)


def border_columns(field, bands, rows, cols):
    width = field.shape[1]
    tall = rows + 2 * MARGIN
    packed = -(-tall * MARGIN // 16) * 16

    def body(field_ref, *refs):
        band_refs = refs[: len(bands)]
        outs, full, left, right = refs[len(bands) : -3], refs[-3], refs[-2], refs[-1]
        _, col = grid_place()
        even = col % 2 == 0
        left[...] = jnp.zeros_like(left)
        right[...] = jnp.zeros_like(right)
        for tile in range(width // LANES):
            above, below = above_below(band_refs, tile)
            full[: MARGIN * cols] = above
            full[MARGIN * cols : (MARGIN + rows) * cols] = field_ref[:, lane_tile(tile)].astype(F32)
            full[(MARGIN + rows) * cols :] = below
            for row in range(tall):
                here = pl.ds(row * MARGIN, MARGIN)
                left[here] = full[pl.ds(row * cols, MARGIN)]
                right[here] = full[pl.ds(row * cols + cols - MARGIN, MARGIN)]
            toward_left, toward_right = left[...], right[...]
            outs[0][:, lane_tile(tile)] = jnp.where(even, toward_right, toward_left).astype(BF16)
            outs[1][:, lane_tile(tile)] = jnp.where(even, toward_left, toward_right).astype(BF16)

    return call(
        body,
        [shape((packed, width), BF16)] * 2,
        [pltpu.VMEM((tall * cols, LANES), F32)] + [pltpu.VMEM((packed, LANES), F32)] * 2,
        [field, *bands],
        size=1107000,
        limit=8,
    )


def fill_middle(padded, field_ref, band_refs, rows, cols):
    width = field_ref.shape[1]
    for tile in range(width // LANES):
        above, below = above_below(band_refs, tile)
        for row in range(MARGIN):
            source = slice(row * cols, (row + 1) * cols)
            padded[tile, pl.ds(row * PITCH + INSET, cols)] = above[source]
            padded[tile, pl.ds((MARGIN + rows + row) * PITCH + INSET, cols)] = below[source]
        for row in range(rows):
            padded[tile, pl.ds((MARGIN + row) * PITCH + INSET, cols)] = field_ref[
                row * cols : (row + 1) * cols, lane_tile(tile)
            ].astype(F32)
        for row in range(rows + 2 * MARGIN):
            padded[tile, pl.ds(row * PITCH, INSET)] = jnp.zeros((INSET, LANES), F32)
            padded[tile, pl.ds(row * PITCH + INSET + cols, INSET)] = jnp.zeros((INSET, LANES), F32)


def left_right(edge, side_refs, lanes):
    _, col = grid_place()
    even = col % 2 == 0
    inner = (col > 0) & (col < GX - 1)
    first = side_refs[0][:, lanes].astype(F32)
    second = jnp.where(inner, side_refs[1][:, lanes].astype(F32), 0.0)
    edge[0] = jnp.where(even, second, first)
    edge[1] = jnp.where(even, first, second)


def side_sums(left, right, edge, taps, near, far, rows, cols, flipped):
    for row in range(rows + 2 * MARGIN):
        left[pl.ds(row * cols, MARGIN)] = edge[0, pl.ds(row * MARGIN, MARGIN)]
        start = row * cols + cols + MARGIN - 8
        right[pl.ds(start, MARGIN)] = edge[1, pl.ds(row * MARGIN, MARGIN)]
    for side, sums, shifts in ((left, near, range(MARGIN)), (right, far, range(KS - MARGIN, KS))):
        for b in shifts:
            for r in range(rows + 2 * MARGIN):
                pixels = side[pl.ds(r * cols + b, 8)]
                for a in range(KS):
                    if 0 <= r - a < rows:
                        index = (KS - 1 - a) * KS + KS - 1 - b if flipped else a * KS + b
                        sums[r - a] = sums[r - a] + taps[index] * pixels
    return near, far


def side_scratch(sides, rows, cols):
    tall = rows + 2 * MARGIN
    return [pltpu.VMEM((tall * cols + 8, LANES), F32)] * 2 + [pltpu.VMEM((2, sides[0].shape[0], LANES), F32)]


def window(padded, tile, row, shift, cols):
    return padded[tile, pl.ds(row * PITCH + INSET - MARGIN + shift, cols), :]


def tap_sums(padded, tile, taps, sums, rows, cols, flipped):
    for b in range(KS):
        for r in range(rows + 2 * MARGIN):
            pixels = window(padded, tile, r, b, cols)
            for a in range(KS):
                if 0 <= r - a < rows:
                    index = (KS - 1 - a) * KS + KS - 1 - b if flipped else a * KS + b
                    sums[r - a] = sums[r - a] + taps[index] * pixels
    return sums


def forward_middle(field, bands, params, rows, cols):
    pixels, width = field.shape
    tiles = width // LANES
    span = (rows + 2 * MARGIN) * PITCH

    def body(*refs):
        field_ref, band_refs, (params_ref, padded, out) = refs[0], refs[1:-3], refs[-3:]
        fill_middle(padded, field_ref, band_refs, rows, cols)

        @pl.loop(0, tiles)
        def _(tile):
            taps = [params_ref[tile, pl.ds(t, 1), :] for t in range(KS * KS)]
            start = jnp.broadcast_to(params_ref[tile, pl.ds(KS * KS, 1), :], (cols, LANES))
            sums = tap_sums(padded, tile, taps, [start] * rows, rows, cols, False)
            for row in range(rows):
                out[tile, pl.ds(row * cols, cols), :] = sums[row]

    return call(
        body,
        [shape((tiles, span, LANES), F32), shape((tiles, pixels, LANES), F32)],
        [],
        [field, *bands, params],
        size=8000000,
        limit=16,
    )


def forward_end(partial, sides, params, rows, cols):
    tiles, pixels, _ = partial.shape
    width = tiles * LANES

    def body(partial_ref, first_ref, second_ref, params_ref, acts, standard, inverse, left, right, edge):
        left[...] = jnp.zeros_like(left)
        right[...] = jnp.zeros_like(right)

        @pl.loop(0, tiles)
        def _(tile):
            left_right(edge, (first_ref, second_ref), pl.ds(pl.multiple_of(tile * LANES, LANES), LANES))
            taps = [params_ref[tile, pl.ds(t, 1), :] for t in range(KS * KS)]
            near = [partial_ref[tile, pl.ds(row * cols, 8), :] for row in range(rows)]
            far = [partial_ref[tile, pl.ds((row + 1) * cols - 8, 8), :] for row in range(rows)]
            if cols > 16:
                standard[tile] = partial_ref[tile]
            near, far = side_sums(left, right, edge, taps, near, far, rows, cols, False)
            for row in range(rows):
                standard[tile, pl.ds(row * cols, 8), :] = near[row]
                standard[tile, pl.ds((row + 1) * cols - 8, 8), :] = far[row]

        total = standard[0]
        for tile in range(1, tiles):
            total = total + standard[tile]
        average = jnp.sum(total, axis=1, keepdims=True) * (1.0 / width)
        total = jnp.zeros((pixels, LANES), F32)
        for tile in range(tiles):
            centered = standard[tile] - average
            total = total + centered * centered
        scale = lax.rsqrt(jnp.sum(total, axis=1, keepdims=True) * (1.0 / width) + 1e-06)
        inverse[...] = jnp.broadcast_to(scale, (pixels, LANES))
        for tile in range(tiles):
            value = (standard[tile] - average) * scale
            standard[tile] = value
            gain = params_ref[tile, KS * KS + 1 : KS * KS + 2, :]
            shift = params_ref[tile, KS * KS + 2 : KS * KS + 3, :]
            acts[:, lane_tile(tile)] = (value * gain + shift).astype(BF16)

    return call(
        body,
        [
            shape((pixels, width), BF16),
            shape((tiles, pixels, LANES), F32),
            shape((pixels, LANES), F32),
        ],
        side_scratch(sides, rows, cols),
        [partial, *sides, params],
        size=6000000,
        limit=8,
    )


def with_sides(padded, sides, rows, cols):
    tiles = padded.shape[0]

    def body(padded_ref, first_ref, second_ref, out, edge):
        for tile in range(tiles):
            out[tile] = padded_ref[tile]
            left_right(edge, (first_ref, second_ref), lane_tile(tile))
            for row in range(rows + 2 * MARGIN):
                here = pl.ds(row * MARGIN, MARGIN)
                out[tile, pl.ds(row * PITCH + INSET - MARGIN, MARGIN)] = edge[0, here]
                out[tile, pl.ds(row * PITCH + INSET + cols, MARGIN)] = edge[1, here]

    return call(
        body,
        [shape(padded.shape, F32)],
        [pltpu.VMEM((2, sides[0].shape[0], LANES), F32)],
        [padded, *sides],
        size=2000000,
        limit=8,
    )[0]


def arrays_of(shards):
    arrays, slots = [], []
    for shard in shards:
        places = []
        for array, start, _ in shard:
            known = [index for index, other in enumerate(arrays) if other is array]
            if not known:
                arrays.append(array)
            places.append((known[0] if known else len(arrays) - 1, start))
        slots.append(places)
    return arrays, slots


def hidden_scratch(rows, units, width):
    return [
        pltpu.VMEM((rows, width), BF16),
        pltpu.VMEM((rows, width), BF16),
        pltpu.VMEM((rows, units), F32),
        pltpu.VMEM((rows, units), F32),
        pltpu.VMEM((rows, units), BF16),
    ]


def weight_scratch(units, width):
    return [pltpu.VMEM((units, width), BF16), pltpu.VMEM((units, width), BF16)]


def place_rows(norm, back, normed_refs, up_refs, starts, params_ref):
    pixels = normed_refs[0].shape[0]
    for index, start in enumerate(starts):
        here = slice(index * pixels, (index + 1) * pixels)
        norm[here] = normed_refs[index][...]
        for tile in range(norm.shape[1] // LANES):
            lanes = lane_tile(tile)
            layer = params_ref[tile, KS * KS + 3 : KS * KS + 4, :]
            rows = up_refs[index][start : start + pixels, lanes]
            back[here, lanes] = (rows.astype(F32) * layer).astype(BF16)


def place_weights(win, wout, shard_refs, slots, units):
    for index, (rows_in, rows_out, _) in enumerate(slots):
        here = slice(index * units, (index + 1) * units)
        win[here] = shard_refs[rows_in[0]][rows_in[1] : rows_in[1] + units]
        wout[here] = shard_refs[rows_out[0]][rows_out[1] : rows_out[1] + units]
    lines = [shard_refs[bias[0]][bias[1] : bias[1] + 1, :units].astype(F32) for *_, bias in slots]
    return lines[0] if len(lines) == 1 else jnp.concatenate(lines, axis=1)


def hidden_block(norm, back, win, wout, line, hid, pre, slope, bpre):
    step = 32
    across = (((1,), (1,)), ((), ()))
    pre[...] = lax.dot_general(norm[...], win[...], across, preferred_element_type=F32) + line
    slope[...] = lax.dot_general(back[...], wout[...], across, preferred_element_type=F32)

    @pl.loop(0, norm.shape[0] // step)
    def _(part):
        here = pl.ds(pl.multiple_of(part * step, step), step)
        value = pre[here, :]
        half = 0.5 * (1.0 + lax.erf(value * 0.7071067811865476))
        hid[here, :] = (value * half).astype(BF16)
        bell = jnp.exp(-0.5 * value * value) * 0.3989422804014327
        bpre[here, :] = (slope[here, :] * (half + value * bell)).astype(BF16)

    return jnp.dot(bpre[...], win[...], preferred_element_type=F32)


def hidden_near(normed, upstream, params, shards, units):
    pixels, width = normed[0].shape
    arrays, slots = arrays_of(shards)
    members, count, every = len(normed), len(arrays), len(shards) * units
    rows = members * pixels

    def body(*refs):
        normed_refs, up_refs, params_ref = refs[:members], refs[members : 2 * members], refs[2 * members]
        shard_refs, rest = refs[2 * members + 1 : 2 * members + 1 + count], refs[2 * members + 1 + count :]
        hid, total, win, wout, norm, back, pre, slope, bpre = rest
        place_rows(norm, back, normed_refs, up_refs, [start for _, start in upstream], params_ref)
        line = place_weights(win, wout, shard_refs, slots, units)
        total[...] = hidden_block(norm, back, win, wout, line, hid, pre, slope, bpre)

    return call(
        body,
        [shape((rows, every), BF16), shape((rows, width), F32)],
        weight_scratch(every, width) + hidden_scratch(rows, every, width),
        [*normed, *[array for array, _ in upstream], params, *arrays],
        size=7000000,
        limit=20,
    )


def hidden_far(normed, upstream, params, shards, early, near_sum, units):
    pixels, width = normed[0].shape
    arrays, slots = arrays_of(shards)
    members, count = len(normed), len(arrays)
    half = members // 2
    rows, every, late = half * pixels, len(shards) * units, (len(shards) - early) * units

    def body(*refs):
        normed_refs, up_refs, params_ref = refs[:members], refs[members : 2 * members], refs[2 * members]
        shard_refs, rest = refs[2 * members + 1 : 2 * members + 1 + count], refs[2 * members + 1 + count :]
        sum_ref, near_hid, far_hid, stay, send = rest[:5]
        win, wout, late_in, late_out = rest[5:9]
        near_norm, near_back, near_pre, near_slope, near_bpre = rest[9:14]
        norm, back, pre, slope, bpre = rest[14:]
        starts = [start for _, start in upstream]
        place_rows(near_norm, near_back, normed_refs[:half], up_refs[:half], starts[:half], params_ref)
        place_rows(norm, back, normed_refs[half:], up_refs[half:], starts[half:], params_ref)
        line = place_weights(win, wout, shard_refs, slots, units)
        late_line = place_weights(late_in, late_out, shard_refs, slots[early:], units)
        far = hidden_block(norm, back, win, wout, line, far_hid, pre, slope, bpre)
        near = sum_ref[...] + hidden_block(
            near_norm, near_back, late_in, late_out, late_line, near_hid, near_pre, near_slope, near_bpre
        )
        stay[:pixels] = near[:pixels]
        stay[pixels:] = far[:pixels]
        send[:pixels] = near[pixels:].astype(BF16)
        send[pixels:] = far[pixels:].astype(BF16)

    return call(
        body,
        [
            shape((rows, late), BF16),
            shape((rows, every), BF16),
            shape((rows, width), F32),
            shape((rows, width), BF16),
        ],
        weight_scratch(every, width)
        + weight_scratch(late, width)
        + hidden_scratch(rows, late, width)
        + hidden_scratch(rows, every, width),
        [*normed, *[array for array, _ in upstream], params, *arrays, near_sum],
        size=9000000,
        limit=28,
    )


def project(hiddens, upstream, shards, units):
    pixels, width = upstream[0][0].shape[0], upstream[0][0].shape[1]
    arrays, slots = arrays_of([[rows_out] for _, rows_out, _ in shards])
    members, count, every = len(upstream), len(arrays), len(shards) * units
    half = members // 2 * pixels
    early, late, _ = hiddens

    def body(early_ref, late_ref, far_ref, *refs):
        up_refs, shard_refs = refs[:members], refs[members : members + count]
        stay, send, scale, wout, hid = refs[members + count :]
        for index, ((slot, start),) in enumerate(slots):
            wout[index * units : (index + 1) * units] = shard_refs[slot][start : start + units]
        hid[:half, : early.shape[1]] = early_ref[...]
        hid[:half, early.shape[1] :] = late_ref[...]
        hid[half:] = far_ref[...]
        projected = jnp.dot(hid[...], wout[...], preferred_element_type=F32)
        stay[:pixels] = projected[:pixels]
        stay[pixels:] = projected[half : half + pixels]
        send[:pixels] = projected[pixels:half].astype(BF16)
        send[pixels:] = projected[half + pixels :].astype(BF16)
        for tile in range(width // LANES):
            lanes = lane_tile(tile)
            sums = jnp.zeros((pixels, LANES), F32)
            for index in range(members):
                rows = projected[index * pixels : (index + 1) * pixels, lanes]
                start = upstream[index][1]
                sums = sums + up_refs[index][start : start + pixels, lanes].astype(F32) * rows
            scale[tile] = jnp.broadcast_to(jnp.sum(sums, axis=0, keepdims=True), (8, LANES))

    return call(
        body,
        [shape((half, width), F32), shape((half, width), BF16), shape((width // LANES, 8, LANES), F32)],
        [pltpu.VMEM((every, width), BF16), pltpu.VMEM((2 * half, every), BF16)],
        [*hiddens, *[array for array, _ in upstream], *arrays],
        size=3911400,
        limit=20,
    )


def pair_sum(mine, peer):
    rows, width = mine.shape
    half = rows // 2

    def body(mine_ref, peer_ref, out):
        out[...] = (mine_ref[half:, :] + peer_ref[half:, :].astype(F32)).astype(BF16)

    return call(body, [shape((half, width), BF16)], [], [mine, peer], size=738000, limit=4)[0]


def norm_backward(own, peer, far, standard, inverse, params, upstream, rows, cols):
    pixels, width = upstream.shape
    tiles = width // LANES
    strip = MARGIN * cols

    def body(own_ref, peer_ref, far_ref, std, inv, params_ref, up_ref, conv, wire, vectors, *sends):
        zero = jnp.zeros((pixels, LANES), F32)
        plain, mixed = zero, zero
        for tile in range(tiles):
            lanes = lane_tile(tile)
            normed = own_ref[:pixels, lanes] + peer_ref[:pixels, lanes].astype(F32) + far_ref[:, lanes].astype(F32)
            gain = params_ref[tile, KS * KS + 1 : KS * KS + 2, :]
            scaled = normed * gain
            product = normed * std[tile]
            conv[tile] = scaled
            plain = plain + scaled
            mixed = mixed + product * gain
            vectors[tile] = jnp.zeros((8, LANES), F32)
            vectors[tile, 1:2, :] = jnp.sum(product, axis=0, keepdims=True)
            vectors[tile, 2:3, :] = jnp.sum(normed, axis=0, keepdims=True)
            out_bias = params_ref[tile, KS * KS + 4 : KS * KS + 5, :]
            vectors[tile, 3:4, :] = jnp.sum(up_ref[:, lanes].astype(F32), axis=0, keepdims=True) * out_bias
        plain = jnp.sum(plain, axis=1, keepdims=True) * (1.0 / width)
        mixed = jnp.sum(mixed, axis=1, keepdims=True) * (1.0 / width)
        for tile in range(tiles):
            value = inv[...] * (conv[tile] - plain - std[tile] * mixed)
            conv[tile] = value
            wire[:, lane_tile(tile)] = value.astype(BF16)
            vectors[tile, 0:1, :] = jnp.sum(value, axis=0, keepdims=True)
        row, _ = grid_place()
        even = row % 2 == 0
        top, bottom = wire[:strip, :], wire[pixels - strip :, :]
        sends[0][...] = jnp.where(even, bottom, top)
        if len(sends) > 1:
            sends[1][...] = jnp.where(even, top, bottom)

    return call(
        body,
        [
            shape((tiles, pixels, LANES), F32),
            shape((pixels, width), BF16),
            shape((tiles, 8, LANES), F32),
        ]
        + [shape((strip, width), BF16)] * row_pairings(),
        [],
        [own, peer, far, standard, inverse, params, upstream],
        size=1845000,
        limit=16,
    )


def block_output(own, peer, far, params, field):
    pixels, width = field.shape

    def body(own_ref, peer_ref, far_ref, params_ref, field_ref, block):
        for tile in range(width // LANES):
            lanes = lane_tile(tile)
            out_bias = params_ref[tile, KS * KS + 4 : KS * KS + 5, :]
            layer = params_ref[tile, KS * KS + 3 : KS * KS + 4, :]
            projected = own_ref[:pixels, lanes] + peer_ref[:pixels, lanes].astype(F32) + far_ref[:, lanes].astype(F32)
            block[:, lanes] = (field_ref[:, lanes].astype(F32) + layer * (projected + out_bias)).astype(BF16)

    return call(
        body,
        [shape((pixels, width), BF16)],
        [],
        [own, peer, far, params, field],
        size=3210300,
        limit=8,
    )[0]


def kernel_gradient(padded, back_conv, vectors, scale_part, rows, cols, groups):
    tiles = back_conv.shape[0]
    share = tiles // groups

    def body(padded_ref, conv, vectors_ref, scale_ref, *refs):
        outs, out = refs[:-1], refs[-1]

        @pl.loop(0, tiles)
        def _(tile):
            grads = [conv[tile, pl.ds(row * cols, cols), :] for row in range(rows)]
            for b in range(KS):
                sums = [None] * KS
                for r in range(rows + 2 * MARGIN):
                    pixels = window(padded_ref, tile, r, b, cols)
                    for a in range(KS):
                        if 0 <= r - a < rows:
                            term = pixels * grads[r - a]
                            sums[a] = term if sums[a] is None else sums[a] + term
                for a in range(KS):
                    out[tile, pl.ds(a * KS + b, 1), :] = jnp.sum(sums[a], axis=0, keepdims=True)
            out[tile, pl.ds(KS * KS, TAP_ROWS - KS * KS), :] = vectors_ref[tile, : TAP_ROWS - KS * KS, :]
            out[tile, pl.ds(KS * KS + 3, 1), :] += scale_ref[tile, :1, :]

        if groups == 1:
            outs[0][...] = out[...]
        else:
            me = lax.axis_index("dp")
            for bits in range(groups):
                for part in range(share):
                    outs[bits][part] = out[(me ^ bits) * share + part]

    return call(
        body,
        [shape((share, TAP_ROWS, LANES), F32)] * groups,
        [pltpu.VMEM((tiles, TAP_ROWS, LANES), F32)],
        [padded, back_conv, vectors, scale_part],
        size=7380000,
        limit=8,
    )


def gradient_middle(wire, bands, params, upstream, rows, cols):
    pixels, width = wire.shape
    tiles = width // LANES
    span = (rows + 2 * MARGIN) * PITCH

    def body(*refs):
        wire_ref, band_refs, (params_ref, up_ref, out, padded) = refs[0], refs[1:-4], refs[-4:]
        fill_middle(padded, wire_ref, band_refs, rows, cols)

        @pl.loop(0, tiles)
        def _(tile):
            lanes = pl.ds(pl.multiple_of(tile * LANES, LANES), LANES)
            taps = [params_ref[tile, pl.ds(t, 1), :] for t in range(KS * KS)]
            start = [up_ref[pl.ds(row * cols, cols), lanes].astype(F32) for row in range(rows)]
            sums = tap_sums(padded, tile, taps, start, rows, cols, True)
            for row in range(rows):
                out[tile, pl.ds(row * cols, cols), :] = sums[row]

    return call(
        body,
        [shape((tiles, pixels, LANES), F32)],
        [pltpu.VMEM((tiles, span, LANES), F32)],
        [wire, *bands, params, upstream],
        size=8000000,
        limit=16,
    )[0]


def gradient_end(partial, sides, params, rows, cols):
    tiles, pixels, _ = partial.shape

    def body(partial_ref, first_ref, second_ref, params_ref, out, left, right, edge):
        left[...] = jnp.zeros_like(left)
        right[...] = jnp.zeros_like(right)

        @pl.loop(0, tiles)
        def _(tile):
            lanes = pl.ds(pl.multiple_of(tile * LANES, LANES), LANES)
            left_right(edge, (first_ref, second_ref), lanes)
            taps = [params_ref[tile, pl.ds(t, 1), :] for t in range(KS * KS)]
            near = [partial_ref[tile, pl.ds(row * cols, 8), :] for row in range(rows)]
            far = [partial_ref[tile, pl.ds((row + 1) * cols - 8, 8), :] for row in range(rows)]
            near, far = side_sums(left, right, edge, taps, near, far, rows, cols, True)
            for row in range(rows):
                middle = partial_ref[tile, pl.ds(row * cols + 8, cols - 16), :] if cols > 16 else None
                whole = [near[row]] + ([middle] if cols > 16 else []) + [far[row]]
                out[pl.ds(row * cols, cols), lanes] = jnp.concatenate(whole).astype(BF16)

    return call(
        body,
        [shape((pixels, tiles * LANES), BF16)],
        side_scratch(sides, rows, cols),
        [partial, *sides, params],
        size=5000000,
        limit=8,
    )[0]


def across(block, bits):
    groups = lax.axis_size("dp")
    return lax.ppermute(block, "dp", [(i, i ^ bits) for i in range(groups)])


def tile_swap(block, bits):
    return lax.ppermute(block, "tile", [(i, i ^ bits) for i in range(lax.axis_size("tile"))])


def place_params(own, joints):
    share, rows, _ = own.shape
    half = rows // 2

    def body(own_ref, *refs):
        joint_refs, out = refs[:-1], refs[-1]
        me = lax.axis_index("dp")
        for part in range(share):
            out[me * share + part] = own_ref[part]
        for bits, ref in enumerate(joint_refs, 1):
            start = ref.shape[0] - PARAM_ROWS
            for part in range(2 * share):
                high = ref[start:, lane_tile(2 * part)].astype(F32)
                value = high + ref[start:, lane_tile(2 * part + 1)].astype(F32)
                out[(me ^ bits) * share + part // 2, pl.ds(part % 2 * half, half), :] = value[:half]

    return call(
        body,
        [shape((4 * share, rows, LANES), F32)],
        [],
        [own, *joints],
        size=738000,
        limit=4,
    )[0]


def gather_params(kernel, vectors):
    own = kernel.shape[1]
    pack = jnp.concatenate([kernel, *vectors, jnp.zeros((TAP_ROWS - KS * KS - len(vectors), own), F32)])
    whole = lax.all_gather(pack, "dp", axis=1, tiled=True)
    return whole.reshape(TAP_ROWS, -1, LANES).transpose(1, 0, 2)


def sum_params(parts, factor):
    flat = parts.transpose(1, 0, 2).reshape(TAP_ROWS, -1)
    sums = lax.psum(lax.psum_scatter(flat, "dp", scatter_dimension=1, tiled=True), "tile") * factor
    taps = KS * KS
    return [sums[:taps]] + [sums[taps + index] for index in range(4)]


def add_blocks(blocks):
    def body(*refs):
        value = refs[0][...]
        for ref in refs[1:-1]:
            value = value + ref[...]
        refs[-1][...] = value

    return call(body, [shape(blocks[0].shape, F32)], [], blocks, size=738000, limit=4)[0]


def finish(total, moved, factor):
    tiles, rows, _ = total.shape
    taps = KS * KS

    def body(*refs):
        outs = refs[1 + len(moved) :]
        for tile in range(tiles):
            value = refs[0][tile]
            for other in refs[1 : 1 + len(moved)]:
                value = value + other[tile]
            value = value * factor
            outs[0][:, lane_tile(tile)] = value[:taps]
            for index in range(4):
                outs[1 + index][:, lane_tile(tile)] = value[taps + index : taps + index + 1]

    taps_sum, *vectors = call(
        body,
        [shape((taps, tiles * LANES), F32)] + [shape((1, tiles * LANES), F32)] * 4,
        [],
        [total, *moved],
        size=2214000,
        limit=4,
    )
    return [taps_sum] + [v.reshape(-1) for v in vectors]


def after(block, *others):
    return lax.optimization_barrier((block, *others))[0]


def pack_shard(rows_in, rows_out, bias):
    units, width = rows_in.shape
    row = jnp.pad(bias.reshape(1, units), ((0, BIAS_ROWS - 1), (0, width - units)))
    return jnp.concatenate([rows_in, rows_out, row])


def first_sends(field, rows_in, rows_out, bias, kernel, vectors, strip):
    pixels, width = field.shape
    units = rows_in.shape[0]
    taps, own = kernel.shape
    half = TAP_ROWS // 2

    def body(bias_ref, field_ref, in_ref, out_ref, kernel_ref, *refs):
        vector_refs, refs = refs[: len(vectors)], refs[len(vectors) :]
        joint, cross, pack, tap_stage, vector_stage, sems = refs
        row, _ = grid_place()
        start = pl.multiple_of((1 - row % 2) * (pixels - strip), 16)
        small = [pltpu.make_async_copy(kernel_ref, tap_stage, sems.at[0])]
        for index, ref in enumerate(vector_refs):
            small.append(pltpu.make_async_copy(ref, vector_stage.at[index], sems.at[1 + index]))
        at = 1 + len(vectors)
        large = [
            pltpu.make_async_copy(field_ref.at[pl.ds(start, strip)], cross.at[pl.ds(0, strip)], sems.at[at]),
            pltpu.make_async_copy(in_ref, joint.at[pl.ds(0, units)], sems.at[at + 1]),
            pltpu.make_async_copy(out_ref, joint.at[pl.ds(units, units)], sems.at[at + 2]),
        ]
        for copy in small + large:
            copy.start()
        line = jnp.concatenate([bias_ref[...].astype(F32), jnp.zeros((1, width - units), F32)], axis=1)
        line = jnp.broadcast_to(line, (BIAS_ROWS, width))
        places = lax.broadcasted_iota(jnp.int32, (BIAS_ROWS, width), 0)
        cross[strip + 2 * units :] = jnp.where(places == 0, line, 0.0).astype(BF16)
        for copy in small:
            copy.wait()
        for tile in range(own // LANES):
            pack[tile, TAP_ROWS - 8 :, :] = jnp.zeros((8, LANES), F32)
            pack[tile, :taps, :] = tap_stage[:, lane_tile(tile)]
            for index in range(len(vectors)):
                pack[tile, taps + index : taps + index + 1, :] = vector_stage[index, :, lane_tile(tile)]
        for part in range(2 * own // LANES):
            value = pack[part // 2, part % 2 * half : (part % 2 + 1) * half, :]
            value = jnp.concatenate([value, jnp.zeros((PARAM_ROWS - half, LANES), F32)])
            high = value.astype(BF16).astype(F32)
            for side, rest in enumerate((high, value - high)):
                lanes = lane_tile(2 * part + side)
                spread = jnp.broadcast_to(line[:1, lanes], (PARAM_ROWS, LANES))
                places = lax.broadcasted_iota(jnp.int32, (PARAM_ROWS, LANES), 0)
                joint[2 * units :, lanes] = jnp.where(places == half, spread, rest).astype(BF16)
        for copy in large:
            copy.wait()
        cross[strip : strip + 2 * units] = joint[: 2 * units]

    outs = [
        shape((2 * units + PARAM_ROWS, width), BF16),
        shape((strip + 2 * units + BIAS_ROWS, width), BF16),
        shape((own // LANES, TAP_ROWS, LANES), F32),
    ]
    args = [bias.reshape(1, units), field, rows_in, rows_out, kernel, *vectors]
    far = pl.BlockSpec(memory_space=pltpu.HBM)
    return pl.pallas_call(
        body,
        out_shape=outs,
        in_specs=[VMEM] + [far] * (len(args) - 1),
        out_specs=[VMEM] * len(outs),
        scratch_shapes=[
            pltpu.VMEM((taps, own), F32),
            pltpu.VMEM((len(vectors), 1, own), F32),
            pltpu.SemaphoreType.DMA((4 + len(vectors),)),
        ],
        compiler_params=pltpu.CompilerParams(vmem_limit_bytes=62 * 1024 * 1024),
        cost_estimate=pl.CostEstimate(flops=10000, bytes_accessed=1000000, transcendentals=0),
    )(*args)


def cut_rows(block, cuts):
    def body(ref, *outs):
        for (start, count), out in zip(cuts, outs):
            out[...] = ref[start : start + count]

    outs = [shape((count, block.shape[1]), block.dtype) for _, count in cuts]
    return call(body, outs, [], [block], size=738000, limit=4)


def row_sends(field, strip):
    row, _ = grid_place()
    starts = [(1 - (row + first) % 2) * (field.shape[0] - strip) for first in range(row_pairings())]
    return [lax.dynamic_slice_in_dim(field, start, strip, 0) for start in starts]


def gathered_shard(in_weight, out_weight, hidden_bias):
    units = in_weight.shape[0]
    groups, count = lax.axis_size("dp"), lax.axis_size("tile")
    place = lax.axis_index("tile")
    member = place % 4

    def mine(array):
        whole = lax.all_gather(array, ("dp", "tile"), axis=0, tiled=True)
        whole = whole.reshape((4, groups * count // 4 * units) + array.shape[1:])
        return lax.dynamic_index_in_dim(whole, member, 0, keepdims=False)

    rows_in, rows_out, bias = mine(in_weight), mine(out_weight), mine(hidden_bias)
    return pack_shard(rows_in, rows_out, bias)


def per_device(
    features,
    cotangent,
    in_weight,
    out_weight,
    hidden_bias,
    kernel,
    conv_bias,
    norm_gain,
    norm_bias,
    layer_scale,
    out_bias,
):
    image_count, _, rows, cols, width = features.shape
    groups, count = lax.axis_size("dp"), lax.axis_size("tile")
    units = in_weight.shape[0]
    pixels = rows * cols
    own = kernel.shape[1]
    strip = MARGIN * cols
    field = features.reshape(pixels, width)
    upstream = cotangent.reshape(pixels, width)

    by_permutes = units % 16 == 0 and groups == 4 and count == 8 and units < width and 4 * own == width
    vectors = [v.reshape(1, own) for v in (conv_bias, norm_gain, norm_bias, layer_scale, out_bias)]
    if by_permutes:
        held, cross, piece = first_sends(field, in_weight, out_weight, hidden_bias, kernel, vectors, strip)
        cross, far_upstream = tile_swap(cross, 4), tile_swap(upstream, 2)
        first, second, far = [across(held, bits) for bits in (1, 2, 3)]
        cross, far_upstream, first, second, far = lax.optimization_barrier(
            (cross, far_upstream, first, second, far)
        )
        params = place_params(piece, [first, second, far])
        bands = cut_rows(cross, [(0, strip)])
        (other,) = cut_rows(cross, [(strip, 2 * units + BIAS_ROWS)])
        other_first, other_second = across(other, 1), across(other, 2)
        (part_in,) = cut_rows(other_first, [(0, units)])
        (part_out,) = cut_rows(other_second, [(units, units + BIAS_ROWS)])
        far_in, far_out = across(part_in, 2), across(part_out, 1)
        after_params = 2 * units + TAP_ROWS // 2
        shards = [
            [(shard, 0, units), (shard, units, units), (shard, after_params, 1)]
            for shard in (held, first, second, far)
        ]
        whole = [(0, units), (units, units), (2 * units, BIAS_ROWS)]
        shards += [[(shard, *rows) for rows in whole] for shard in (other, other_first, other_second)]
        shards.append([(far_in, 0, units), (far_out, 0, units), (far_out, units, BIAS_ROWS)])
    else:
        bands = swap_rows(row_sends(field, strip))
        params = gather_params(kernel, vectors)
        far_upstream = tile_swap(upstream, 2)
        shards = [gathered_shard(in_weight, out_weight, hidden_bias)]
        units = shards[0].shape[0] // 2 - BIAS_ROWS // 2
        shards = [[(shards[0], 0, units), (shards[0], units, units), (shards[0], 2 * units, BIAS_ROWS)]]
    sides = swap_cols(border_columns(field, bands, rows, cols))
    padded, partial = forward_middle(field, bands, params, rows, cols)
    acts, standard, inverse = forward_end(partial, sides, params, rows, cols)
    padded = with_sides(padded, sides, rows, cols)
    near_acts, far_acts = tile_swap(acts, 1), tile_swap(acts, 2)
    near_upstream = tile_swap(upstream, 1)
    early = max(1, len(shards) - 1)
    if by_permutes:
        chip = [(upstream, 0), (near_upstream, 0)]
        near_hidden, near_sum = hidden_near([acts, near_acts], chip, params, shards[:early], units)
        far_acts = after(far_acts, far_in, far_out, padded, near_sum)
    else:
        half = units // 2
        cuts = [[(array, first + at, half) for array, first, _ in shards[0][:2]] for at in (0, half)]
        bias, row, _ = shards[0][2]
        lines = [jnp.pad(bias[row : row + 1, at : at + half], ((0, 0), (0, 0))) for at in (0, half)]
        shards = [[*cut, (line, 0, 1)] for cut, line in zip(cuts, lines)]
        units = half
        chip = [(upstream, 0), (near_upstream, 0)]
        near_hidden, near_sum = hidden_near([acts, near_acts], chip, params, shards[:early], units)
    normed = [acts, near_acts, far_acts, tile_swap(far_acts, 1)]
    upstreams = [*chip, (far_upstream, 0), (tile_swap(far_upstream, 1), 0)]
    late_hidden, far_hidden, back_own, back_send = hidden_far(
        normed, upstreams, params, shards, early, near_sum, units
    )
    hiddens = [near_hidden, late_hidden, far_hidden]

    def group_sum(mine, theirs, *others):
        peer = tile_swap(theirs, 1)
        return mine, peer, tile_swap(after(pair_sum(mine, peer), *others), 2)

    back_sums = group_sum(back_own, back_send)
    out_own, out_send, scale_part = project(hiddens, upstreams, shards, units)
    back_conv, wire, vector_parts, *back_sends = norm_backward(
        *back_sums, standard, inverse, params, upstream, rows, cols
    )
    parts = kernel_gradient(
        padded, back_conv, vector_parts, scale_part, rows, cols, groups if by_permutes else 1
    )
    back_bands = swap_rows([after(send, parts[0]) for send in back_sends])
    back_sides = swap_cols(border_columns(wire, back_bands, rows, cols))
    middle = gradient_middle(wire, back_bands, params, upstream, rows, cols)
    grad = gradient_end(middle, back_sides, params, rows, cols)
    factor = 1.0 / math.sqrt(image_count * groups * count * pixels)
    if by_permutes:
        total = add_blocks([parts[0]] + [across(parts[bits], bits) for bits in range(1, groups)])
        block = block_output(*group_sum(out_own, out_send, total), params, field)
        total = after(total, *back_bands)
        total = add_blocks([total, tile_swap(total, 1)])
        total = after(add_blocks([total, tile_swap(total, 4)]), middle, *back_sides)
        sums = finish(after(total, block, grad), [tile_swap(total, 2)], factor)
    else:
        block = block_output(*group_sum(out_own, out_send), params, field)
        sums = sum_params(parts[0], factor)
    return (block.reshape(features.shape), grad.reshape(features.shape), *sums)


def solution(mesh):
    placed = (
        P("dp", "tile", None, None, None),
        P("dp", "tile", None, None, None),
        P(("dp", "tile"), None),
        P(("dp", "tile"), None),
        P(("dp", "tile")),
        P(None, "dp"),
        P("dp"),
        P("dp"),
        P("dp"),
        P("dp"),
        P("dp"),
    )
    return jax.shard_map(
        per_device,
        mesh=mesh,
        in_specs=placed,
        out_specs=(
            P("dp", "tile", None, None, None),
            P("dp", "tile", None, None, None),
            P(None, "dp"),
            P("dp"),
            P("dp"),
            P("dp"),
            P("dp"),
        ),
        check_vma=False,
    )
```

```python
import math

import jax
import jax.numpy as jnp
from jax import lax
from jax.experimental import pallas as pl
from jax.experimental.pallas import tpu as pltpu
from jax.sharding import PartitionSpec as P

KS = 7
GX = 4
MARGIN = KS // 2
LANES = 128
PITCH = 32
INSET = 8
TAP_ROWS = 56
BIAS_ROWS = 8
PARAM_ROWS = 32
F32 = jnp.float32
BF16 = jnp.bfloat16

VMEM = pl.BlockSpec(memory_space=pltpu.VMEM)


def call(body, outs, scratch, args, flops=0, size=0, aliases=None, limit=32):
    return pl.pallas_call(
        body,
        out_shape=outs,
        in_specs=[VMEM] * len(args),
        out_specs=[VMEM] * len(outs),
        scratch_shapes=scratch,
        input_output_aliases=aliases or {},
        compiler_params=pltpu.CompilerParams(vmem_limit_bytes=limit * 1024 * 1024),
        cost_estimate=pl.CostEstimate(flops=flops, bytes_accessed=size, transcendentals=0),
    )(*args)


def shape(dims, kind):
    return jax.ShapeDtypeStruct(dims, kind)


def lane_tile(tile):
    return slice(tile * LANES, (tile + 1) * LANES)


def grid_place():
    place = lax.axis_index("tile")
    return place // GX, place % GX


def swap_rows(sends):
    count = lax.axis_size("tile")
    grid_rows = count // GX
    moved = []
    for first, block in enumerate(sends):
        route = []
        for place in range(count):
            row = place // GX
            if row % 2 == first and row + 1 < grid_rows:
                route += [(place, place + GX), (place + GX, place)]
        moved.append(lax.ppermute(block, "tile", route))
    return moved


def swap_cols(sends):
    count = lax.axis_size("tile")
    moved = []
    for first, block in enumerate(sends):
        route = []
        for place in range(count):
            col = place % GX
            if col % 2 == first:
                other = place - col + (col + 1) % GX
                route += [(place, other), (other, place)]
        moved.append(lax.ppermute(block, "tile", route))
    return moved


def row_pairings():
    return 1 if lax.axis_size("tile") // GX == 2 else 2


def above_below(bands, tile):
    row, _ = grid_place()
    even = row % 2 == 0
    first = bands[0][:, lane_tile(tile)].astype(F32)
    second = bands[1][:, lane_tile(tile)].astype(F32) if len(bands) > 1 else jnp.zeros_like(first)
    return jnp.where(even, second, first), jnp.where(even, first, second)


def border_columns(field, bands, rows, cols):
    width = field.shape[1]
    tall = rows + 2 * MARGIN
    packed = -(-tall * MARGIN // 16) * 16

    def body(field_ref, *refs):
        band_refs = refs[: len(bands)]
        outs, full, left, right = refs[len(bands) : -3], refs[-3], refs[-2], refs[-1]
        _, col = grid_place()
        even = col % 2 == 0
        left[...] = jnp.zeros_like(left)
        right[...] = jnp.zeros_like(right)
        for tile in range(width // LANES):
            above, below = above_below(band_refs, tile)
            full[: MARGIN * cols] = above
            full[MARGIN * cols : (MARGIN + rows) * cols] = field_ref[:, lane_tile(tile)].astype(F32)
            full[(MARGIN + rows) * cols :] = below
            for row in range(tall):
                here = pl.ds(row * MARGIN, MARGIN)
                left[here] = full[pl.ds(row * cols, MARGIN)]
                right[here] = full[pl.ds(row * cols + cols - MARGIN, MARGIN)]
            toward_left, toward_right = left[...], right[...]
            outs[0][:, lane_tile(tile)] = jnp.where(even, toward_right, toward_left).astype(BF16)
            outs[1][:, lane_tile(tile)] = jnp.where(even, toward_left, toward_right).astype(BF16)

    return call(
        body,
        [shape((packed, width), BF16)] * 2,
        [pltpu.VMEM((tall * cols, LANES), F32)] + [pltpu.VMEM((packed, LANES), F32)] * 2,
        [field, *bands],
        size=1107000,
        limit=8,
    )


def fill_middle(padded, field_ref, band_refs, rows, cols):
    width = field_ref.shape[1]
    for tile in range(width // LANES):
        above, below = above_below(band_refs, tile)
        for row in range(MARGIN):
            source = slice(row * cols, (row + 1) * cols)
            padded[tile, pl.ds(row * PITCH + INSET, cols)] = above[source]
            padded[tile, pl.ds((MARGIN + rows + row) * PITCH + INSET, cols)] = below[source]
        for row in range(rows):
            padded[tile, pl.ds((MARGIN + row) * PITCH + INSET, cols)] = field_ref[
                row * cols : (row + 1) * cols, lane_tile(tile)
            ].astype(F32)
        for row in range(rows + 2 * MARGIN):
            padded[tile, pl.ds(row * PITCH, INSET)] = jnp.zeros((INSET, LANES), F32)
            padded[tile, pl.ds(row * PITCH + INSET + cols, INSET)] = jnp.zeros((INSET, LANES), F32)


def left_right(edge, side_refs, lanes):
    _, col = grid_place()
    even = col % 2 == 0
    inner = (col > 0) & (col < GX - 1)
    first = side_refs[0][:, lanes].astype(F32)
    second = jnp.where(inner, side_refs[1][:, lanes].astype(F32), 0.0)
    edge[0] = jnp.where(even, second, first)
    edge[1] = jnp.where(even, first, second)


def side_sums(left, right, edge, taps, near, far, rows, cols, flipped):
    for row in range(rows + 2 * MARGIN):
        left[pl.ds(row * cols, MARGIN)] = edge[0, pl.ds(row * MARGIN, MARGIN)]
        start = row * cols + cols + MARGIN - 8
        right[pl.ds(start, MARGIN)] = edge[1, pl.ds(row * MARGIN, MARGIN)]
    for side, sums, shifts in ((left, near, range(MARGIN)), (right, far, range(KS - MARGIN, KS))):
        for b in shifts:
            for r in range(rows + 2 * MARGIN):
                pixels = side[pl.ds(r * cols + b, 8)]
                for a in range(KS):
                    if 0 <= r - a < rows:
                        index = (KS - 1 - a) * KS + KS - 1 - b if flipped else a * KS + b
                        sums[r - a] = sums[r - a] + taps[index] * pixels
    return near, far


def side_scratch(sides, rows, cols):
    tall = rows + 2 * MARGIN
    return [pltpu.VMEM((tall * cols + 8, LANES), F32)] * 2 + [pltpu.VMEM((2, sides[0].shape[0], LANES), F32)]


def window(padded, tile, row, shift, cols):
    return padded[tile, pl.ds(row * PITCH + INSET - MARGIN + shift, cols), :]


def tap_sums(padded, tile, taps, sums, rows, cols, flipped):
    for b in range(KS):
        for r in range(rows + 2 * MARGIN):
            pixels = window(padded, tile, r, b, cols)
            for a in range(KS):
                if 0 <= r - a < rows:
                    index = (KS - 1 - a) * KS + KS - 1 - b if flipped else a * KS + b
                    sums[r - a] = sums[r - a] + taps[index] * pixels
    return sums


def forward_middle(field, bands, params, rows, cols):
    pixels, width = field.shape
    tiles = width // LANES
    span = (rows + 2 * MARGIN) * PITCH

    def body(*refs):
        field_ref, band_refs, (params_ref, padded, out) = refs[0], refs[1:-3], refs[-3:]
        fill_middle(padded, field_ref, band_refs, rows, cols)

        @pl.loop(0, tiles)
        def _(tile):
            taps = [params_ref[tile, pl.ds(t, 1), :] for t in range(KS * KS)]
            start = jnp.broadcast_to(params_ref[tile, pl.ds(KS * KS, 1), :], (cols, LANES))
            sums = tap_sums(padded, tile, taps, [start] * rows, rows, cols, False)
            for row in range(rows):
                out[tile, pl.ds(row * cols, cols), :] = sums[row]

    return call(
        body,
        [shape((tiles, span, LANES), F32), shape((tiles, pixels, LANES), F32)],
        [],
        [field, *bands, params],
        size=8000000,
        limit=16,
    )


def forward_end(partial, sides, params, rows, cols):
    tiles, pixels, _ = partial.shape
    width = tiles * LANES

    def body(partial_ref, first_ref, second_ref, params_ref, acts, standard, inverse, left, right, edge):
        left[...] = jnp.zeros_like(left)
        right[...] = jnp.zeros_like(right)

        @pl.loop(0, tiles)
        def _(tile):
            left_right(edge, (first_ref, second_ref), pl.ds(pl.multiple_of(tile * LANES, LANES), LANES))
            taps = [params_ref[tile, pl.ds(t, 1), :] for t in range(KS * KS)]
            near = [partial_ref[tile, pl.ds(row * cols, 8), :] for row in range(rows)]
            far = [partial_ref[tile, pl.ds((row + 1) * cols - 8, 8), :] for row in range(rows)]
            if cols > 16:
                standard[tile] = partial_ref[tile]
            near, far = side_sums(left, right, edge, taps, near, far, rows, cols, False)
            for row in range(rows):
                standard[tile, pl.ds(row * cols, 8), :] = near[row]
                standard[tile, pl.ds((row + 1) * cols - 8, 8), :] = far[row]

        total = standard[0]
        for tile in range(1, tiles):
            total = total + standard[tile]
        average = jnp.sum(total, axis=1, keepdims=True) * (1.0 / width)
        total = jnp.zeros((pixels, LANES), F32)
        for tile in range(tiles):
            centered = standard[tile] - average
            total = total + centered * centered
        scale = lax.rsqrt(jnp.sum(total, axis=1, keepdims=True) * (1.0 / width) + 1e-06)
        inverse[...] = jnp.broadcast_to(scale, (pixels, LANES))
        for tile in range(tiles):
            value = (standard[tile] - average) * scale
            standard[tile] = value
            gain = params_ref[tile, KS * KS + 1 : KS * KS + 2, :]
            shift = params_ref[tile, KS * KS + 2 : KS * KS + 3, :]
            acts[:, lane_tile(tile)] = (value * gain + shift).astype(BF16)

    return call(
        body,
        [
            shape((pixels, width), BF16),
            shape((tiles, pixels, LANES), F32),
            shape((pixels, LANES), F32),
        ],
        side_scratch(sides, rows, cols),
        [partial, *sides, params],
        size=6000000,
        limit=8,
    )


def with_sides(padded, sides, rows, cols):
    tiles = padded.shape[0]

    def body(padded_ref, first_ref, second_ref, out, edge):
        for tile in range(tiles):
            out[tile] = padded_ref[tile]
            left_right(edge, (first_ref, second_ref), lane_tile(tile))
            for row in range(rows + 2 * MARGIN):
                here = pl.ds(row * MARGIN, MARGIN)
                out[tile, pl.ds(row * PITCH + INSET - MARGIN, MARGIN)] = edge[0, here]
                out[tile, pl.ds(row * PITCH + INSET + cols, MARGIN)] = edge[1, here]

    return call(
        body,
        [shape(padded.shape, F32)],
        [pltpu.VMEM((2, sides[0].shape[0], LANES), F32)],
        [padded, *sides],
        size=2000000,
        limit=8,
    )[0]


def arrays_of(shards):
    arrays, slots = [], []
    for shard in shards:
        places = []
        for array, start, _ in shard:
            known = [index for index, other in enumerate(arrays) if other is array]
            if not known:
                arrays.append(array)
            places.append((known[0] if known else len(arrays) - 1, start))
        slots.append(places)
    return arrays, slots


def hidden_scratch(rows, units, width):
    return [
        pltpu.VMEM((rows, width), BF16),
        pltpu.VMEM((rows, width), BF16),
        pltpu.VMEM((rows, units), F32),
        pltpu.VMEM((rows, units), F32),
        pltpu.VMEM((rows, units), BF16),
    ]


def weight_scratch(units, width):
    return [pltpu.VMEM((units, width), BF16), pltpu.VMEM((units, width), BF16)]


def place_rows(norm, back, normed_refs, up_refs, starts, params_ref):
    pixels = normed_refs[0].shape[0]
    for index, start in enumerate(starts):
        here = slice(index * pixels, (index + 1) * pixels)
        norm[here] = normed_refs[index][...]
        for tile in range(norm.shape[1] // LANES):
            lanes = lane_tile(tile)
            layer = params_ref[tile, KS * KS + 3 : KS * KS + 4, :]
            rows = up_refs[index][start : start + pixels, lanes]
            back[here, lanes] = (rows.astype(F32) * layer).astype(BF16)


def place_weights(win, wout, shard_refs, slots, units):
    for index, (rows_in, rows_out, _) in enumerate(slots):
        here = slice(index * units, (index + 1) * units)
        win[here] = shard_refs[rows_in[0]][rows_in[1] : rows_in[1] + units]
        wout[here] = shard_refs[rows_out[0]][rows_out[1] : rows_out[1] + units]
    lines = [shard_refs[bias[0]][bias[1] : bias[1] + 1, :units].astype(F32) for *_, bias in slots]
    return lines[0] if len(lines) == 1 else jnp.concatenate(lines, axis=1)


def hidden_block(norm, back, win, wout, line, hid, pre, slope, bpre):
    step = 32
    across = (((1,), (1,)), ((), ()))
    pre[...] = lax.dot_general(norm[...], win[...], across, preferred_element_type=F32) + line
    slope[...] = lax.dot_general(back[...], wout[...], across, preferred_element_type=F32)

    @pl.loop(0, norm.shape[0] // step)
    def _(part):
        here = pl.ds(pl.multiple_of(part * step, step), step)
        value = pre[here, :]
        half = 0.5 * (1.0 + lax.erf(value * 0.7071067811865476))
        hid[here, :] = (value * half).astype(BF16)
        bell = jnp.exp(-0.5 * value * value) * 0.3989422804014327
        bpre[here, :] = (slope[here, :] * (half + value * bell)).astype(BF16)

    return jnp.dot(bpre[...], win[...], preferred_element_type=F32)


def hidden_near(normed, upstream, params, shards, units):
    pixels, width = normed[0].shape
    arrays, slots = arrays_of(shards)
    members, count, every = len(normed), len(arrays), len(shards) * units
    rows = members * pixels

    def body(*refs):
        normed_refs, up_refs, params_ref = refs[:members], refs[members : 2 * members], refs[2 * members]
        shard_refs, rest = refs[2 * members + 1 : 2 * members + 1 + count], refs[2 * members + 1 + count :]
        hid, total, win, wout, norm, back, pre, slope, bpre = rest
        place_rows(norm, back, normed_refs, up_refs, [start for _, start in upstream], params_ref)
        line = place_weights(win, wout, shard_refs, slots, units)
        total[...] = hidden_block(norm, back, win, wout, line, hid, pre, slope, bpre)

    return call(
        body,
        [shape((rows, every), BF16), shape((rows, width), F32)],
        weight_scratch(every, width) + hidden_scratch(rows, every, width),
        [*normed, *[array for array, _ in upstream], params, *arrays],
        size=7000000,
        limit=20,
    )


def hidden_far(normed, upstream, params, shards, early, near_sum, units):
    pixels, width = normed[0].shape
    arrays, slots = arrays_of(shards)
    members, count = len(normed), len(arrays)
    half = members // 2
    rows, every, late = half * pixels, len(shards) * units, (len(shards) - early) * units

    def body(*refs):
        normed_refs, up_refs, params_ref = refs[:members], refs[members : 2 * members], refs[2 * members]
        shard_refs, rest = refs[2 * members + 1 : 2 * members + 1 + count], refs[2 * members + 1 + count :]
        sum_ref, near_hid, far_hid, stay, send = rest[:5]
        win, wout, late_in, late_out = rest[5:9]
        near_norm, near_back, near_pre, near_slope, near_bpre = rest[9:14]
        norm, back, pre, slope, bpre = rest[14:]
        starts = [start for _, start in upstream]
        place_rows(near_norm, near_back, normed_refs[:half], up_refs[:half], starts[:half], params_ref)
        place_rows(norm, back, normed_refs[half:], up_refs[half:], starts[half:], params_ref)
        line = place_weights(win, wout, shard_refs, slots, units)
        late_line = place_weights(late_in, late_out, shard_refs, slots[early:], units)
        far = hidden_block(norm, back, win, wout, line, far_hid, pre, slope, bpre)
        near = sum_ref[...] + hidden_block(
            near_norm, near_back, late_in, late_out, late_line, near_hid, near_pre, near_slope, near_bpre
        )
        stay[:pixels] = near[:pixels]
        stay[pixels:] = far[:pixels]
        send[:pixels] = near[pixels:].astype(BF16)
        send[pixels:] = far[pixels:].astype(BF16)

    return call(
        body,
        [
            shape((rows, late), BF16),
            shape((rows, every), BF16),
            shape((rows, width), F32),
            shape((rows, width), BF16),
        ],
        weight_scratch(every, width)
        + weight_scratch(late, width)
        + hidden_scratch(rows, late, width)
        + hidden_scratch(rows, every, width),
        [*normed, *[array for array, _ in upstream], params, *arrays, near_sum],
        size=9000000,
        limit=28,
    )


def project(hiddens, upstream, shards, units):
    pixels, width = upstream[0][0].shape[0], upstream[0][0].shape[1]
    arrays, slots = arrays_of([[rows_out] for _, rows_out, _ in shards])
    members, count, every = len(upstream), len(arrays), len(shards) * units
    half = members // 2 * pixels
    early, late, _ = hiddens

    def body(early_ref, late_ref, far_ref, *refs):
        up_refs, shard_refs = refs[:members], refs[members : members + count]
        stay, send, scale, wout, hid = refs[members + count :]
        for index, ((slot, start),) in enumerate(slots):
            wout[index * units : (index + 1) * units] = shard_refs[slot][start : start + units]
        hid[:half, : early.shape[1]] = early_ref[...]
        hid[:half, early.shape[1] :] = late_ref[...]
        hid[half:] = far_ref[...]
        projected = jnp.dot(hid[...], wout[...], preferred_element_type=F32)
        stay[:pixels] = projected[:pixels]
        stay[pixels:] = projected[half : half + pixels]
        send[:pixels] = projected[pixels:half].astype(BF16)
        send[pixels:] = projected[half + pixels :].astype(BF16)
        for tile in range(width // LANES):
            lanes = lane_tile(tile)
            sums = jnp.zeros((pixels, LANES), F32)
            for index in range(members):
                rows = projected[index * pixels : (index + 1) * pixels, lanes]
                start = upstream[index][1]
                sums = sums + up_refs[index][start : start + pixels, lanes].astype(F32) * rows
            scale[tile] = jnp.broadcast_to(jnp.sum(sums, axis=0, keepdims=True), (8, LANES))

    return call(
        body,
        [shape((half, width), F32), shape((half, width), BF16), shape((width // LANES, 8, LANES), F32)],
        [pltpu.VMEM((every, width), BF16), pltpu.VMEM((2 * half, every), BF16)],
        [*hiddens, *[array for array, _ in upstream], *arrays],
        size=3911400,
        limit=20,
    )


def pair_sum(mine, peer):
    rows, width = mine.shape
    half = rows // 2

    def body(mine_ref, peer_ref, out):
        out[...] = (mine_ref[half:, :] + peer_ref[half:, :].astype(F32)).astype(BF16)

    return call(body, [shape((half, width), BF16)], [], [mine, peer], size=738000, limit=4)[0]


def norm_backward(own, peer, far, standard, inverse, params, upstream, rows, cols):
    pixels, width = upstream.shape
    tiles = width // LANES
    strip = MARGIN * cols

    def body(own_ref, peer_ref, far_ref, std, inv, params_ref, up_ref, conv, wire, vectors, *sends):
        zero = jnp.zeros((pixels, LANES), F32)
        plain, mixed = zero, zero
        for tile in range(tiles):
            lanes = lane_tile(tile)
            normed = own_ref[:pixels, lanes] + peer_ref[:pixels, lanes].astype(F32) + far_ref[:, lanes].astype(F32)
            gain = params_ref[tile, KS * KS + 1 : KS * KS + 2, :]
            scaled = normed * gain
            product = normed * std[tile]
            conv[tile] = scaled
            plain = plain + scaled
            mixed = mixed + product * gain
            vectors[tile] = jnp.zeros((8, LANES), F32)
            vectors[tile, 1:2, :] = jnp.sum(product, axis=0, keepdims=True)
            vectors[tile, 2:3, :] = jnp.sum(normed, axis=0, keepdims=True)
            out_bias = params_ref[tile, KS * KS + 4 : KS * KS + 5, :]
            vectors[tile, 3:4, :] = jnp.sum(up_ref[:, lanes].astype(F32), axis=0, keepdims=True) * out_bias
        plain = jnp.sum(plain, axis=1, keepdims=True) * (1.0 / width)
        mixed = jnp.sum(mixed, axis=1, keepdims=True) * (1.0 / width)
        for tile in range(tiles):
            value = inv[...] * (conv[tile] - plain - std[tile] * mixed)
            conv[tile] = value
            wire[:, lane_tile(tile)] = value.astype(BF16)
            vectors[tile, 0:1, :] = jnp.sum(value, axis=0, keepdims=True)
        row, _ = grid_place()
        even = row % 2 == 0
        top, bottom = wire[:strip, :], wire[pixels - strip :, :]
        sends[0][...] = jnp.where(even, bottom, top)
        if len(sends) > 1:
            sends[1][...] = jnp.where(even, top, bottom)

    return call(
        body,
        [
            shape((tiles, pixels, LANES), F32),
            shape((pixels, width), BF16),
            shape((tiles, 8, LANES), F32),
        ]
        + [shape((strip, width), BF16)] * row_pairings(),
        [],
        [own, peer, far, standard, inverse, params, upstream],
        size=1845000,
        limit=16,
    )


def block_output(own, peer, far, params, field):
    pixels, width = field.shape

    def body(own_ref, peer_ref, far_ref, params_ref, field_ref, block):
        for tile in range(width // LANES):
            lanes = lane_tile(tile)
            out_bias = params_ref[tile, KS * KS + 4 : KS * KS + 5, :]
            layer = params_ref[tile, KS * KS + 3 : KS * KS + 4, :]
            projected = own_ref[:pixels, lanes] + peer_ref[:pixels, lanes].astype(F32) + far_ref[:, lanes].astype(F32)
            block[:, lanes] = (field_ref[:, lanes].astype(F32) + layer * (projected + out_bias)).astype(BF16)

    return call(
        body,
        [shape((pixels, width), BF16)],
        [],
        [own, peer, far, params, field],
        size=3210300,
        limit=8,
    )[0]


def kernel_gradient(padded, back_conv, vectors, scale_part, rows, cols, groups):
    tiles = back_conv.shape[0]
    share = tiles // groups

    def body(padded_ref, conv, vectors_ref, scale_ref, *refs):
        outs, out = refs[:-1], refs[-1]

        @pl.loop(0, tiles)
        def _(tile):
            grads = [conv[tile, pl.ds(row * cols, cols), :] for row in range(rows)]
            for b in range(KS):
                sums = [None] * KS
                for r in range(rows + 2 * MARGIN):
                    pixels = window(padded_ref, tile, r, b, cols)
                    for a in range(KS):
                        if 0 <= r - a < rows:
                            term = pixels * grads[r - a]
                            sums[a] = term if sums[a] is None else sums[a] + term
                for a in range(KS):
                    out[tile, pl.ds(a * KS + b, 1), :] = jnp.sum(sums[a], axis=0, keepdims=True)
            out[tile, pl.ds(KS * KS, TAP_ROWS - KS * KS), :] = vectors_ref[tile, : TAP_ROWS - KS * KS, :]
            out[tile, pl.ds(KS * KS + 3, 1), :] += scale_ref[tile, :1, :]

        if groups == 1:
            outs[0][...] = out[...]
        else:
            me = lax.axis_index("dp")
            for bits in range(groups):
                for part in range(share):
                    outs[bits][part] = out[(me ^ bits) * share + part]

    return call(
        body,
        [shape((share, TAP_ROWS, LANES), F32)] * groups,
        [pltpu.VMEM((tiles, TAP_ROWS, LANES), F32)],
        [padded, back_conv, vectors, scale_part],
        size=7380000,
        limit=8,
    )


def gradient_middle(wire, bands, params, upstream, rows, cols):
    pixels, width = wire.shape
    tiles = width // LANES
    span = (rows + 2 * MARGIN) * PITCH

    def body(*refs):
        wire_ref, band_refs, (params_ref, up_ref, out, padded) = refs[0], refs[1:-4], refs[-4:]
        fill_middle(padded, wire_ref, band_refs, rows, cols)

        @pl.loop(0, tiles)
        def _(tile):
            lanes = pl.ds(pl.multiple_of(tile * LANES, LANES), LANES)
            taps = [params_ref[tile, pl.ds(t, 1), :] for t in range(KS * KS)]
            start = [up_ref[pl.ds(row * cols, cols), lanes].astype(F32) for row in range(rows)]
            sums = tap_sums(padded, tile, taps, start, rows, cols, True)
            for row in range(rows):
                out[tile, pl.ds(row * cols, cols), :] = sums[row]

    return call(
        body,
        [shape((tiles, pixels, LANES), F32)],
        [pltpu.VMEM((tiles, span, LANES), F32)],
        [wire, *bands, params, upstream],
        size=8000000,
        limit=16,
    )[0]


def gradient_end(partial, sides, params, rows, cols):
    tiles, pixels, _ = partial.shape

    def body(partial_ref, first_ref, second_ref, params_ref, out, left, right, edge):
        left[...] = jnp.zeros_like(left)
        right[...] = jnp.zeros_like(right)

        @pl.loop(0, tiles)
        def _(tile):
            lanes = pl.ds(pl.multiple_of(tile * LANES, LANES), LANES)
            left_right(edge, (first_ref, second_ref), lanes)
            taps = [params_ref[tile, pl.ds(t, 1), :] for t in range(KS * KS)]
            near = [partial_ref[tile, pl.ds(row * cols, 8), :] for row in range(rows)]
            far = [partial_ref[tile, pl.ds((row + 1) * cols - 8, 8), :] for row in range(rows)]
            near, far = side_sums(left, right, edge, taps, near, far, rows, cols, True)
            for row in range(rows):
                middle = partial_ref[tile, pl.ds(row * cols + 8, cols - 16), :] if cols > 16 else None
                whole = [near[row]] + ([middle] if cols > 16 else []) + [far[row]]
                out[pl.ds(row * cols, cols), lanes] = jnp.concatenate(whole).astype(BF16)

    return call(
        body,
        [shape((pixels, tiles * LANES), BF16)],
        side_scratch(sides, rows, cols),
        [partial, *sides, params],
        size=5000000,
        limit=8,
    )[0]


def across(block, bits):
    groups = lax.axis_size("dp")
    return lax.ppermute(block, "dp", [(i, i ^ bits) for i in range(groups)])


def tile_swap(block, bits):
    return lax.ppermute(block, "tile", [(i, i ^ bits) for i in range(lax.axis_size("tile"))])


def place_params(own, joints):
    share, rows, _ = own.shape
    half = rows // 2

    def body(own_ref, *refs):
        joint_refs, out = refs[:-1], refs[-1]
        me = lax.axis_index("dp")
        for part in range(share):
            out[me * share + part] = own_ref[part]
        for bits, ref in enumerate(joint_refs, 1):
            start = ref.shape[0] - PARAM_ROWS
            for part in range(2 * share):
                high = ref[start:, lane_tile(2 * part)].astype(F32)
                value = high + ref[start:, lane_tile(2 * part + 1)].astype(F32)
                out[(me ^ bits) * share + part // 2, pl.ds(part % 2 * half, half), :] = value[:half]

    return call(
        body,
        [shape((4 * share, rows, LANES), F32)],
        [],
        [own, *joints],
        size=738000,
        limit=4,
    )[0]


def gather_params(kernel, vectors):
    own = kernel.shape[1]
    pack = jnp.concatenate([kernel, *vectors, jnp.zeros((TAP_ROWS - KS * KS - len(vectors), own), F32)])
    whole = lax.all_gather(pack, "dp", axis=1, tiled=True)
    return whole.reshape(TAP_ROWS, -1, LANES).transpose(1, 0, 2)


def sum_params(parts, factor):
    flat = parts.transpose(1, 0, 2).reshape(TAP_ROWS, -1)
    sums = lax.psum(lax.psum_scatter(flat, "dp", scatter_dimension=1, tiled=True), "tile") * factor
    taps = KS * KS
    return [sums[:taps]] + [sums[taps + index] for index in range(4)]


def add_blocks(blocks):
    def body(*refs):
        value = refs[0][...]
        for ref in refs[1:-1]:
            value = value + ref[...]
        refs[-1][...] = value

    return call(body, [shape(blocks[0].shape, F32)], [], blocks, size=738000, limit=4)[0]


def finish(total, moved, factor):
    tiles, rows, _ = total.shape
    taps = KS * KS

    def body(*refs):
        outs = refs[1 + len(moved) :]
        for tile in range(tiles):
            value = refs[0][tile]
            for other in refs[1 : 1 + len(moved)]:
                value = value + other[tile]
            value = value * factor
            outs[0][:, lane_tile(tile)] = value[:taps]
            for index in range(4):
                outs[1 + index][:, lane_tile(tile)] = value[taps + index : taps + index + 1]

    taps_sum, *vectors = call(
        body,
        [shape((taps, tiles * LANES), F32)] + [shape((1, tiles * LANES), F32)] * 4,
        [],
        [total, *moved],
        size=2214000,
        limit=4,
    )
    return [taps_sum] + [v.reshape(-1) for v in vectors]


def after(block, *others):
    return lax.optimization_barrier((block, *others))[0]


def pack_shard(rows_in, rows_out, bias):
    units, width = rows_in.shape
    row = jnp.pad(bias.reshape(1, units), ((0, BIAS_ROWS - 1), (0, width - units)))
    return jnp.concatenate([rows_in, rows_out, row])


def first_sends(field, rows_in, rows_out, bias, kernel, vectors, strip):
    pixels, width = field.shape
    units = rows_in.shape[0]
    taps, own = kernel.shape
    half = TAP_ROWS // 2

    def body(bias_ref, field_ref, in_ref, out_ref, kernel_ref, *refs):
        vector_refs, refs = refs[: len(vectors)], refs[len(vectors) :]
        joint, cross, pack, tap_stage, vector_stage, sems = refs
        row, _ = grid_place()
        start = pl.multiple_of((1 - row % 2) * (pixels - strip), 16)
        small = [pltpu.make_async_copy(kernel_ref, tap_stage, sems.at[0])]
        for index, ref in enumerate(vector_refs):
            small.append(pltpu.make_async_copy(ref, vector_stage.at[index], sems.at[1 + index]))
        at = 1 + len(vectors)
        large = [
            pltpu.make_async_copy(field_ref.at[pl.ds(start, strip)], cross.at[pl.ds(0, strip)], sems.at[at]),
            pltpu.make_async_copy(in_ref, joint.at[pl.ds(0, units)], sems.at[at + 1]),
            pltpu.make_async_copy(out_ref, joint.at[pl.ds(units, units)], sems.at[at + 2]),
        ]
        for copy in small + large:
            copy.start()
        line = jnp.concatenate([bias_ref[...].astype(F32), jnp.zeros((1, width - units), F32)], axis=1)
        line = jnp.broadcast_to(line, (BIAS_ROWS, width))
        places = lax.broadcasted_iota(jnp.int32, (BIAS_ROWS, width), 0)
        cross[strip + 2 * units :] = jnp.where(places == 0, line, 0.0).astype(BF16)
        for copy in small:
            copy.wait()
        for tile in range(own // LANES):
            pack[tile, TAP_ROWS - 8 :, :] = jnp.zeros((8, LANES), F32)
            pack[tile, :taps, :] = tap_stage[:, lane_tile(tile)]
            for index in range(len(vectors)):
                pack[tile, taps + index : taps + index + 1, :] = vector_stage[index, :, lane_tile(tile)]
        for part in range(2 * own // LANES):
            value = pack[part // 2, part % 2 * half : (part % 2 + 1) * half, :]
            value = jnp.concatenate([value, jnp.zeros((PARAM_ROWS - half, LANES), F32)])
            high = value.astype(BF16).astype(F32)
            for side, rest in enumerate((high, value - high)):
                lanes = lane_tile(2 * part + side)
                spread = jnp.broadcast_to(line[:1, lanes], (PARAM_ROWS, LANES))
                places = lax.broadcasted_iota(jnp.int32, (PARAM_ROWS, LANES), 0)
                joint[2 * units :, lanes] = jnp.where(places == half, spread, rest).astype(BF16)
        for copy in large:
            copy.wait()
        cross[strip : strip + 2 * units] = joint[: 2 * units]

    outs = [
        shape((2 * units + PARAM_ROWS, width), BF16),
        shape((strip + 2 * units + BIAS_ROWS, width), BF16),
        shape((own // LANES, TAP_ROWS, LANES), F32),
    ]
    args = [bias.reshape(1, units), field, rows_in, rows_out, kernel, *vectors]
    far = pl.BlockSpec(memory_space=pltpu.HBM)
    return pl.pallas_call(
        body,
        out_shape=outs,
        in_specs=[VMEM] + [far] * (len(args) - 1),
        out_specs=[VMEM] * len(outs),
        scratch_shapes=[
            pltpu.VMEM((taps, own), F32),
            pltpu.VMEM((len(vectors), 1, own), F32),
            pltpu.SemaphoreType.DMA((4 + len(vectors),)),
        ],
        compiler_params=pltpu.CompilerParams(vmem_limit_bytes=62 * 1024 * 1024),
        cost_estimate=pl.CostEstimate(flops=10000, bytes_accessed=1000000, transcendentals=0),
    )(*args)


def cut_rows(block, cuts):
    def body(ref, *outs):
        for (start, count), out in zip(cuts, outs):
            out[...] = ref[start : start + count]

    outs = [shape((count, block.shape[1]), block.dtype) for _, count in cuts]
    return call(body, outs, [], [block], size=738000, limit=4)


def row_sends(field, strip):
    row, _ = grid_place()
    starts = [(1 - (row + first) % 2) * (field.shape[0] - strip) for first in range(row_pairings())]
    return [lax.dynamic_slice_in_dim(field, start, strip, 0) for start in starts]


def gathered_shard(in_weight, out_weight, hidden_bias):
    units = in_weight.shape[0]
    groups, count = lax.axis_size("dp"), lax.axis_size("tile")
    place = lax.axis_index("tile")
    member = place % 4

    def mine(array):
        whole = lax.all_gather(array, ("dp", "tile"), axis=0, tiled=True)
        whole = whole.reshape((4, groups * count // 4 * units) + array.shape[1:])
        return lax.dynamic_index_in_dim(whole, member, 0, keepdims=False)

    rows_in, rows_out, bias = mine(in_weight), mine(out_weight), mine(hidden_bias)
    return pack_shard(rows_in, rows_out, bias)


def per_device(
    features,
    cotangent,
    in_weight,
    out_weight,
    hidden_bias,
    kernel,
    conv_bias,
    norm_gain,
    norm_bias,
    layer_scale,
    out_bias,
):
    image_count, _, rows, cols, width = features.shape
    groups, count = lax.axis_size("dp"), lax.axis_size("tile")
    units = in_weight.shape[0]
    pixels = rows * cols
    own = kernel.shape[1]
    strip = MARGIN * cols
    field = features.reshape(pixels, width)
    upstream = cotangent.reshape(pixels, width)

    by_permutes = units % 16 == 0 and groups == 4 and count == 8 and units < width and 4 * own == width
    vectors = [v.reshape(1, own) for v in (conv_bias, norm_gain, norm_bias, layer_scale, out_bias)]
    if by_permutes:
        held, cross, piece = first_sends(field, in_weight, out_weight, hidden_bias, kernel, vectors, strip)
        cross, far_upstream = tile_swap(cross, 4), tile_swap(upstream, 2)
        first, second, far = [across(held, bits) for bits in (1, 2, 3)]
        cross, far_upstream, first, second, far = lax.optimization_barrier(
            (cross, far_upstream, first, second, far)
        )
        params = place_params(piece, [first, second, far])
        bands = cut_rows(cross, [(0, strip)])
        (other,) = cut_rows(cross, [(strip, 2 * units + BIAS_ROWS)])
        other_first, other_second = across(other, 1), across(other, 2)
        (part_in,) = cut_rows(other_first, [(0, units)])
        (part_out,) = cut_rows(other_second, [(units, units + BIAS_ROWS)])
        far_in, far_out = across(part_in, 2), across(part_out, 1)
        after_params = 2 * units + TAP_ROWS // 2
        shards = [
            [(shard, 0, units), (shard, units, units), (shard, after_params, 1)]
            for shard in (held, first, second, far)
        ]
        whole = [(0, units), (units, units), (2 * units, BIAS_ROWS)]
        shards += [[(shard, *rows) for rows in whole] for shard in (other, other_first, other_second)]
        shards.append([(far_in, 0, units), (far_out, 0, units), (far_out, units, BIAS_ROWS)])
    else:
        bands = swap_rows(row_sends(field, strip))
        params = gather_params(kernel, vectors)
        far_upstream = tile_swap(upstream, 2)
        shards = [gathered_shard(in_weight, out_weight, hidden_bias)]
        units = shards[0].shape[0] // 2 - BIAS_ROWS // 2
        shards = [[(shards[0], 0, units), (shards[0], units, units), (shards[0], 2 * units, BIAS_ROWS)]]
    sides = swap_cols(border_columns(field, bands, rows, cols))
    padded, partial = forward_middle(field, bands, params, rows, cols)
    acts, standard, inverse = forward_end(partial, sides, params, rows, cols)
    padded = with_sides(padded, sides, rows, cols)
    near_acts, far_acts = tile_swap(acts, 1), tile_swap(acts, 2)
    near_upstream = tile_swap(upstream, 1)
    early = max(1, len(shards) - 1)
    if by_permutes:
        chip = [(upstream, 0), (near_upstream, 0)]
        near_hidden, near_sum = hidden_near([acts, near_acts], chip, params, shards[:early], units)
        far_acts = after(far_acts, far_in, far_out, padded, near_sum)
    else:
        half = units // 2
        cuts = [[(array, first + at, half) for array, first, _ in shards[0][:2]] for at in (0, half)]
        bias, row, _ = shards[0][2]
        lines = [jnp.pad(bias[row : row + 1, at : at + half], ((0, 0), (0, 0))) for at in (0, half)]
        shards = [[*cut, (line, 0, 1)] for cut, line in zip(cuts, lines)]
        units = half
        chip = [(upstream, 0), (near_upstream, 0)]
        near_hidden, near_sum = hidden_near([acts, near_acts], chip, params, shards[:early], units)
    normed = [acts, near_acts, far_acts, tile_swap(far_acts, 1)]
    upstreams = [*chip, (far_upstream, 0), (tile_swap(far_upstream, 1), 0)]
    late_hidden, far_hidden, back_own, back_send = hidden_far(
        normed, upstreams, params, shards, early, near_sum, units
    )
    hiddens = [near_hidden, late_hidden, far_hidden]

    def group_sum(mine, theirs, *others):
        peer = tile_swap(theirs, 1)
        return mine, peer, tile_swap(after(pair_sum(mine, peer), *others), 2)

    back_sums = group_sum(back_own, back_send)
    out_own, out_send, scale_part = project(hiddens, upstreams, shards, units)
    back_conv, wire, vector_parts, *back_sends = norm_backward(
        *back_sums, standard, inverse, params, upstream, rows, cols
    )
    parts = kernel_gradient(
        padded, back_conv, vector_parts, scale_part, rows, cols, groups if by_permutes else 1
    )
    back_bands = swap_rows([after(send, parts[0]) for send in back_sends])
    back_sides = swap_cols(border_columns(wire, back_bands, rows, cols))
    middle = gradient_middle(wire, back_bands, params, upstream, rows, cols)
    grad = gradient_end(middle, back_sides, params, rows, cols)
    factor = 1.0 / math.sqrt(image_count * groups * count * pixels)
    if by_permutes:
        total = add_blocks([parts[0]] + [across(parts[bits], bits) for bits in range(1, groups)])
        block = block_output(*group_sum(out_own, out_send, total), params, field)
        total = after(total, *back_bands)
        total = add_blocks([total, tile_swap(total, 1)])
        total = after(add_blocks([total, tile_swap(total, 4)]), middle, *back_sides)
        sums = finish(after(total, block, grad), [tile_swap(total, 2)], factor)
    else:
        block = block_output(*group_sum(out_own, out_send), params, field)
        sums = sum_params(parts[0], factor)
    return (block.reshape(features.shape), grad.reshape(features.shape), *sums)


def solution(mesh):
    placed = (
        P("dp", "tile", None, None, None),
        P("dp", "tile", None, None, None),
        P(("dp", "tile"), None),
        P(("dp", "tile"), None),
        P(("dp", "tile")),
        P(None, "dp"),
        P("dp"),
        P("dp"),
        P("dp"),
        P("dp"),
        P("dp"),
    )
    return jax.shard_map(
        per_device,
        mesh=mesh,
        in_specs=placed,
        out_specs=(
            P("dp", "tile", None, None, None),
            P("dp", "tile", None, None, None),
            P(None, "dp"),
            P("dp"),
            P("dp"),
            P("dp"),
            P("dp"),
        ),
        check_vma=False,
    )
```

```python
import math

import jax
import jax.numpy as jnp
from jax import lax
from jax.experimental import pallas as pl
from jax.experimental.pallas import tpu as pltpu
from jax.sharding import PartitionSpec as P

KS = 7
GX = 4
MARGIN = KS // 2
LANES = 128
PITCH = 32
INSET = 8
TAP_ROWS = 56
BIAS_ROWS = 8
PARAM_ROWS = 32
F32 = jnp.float32
BF16 = jnp.bfloat16

VMEM = pl.BlockSpec(memory_space=pltpu.VMEM)


def call(body, outs, scratch, args, flops=0, size=0, aliases=None, limit=32):
    return pl.pallas_call(
        body,
        out_shape=outs,
        in_specs=[VMEM] * len(args),
        out_specs=[VMEM] * len(outs),
        scratch_shapes=scratch,
        input_output_aliases=aliases or {},
        compiler_params=pltpu.CompilerParams(vmem_limit_bytes=limit * 1024 * 1024),
        cost_estimate=pl.CostEstimate(flops=flops, bytes_accessed=size, transcendentals=0),
    )(*args)


def shape(dims, kind):
    return jax.ShapeDtypeStruct(dims, kind)


def lane_tile(tile):
    return slice(tile * LANES, (tile + 1) * LANES)


def grid_place():
    place = lax.axis_index("tile")
    return place // GX, place % GX


def swap_rows(sends):
    count = lax.axis_size("tile")
    grid_rows = count // GX
    moved = []
    for first, block in enumerate(sends):
        route = []
        for place in range(count):
            row = place // GX
            if row % 2 == first and row + 1 < grid_rows:
                route += [(place, place + GX), (place + GX, place)]
        moved.append(lax.ppermute(block, "tile", route))
    return moved


def swap_cols(sends):
    count = lax.axis_size("tile")
    moved = []
    for first, block in enumerate(sends):
        route = []
        for place in range(count):
            col = place % GX
            if col % 2 == first:
                other = place - col + (col + 1) % GX
                route += [(place, other), (other, place)]
        moved.append(lax.ppermute(block, "tile", route))
    return moved


def row_pairings():
    return 1 if lax.axis_size("tile") // GX == 2 else 2


def above_below(bands, tile):
    row, _ = grid_place()
    even = row % 2 == 0
    first = bands[0][:, lane_tile(tile)].astype(F32)
    second = bands[1][:, lane_tile(tile)].astype(F32) if len(bands) > 1 else jnp.zeros_like(first)
    return jnp.where(even, second, first), jnp.where(even, first, second)


def border_columns(field, bands, rows, cols):
    width = field.shape[1]
    tall = rows + 2 * MARGIN
    packed = -(-tall * MARGIN // 16) * 16

    def body(field_ref, *refs):
        band_refs = refs[: len(bands)]
        outs, full, left, right = refs[len(bands) : -3], refs[-3], refs[-2], refs[-1]
        _, col = grid_place()
        even = col % 2 == 0
        left[...] = jnp.zeros_like(left)
        right[...] = jnp.zeros_like(right)
        for tile in range(width // LANES):
            above, below = above_below(band_refs, tile)
            full[: MARGIN * cols] = above
            full[MARGIN * cols : (MARGIN + rows) * cols] = field_ref[:, lane_tile(tile)].astype(F32)
            full[(MARGIN + rows) * cols :] = below
            for row in range(tall):
                here = pl.ds(row * MARGIN, MARGIN)
                left[here] = full[pl.ds(row * cols, MARGIN)]
                right[here] = full[pl.ds(row * cols + cols - MARGIN, MARGIN)]
            toward_left, toward_right = left[...], right[...]
            outs[0][:, lane_tile(tile)] = jnp.where(even, toward_right, toward_left).astype(BF16)
            outs[1][:, lane_tile(tile)] = jnp.where(even, toward_left, toward_right).astype(BF16)

    return call(
        body,
        [shape((packed, width), BF16)] * 2,
        [pltpu.VMEM((tall * cols, LANES), F32)] + [pltpu.VMEM((packed, LANES), F32)] * 2,
        [field, *bands],
        size=1107000,
        limit=8,
    )


def fill_middle(padded, field_ref, band_refs, rows, cols):
    width = field_ref.shape[1]
    for tile in range(width // LANES):
        above, below = above_below(band_refs, tile)
        for row in range(MARGIN):
            source = slice(row * cols, (row + 1) * cols)
            padded[tile, pl.ds(row * PITCH + INSET, cols)] = above[source]
            padded[tile, pl.ds((MARGIN + rows + row) * PITCH + INSET, cols)] = below[source]
        for row in range(rows):
            padded[tile, pl.ds((MARGIN + row) * PITCH + INSET, cols)] = field_ref[
                row * cols : (row + 1) * cols, lane_tile(tile)
            ].astype(F32)
        for row in range(rows + 2 * MARGIN):
            padded[tile, pl.ds(row * PITCH, INSET)] = jnp.zeros((INSET, LANES), F32)
            padded[tile, pl.ds(row * PITCH + INSET + cols, INSET)] = jnp.zeros((INSET, LANES), F32)


def left_right(edge, side_refs, lanes):
    _, col = grid_place()
    even = col % 2 == 0
    inner = (col > 0) & (col < GX - 1)
    first = side_refs[0][:, lanes].astype(F32)
    second = jnp.where(inner, side_refs[1][:, lanes].astype(F32), 0.0)
    edge[0] = jnp.where(even, second, first)
    edge[1] = jnp.where(even, first, second)


def side_sums(left, right, edge, taps, near, far, rows, cols, flipped):
    for row in range(rows + 2 * MARGIN):
        left[pl.ds(row * cols, MARGIN)] = edge[0, pl.ds(row * MARGIN, MARGIN)]
        start = row * cols + cols + MARGIN - 8
        right[pl.ds(start, MARGIN)] = edge[1, pl.ds(row * MARGIN, MARGIN)]
    for side, sums, shifts in ((left, near, range(MARGIN)), (right, far, range(KS - MARGIN, KS))):
        for b in shifts:
            for r in range(rows + 2 * MARGIN):
                pixels = side[pl.ds(r * cols + b, 8)]
                for a in range(KS):
                    if 0 <= r - a < rows:
                        index = (KS - 1 - a) * KS + KS - 1 - b if flipped else a * KS + b
                        sums[r - a] = sums[r - a] + taps[index] * pixels
    return near, far


def side_scratch(sides, rows, cols):
    tall = rows + 2 * MARGIN
    return [pltpu.VMEM((tall * cols + 8, LANES), F32)] * 2 + [pltpu.VMEM((2, sides[0].shape[0], LANES), F32)]


def window(padded, tile, row, shift, cols):
    return padded[tile, pl.ds(row * PITCH + INSET - MARGIN + shift, cols), :]


def tap_sums(padded, tile, taps, sums, rows, cols, flipped):
    for b in range(KS):
        for r in range(rows + 2 * MARGIN):
            pixels = window(padded, tile, r, b, cols)
            for a in range(KS):
                if 0 <= r - a < rows:
                    index = (KS - 1 - a) * KS + KS - 1 - b if flipped else a * KS + b
                    sums[r - a] = sums[r - a] + taps[index] * pixels
    return sums


def forward_middle(field, bands, params, rows, cols):
    pixels, width = field.shape
    tiles = width // LANES
    span = (rows + 2 * MARGIN) * PITCH

    def body(*refs):
        field_ref, band_refs, (params_ref, padded, out) = refs[0], refs[1:-3], refs[-3:]
        fill_middle(padded, field_ref, band_refs, rows, cols)

        @pl.loop(0, tiles)
        def _(tile):
            taps = [params_ref[tile, pl.ds(t, 1), :] for t in range(KS * KS)]
            start = jnp.broadcast_to(params_ref[tile, pl.ds(KS * KS, 1), :], (cols, LANES))
            sums = tap_sums(padded, tile, taps, [start] * rows, rows, cols, False)
            for row in range(rows):
                out[tile, pl.ds(row * cols, cols), :] = sums[row]

    return call(
        body,
        [shape((tiles, span, LANES), F32), shape((tiles, pixels, LANES), F32)],
        [],
        [field, *bands, params],
        size=8000000,
        limit=16,
    )


def forward_end(partial, sides, params, rows, cols):
    tiles, pixels, _ = partial.shape
    width = tiles * LANES

    def body(partial_ref, first_ref, second_ref, params_ref, acts, standard, inverse, left, right, edge):
        left[...] = jnp.zeros_like(left)
        right[...] = jnp.zeros_like(right)

        @pl.loop(0, tiles)
        def _(tile):
            left_right(edge, (first_ref, second_ref), pl.ds(pl.multiple_of(tile * LANES, LANES), LANES))
            taps = [params_ref[tile, pl.ds(t, 1), :] for t in range(KS * KS)]
            near = [partial_ref[tile, pl.ds(row * cols, 8), :] for row in range(rows)]
            far = [partial_ref[tile, pl.ds((row + 1) * cols - 8, 8), :] for row in range(rows)]
            if cols > 16:
                standard[tile] = partial_ref[tile]
            near, far = side_sums(left, right, edge, taps, near, far, rows, cols, False)
            for row in range(rows):
                standard[tile, pl.ds(row * cols, 8), :] = near[row]
                standard[tile, pl.ds((row + 1) * cols - 8, 8), :] = far[row]

        total = standard[0]
        for tile in range(1, tiles):
            total = total + standard[tile]
        average = jnp.sum(total, axis=1, keepdims=True) * (1.0 / width)
        total = jnp.zeros((pixels, LANES), F32)
        for tile in range(tiles):
            centered = standard[tile] - average
            total = total + centered * centered
        scale = lax.rsqrt(jnp.sum(total, axis=1, keepdims=True) * (1.0 / width) + 1e-06)
        inverse[...] = jnp.broadcast_to(scale, (pixels, LANES))
        for tile in range(tiles):
            value = (standard[tile] - average) * scale
            standard[tile] = value
            gain = params_ref[tile, KS * KS + 1 : KS * KS + 2, :]
            shift = params_ref[tile, KS * KS + 2 : KS * KS + 3, :]
            acts[:, lane_tile(tile)] = (value * gain + shift).astype(BF16)

    return call(
        body,
        [
            shape((pixels, width), BF16),
            shape((tiles, pixels, LANES), F32),
            shape((pixels, LANES), F32),
        ],
        side_scratch(sides, rows, cols),
        [partial, *sides, params],
        size=6000000,
        limit=8,
    )


def with_sides(padded, sides, rows, cols):
    tiles = padded.shape[0]

    def body(padded_ref, first_ref, second_ref, out, edge):
        for tile in range(tiles):
            out[tile] = padded_ref[tile]
            left_right(edge, (first_ref, second_ref), lane_tile(tile))
            for row in range(rows + 2 * MARGIN):
                here = pl.ds(row * MARGIN, MARGIN)
                out[tile, pl.ds(row * PITCH + INSET - MARGIN, MARGIN)] = edge[0, here]
                out[tile, pl.ds(row * PITCH + INSET + cols, MARGIN)] = edge[1, here]

    return call(
        body,
        [shape(padded.shape, F32)],
        [pltpu.VMEM((2, sides[0].shape[0], LANES), F32)],
        [padded, *sides],
        size=2000000,
        limit=8,
    )[0]


def arrays_of(shards):
    arrays, slots = [], []
    for shard in shards:
        places = []
        for array, start, _ in shard:
            known = [index for index, other in enumerate(arrays) if other is array]
            if not known:
                arrays.append(array)
            places.append((known[0] if known else len(arrays) - 1, start))
        slots.append(places)
    return arrays, slots


def hidden_scratch(rows, units, width):
    return [
        pltpu.VMEM((rows, width), BF16),
        pltpu.VMEM((rows, width), BF16),
        pltpu.VMEM((rows, units), F32),
        pltpu.VMEM((rows, units), F32),
        pltpu.VMEM((rows, units), BF16),
    ]


def weight_scratch(units, width):
    return [pltpu.VMEM((units, width), BF16), pltpu.VMEM((units, width), BF16)]


def place_rows(norm, back, normed_refs, up_refs, starts, params_ref):
    pixels = normed_refs[0].shape[0]
    for index, start in enumerate(starts):
        here = slice(index * pixels, (index + 1) * pixels)
        norm[here] = normed_refs[index][...]
        for tile in range(norm.shape[1] // LANES):
            lanes = lane_tile(tile)
            layer = params_ref[tile, KS * KS + 3 : KS * KS + 4, :]
            rows = up_refs[index][start : start + pixels, lanes]
            back[here, lanes] = (rows.astype(F32) * layer).astype(BF16)


def place_weights(win, wout, shard_refs, slots, units):
    for index, (rows_in, rows_out, _) in enumerate(slots):
        here = slice(index * units, (index + 1) * units)
        win[here] = shard_refs[rows_in[0]][rows_in[1] : rows_in[1] + units]
        wout[here] = shard_refs[rows_out[0]][rows_out[1] : rows_out[1] + units]
    lines = [shard_refs[bias[0]][bias[1] : bias[1] + 1, :units].astype(F32) for *_, bias in slots]
    return lines[0] if len(lines) == 1 else jnp.concatenate(lines, axis=1)


def hidden_block(norm, back, win, wout, line, hid, pre, slope, bpre):
    step = 32
    across = (((1,), (1,)), ((), ()))
    pre[...] = lax.dot_general(norm[...], win[...], across, preferred_element_type=F32) + line
    slope[...] = lax.dot_general(back[...], wout[...], across, preferred_element_type=F32)

    @pl.loop(0, norm.shape[0] // step)
    def _(part):
        here = pl.ds(pl.multiple_of(part * step, step), step)
        value = pre[here, :]
        half = 0.5 * (1.0 + lax.erf(value * 0.7071067811865476))
        hid[here, :] = (value * half).astype(BF16)
        bell = jnp.exp(-0.5 * value * value) * 0.3989422804014327
        bpre[here, :] = (slope[here, :] * (half + value * bell)).astype(BF16)

    return jnp.dot(bpre[...], win[...], preferred_element_type=F32)


def hidden_near(normed, upstream, params, shards, units):
    pixels, width = normed[0].shape
    arrays, slots = arrays_of(shards)
    members, count, every = len(normed), len(arrays), len(shards) * units
    rows = members * pixels

    def body(*refs):
        normed_refs, up_refs, params_ref = refs[:members], refs[members : 2 * members], refs[2 * members]
        shard_refs, rest = refs[2 * members + 1 : 2 * members + 1 + count], refs[2 * members + 1 + count :]
        hid, total, win, wout, norm, back, pre, slope, bpre = rest
        place_rows(norm, back, normed_refs, up_refs, [start for _, start in upstream], params_ref)
        line = place_weights(win, wout, shard_refs, slots, units)
        total[...] = hidden_block(norm, back, win, wout, line, hid, pre, slope, bpre)

    return call(
        body,
        [shape((rows, every), BF16), shape((rows, width), F32)],
        weight_scratch(every, width) + hidden_scratch(rows, every, width),
        [*normed, *[array for array, _ in upstream], params, *arrays],
        size=7000000,
        limit=20,
    )


def hidden_far(normed, upstream, params, shards, near_sums, units):
    pixels, width = normed[0].shape
    arrays, slots = arrays_of(shards)
    members, count, every = len(normed), len(arrays), len(shards) * units
    rows = members * pixels

    def body(*refs):
        normed_refs, up_refs, params_ref = refs[:members], refs[members : 2 * members], refs[2 * members]
        shard_refs, rest = refs[2 * members + 1 : 2 * members + 1 + count], refs[2 * members + 1 + count :]
        sum_refs, rest = rest[: len(near_sums)], rest[len(near_sums) :]
        hid, stay, send, win, wout, norm, back, pre, slope, bpre = rest
        place_rows(norm, back, normed_refs, up_refs, [start for _, start in upstream], params_ref)
        line = place_weights(win, wout, shard_refs, slots, units)
        far = hidden_block(norm, back, win, wout, line, hid, pre, slope, bpre)
        near = sum_refs[0][...]
        for ref in sum_refs[1:]:
            near = near + ref[...]
        stay[:pixels] = near[:pixels]
        stay[pixels:] = far[:pixels]
        send[:pixels] = near[pixels:].astype(BF16)
        send[pixels:] = far[pixels:].astype(BF16)

    return call(
        body,
        [shape((rows, every), BF16), shape((rows, width), F32), shape((rows, width), BF16)],
        weight_scratch(every, width) + hidden_scratch(rows, every, width),
        [*normed, *[array for array, _ in upstream], params, *arrays, *near_sums],
        size=8000000,
        limit=28,
    )


def project(hiddens, upstream, shards, units):
    pixels, width = upstream[0][0].shape[0], upstream[0][0].shape[1]
    arrays, slots = arrays_of([[rows_out] for _, rows_out, _ in shards])
    members, count, every = len(upstream), len(arrays), len(shards) * units
    half = members // 2 * pixels
    early, late, _ = hiddens

    def body(early_ref, late_ref, far_ref, *refs):
        up_refs, shard_refs = refs[:members], refs[members : members + count]
        stay, send, scale, wout, hid = refs[members + count :]
        for index, ((slot, start),) in enumerate(slots):
            wout[index * units : (index + 1) * units] = shard_refs[slot][start : start + units]
        hid[:half, : early.shape[1]] = early_ref[...]
        hid[:half, early.shape[1] :] = late_ref[...]
        hid[half:] = far_ref[...]
        projected = jnp.dot(hid[...], wout[...], preferred_element_type=F32)
        stay[:pixels] = projected[:pixels]
        stay[pixels:] = projected[half : half + pixels]
        send[:pixels] = projected[pixels:half].astype(BF16)
        send[pixels:] = projected[half + pixels :].astype(BF16)
        for tile in range(width // LANES):
            lanes = lane_tile(tile)
            sums = jnp.zeros((pixels, LANES), F32)
            for index in range(members):
                rows = projected[index * pixels : (index + 1) * pixels, lanes]
                start = upstream[index][1]
                sums = sums + up_refs[index][start : start + pixels, lanes].astype(F32) * rows
            scale[tile] = jnp.broadcast_to(jnp.sum(sums, axis=0, keepdims=True), (8, LANES))

    return call(
        body,
        [shape((half, width), F32), shape((half, width), BF16), shape((width // LANES, 8, LANES), F32)],
        [pltpu.VMEM((every, width), BF16), pltpu.VMEM((2 * half, every), BF16)],
        [*hiddens, *[array for array, _ in upstream], *arrays],
        size=3911400,
        limit=20,
    )


def pair_sum(mine, peer):
    rows, width = mine.shape
    half = rows // 2

    def body(mine_ref, peer_ref, out):
        out[...] = (mine_ref[half:, :] + peer_ref[half:, :].astype(F32)).astype(BF16)

    return call(body, [shape((half, width), BF16)], [], [mine, peer], size=738000, limit=4)[0]


def norm_backward(own, peer, far, standard, inverse, params, upstream, rows, cols):
    pixels, width = upstream.shape
    tiles = width // LANES
    strip = MARGIN * cols

    def body(own_ref, peer_ref, far_ref, std, inv, params_ref, up_ref, conv, wire, vectors, *sends):
        zero = jnp.zeros((pixels, LANES), F32)
        plain, mixed = zero, zero
        for tile in range(tiles):
            lanes = lane_tile(tile)
            normed = own_ref[:pixels, lanes] + peer_ref[:pixels, lanes].astype(F32) + far_ref[:, lanes].astype(F32)
            gain = params_ref[tile, KS * KS + 1 : KS * KS + 2, :]
            scaled = normed * gain
            product = normed * std[tile]
            conv[tile] = scaled
            plain = plain + scaled
            mixed = mixed + product * gain
            vectors[tile] = jnp.zeros((8, LANES), F32)
            vectors[tile, 1:2, :] = jnp.sum(product, axis=0, keepdims=True)
            vectors[tile, 2:3, :] = jnp.sum(normed, axis=0, keepdims=True)
            out_bias = params_ref[tile, KS * KS + 4 : KS * KS + 5, :]
            vectors[tile, 3:4, :] = jnp.sum(up_ref[:, lanes].astype(F32), axis=0, keepdims=True) * out_bias
        plain = jnp.sum(plain, axis=1, keepdims=True) * (1.0 / width)
        mixed = jnp.sum(mixed, axis=1, keepdims=True) * (1.0 / width)
        for tile in range(tiles):
            value = inv[...] * (conv[tile] - plain - std[tile] * mixed)
            conv[tile] = value
            wire[:, lane_tile(tile)] = value.astype(BF16)
            vectors[tile, 0:1, :] = jnp.sum(value, axis=0, keepdims=True)
        row, _ = grid_place()
        even = row % 2 == 0
        top, bottom = wire[:strip, :], wire[pixels - strip :, :]
        sends[0][...] = jnp.where(even, bottom, top)
        if len(sends) > 1:
            sends[1][...] = jnp.where(even, top, bottom)

    return call(
        body,
        [
            shape((tiles, pixels, LANES), F32),
            shape((pixels, width), BF16),
            shape((tiles, 8, LANES), F32),
        ]
        + [shape((strip, width), BF16)] * row_pairings(),
        [],
        [own, peer, far, standard, inverse, params, upstream],
        size=1845000,
        limit=16,
    )


def block_output(own, peer, far, params, field):
    pixels, width = field.shape

    def body(own_ref, peer_ref, far_ref, params_ref, field_ref, block):
        for tile in range(width // LANES):
            lanes = lane_tile(tile)
            out_bias = params_ref[tile, KS * KS + 4 : KS * KS + 5, :]
            layer = params_ref[tile, KS * KS + 3 : KS * KS + 4, :]
            projected = own_ref[:pixels, lanes] + peer_ref[:pixels, lanes].astype(F32) + far_ref[:, lanes].astype(F32)
            block[:, lanes] = (field_ref[:, lanes].astype(F32) + layer * (projected + out_bias)).astype(BF16)

    return call(
        body,
        [shape((pixels, width), BF16)],
        [],
        [own, peer, far, params, field],
        size=3210300,
        limit=8,
    )[0]


def kernel_gradient(padded, back_conv, vectors, scale_part, rows, cols, groups):
    tiles = back_conv.shape[0]
    share = tiles // groups

    def body(padded_ref, conv, vectors_ref, scale_ref, *refs):
        outs, out = refs[:-1], refs[-1]

        @pl.loop(0, tiles)
        def _(tile):
            grads = [conv[tile, pl.ds(row * cols, cols), :] for row in range(rows)]
            for b in range(KS):
                sums = [None] * KS
                for r in range(rows + 2 * MARGIN):
                    pixels = window(padded_ref, tile, r, b, cols)
                    for a in range(KS):
                        if 0 <= r - a < rows:
                            term = pixels * grads[r - a]
                            sums[a] = term if sums[a] is None else sums[a] + term
                for a in range(KS):
                    out[tile, pl.ds(a * KS + b, 1), :] = jnp.sum(sums[a], axis=0, keepdims=True)
            out[tile, pl.ds(KS * KS, TAP_ROWS - KS * KS), :] = vectors_ref[tile, : TAP_ROWS - KS * KS, :]
            out[tile, pl.ds(KS * KS + 3, 1), :] += scale_ref[tile, :1, :]

        if groups == 1:
            outs[0][...] = out[...]
        else:
            me = lax.axis_index("dp")
            for bits in range(groups):
                for part in range(share):
                    outs[bits][part] = out[(me ^ bits) * share + part]

    return call(
        body,
        [shape((share, TAP_ROWS, LANES), F32)] * groups,
        [pltpu.VMEM((tiles, TAP_ROWS, LANES), F32)],
        [padded, back_conv, vectors, scale_part],
        size=7380000,
        limit=8,
    )


def gradient_middle(wire, bands, params, upstream, rows, cols):
    pixels, width = wire.shape
    tiles = width // LANES
    span = (rows + 2 * MARGIN) * PITCH

    def body(*refs):
        wire_ref, band_refs, (params_ref, up_ref, out, padded) = refs[0], refs[1:-4], refs[-4:]
        fill_middle(padded, wire_ref, band_refs, rows, cols)

        @pl.loop(0, tiles)
        def _(tile):
            lanes = pl.ds(pl.multiple_of(tile * LANES, LANES), LANES)
            taps = [params_ref[tile, pl.ds(t, 1), :] for t in range(KS * KS)]
            start = [up_ref[pl.ds(row * cols, cols), lanes].astype(F32) for row in range(rows)]
            sums = tap_sums(padded, tile, taps, start, rows, cols, True)
            for row in range(rows):
                out[tile, pl.ds(row * cols, cols), :] = sums[row]

    return call(
        body,
        [shape((tiles, pixels, LANES), F32)],
        [pltpu.VMEM((tiles, span, LANES), F32)],
        [wire, *bands, params, upstream],
        size=8000000,
        limit=16,
    )[0]


def gradient_end(partial, sides, params, rows, cols):
    tiles, pixels, _ = partial.shape

    def body(partial_ref, first_ref, second_ref, params_ref, out, left, right, edge):
        left[...] = jnp.zeros_like(left)
        right[...] = jnp.zeros_like(right)

        @pl.loop(0, tiles)
        def _(tile):
            lanes = pl.ds(pl.multiple_of(tile * LANES, LANES), LANES)
            left_right(edge, (first_ref, second_ref), lanes)
            taps = [params_ref[tile, pl.ds(t, 1), :] for t in range(KS * KS)]
            near = [partial_ref[tile, pl.ds(row * cols, 8), :] for row in range(rows)]
            far = [partial_ref[tile, pl.ds((row + 1) * cols - 8, 8), :] for row in range(rows)]
            near, far = side_sums(left, right, edge, taps, near, far, rows, cols, True)
            for row in range(rows):
                middle = partial_ref[tile, pl.ds(row * cols + 8, cols - 16), :] if cols > 16 else None
                whole = [near[row]] + ([middle] if cols > 16 else []) + [far[row]]
                out[pl.ds(row * cols, cols), lanes] = jnp.concatenate(whole).astype(BF16)

    return call(
        body,
        [shape((pixels, tiles * LANES), BF16)],
        side_scratch(sides, rows, cols),
        [partial, *sides, params],
        size=5000000,
        limit=8,
    )[0]


def across(block, bits):
    groups = lax.axis_size("dp")
    return lax.ppermute(block, "dp", [(i, i ^ bits) for i in range(groups)])


def tile_swap(block, bits):
    return lax.ppermute(block, "tile", [(i, i ^ bits) for i in range(lax.axis_size("tile"))])


def place_params(own, joints):
    share, rows, _ = own.shape
    half = rows // 2

    def body(own_ref, *refs):
        joint_refs, out = refs[:-1], refs[-1]
        me = lax.axis_index("dp")
        for part in range(share):
            out[me * share + part] = own_ref[part]
        for bits, ref in enumerate(joint_refs, 1):
            start = ref.shape[0] - PARAM_ROWS
            for part in range(2 * share):
                high = ref[start:, lane_tile(2 * part)].astype(F32)
                value = high + ref[start:, lane_tile(2 * part + 1)].astype(F32)
                out[(me ^ bits) * share + part // 2, pl.ds(part % 2 * half, half), :] = value[:half]

    return call(
        body,
        [shape((4 * share, rows, LANES), F32)],
        [],
        [own, *joints],
        size=738000,
        limit=4,
    )[0]


def gather_params(kernel, vectors):
    own = kernel.shape[1]
    pack = jnp.concatenate([kernel, *vectors, jnp.zeros((TAP_ROWS - KS * KS - len(vectors), own), F32)])
    whole = lax.all_gather(pack, "dp", axis=1, tiled=True)
    return whole.reshape(TAP_ROWS, -1, LANES).transpose(1, 0, 2)


def sum_params(parts, factor):
    flat = parts.transpose(1, 0, 2).reshape(TAP_ROWS, -1)
    sums = lax.psum(lax.psum_scatter(flat, "dp", scatter_dimension=1, tiled=True), "tile") * factor
    taps = KS * KS
    return [sums[:taps]] + [sums[taps + index] for index in range(4)]


def add_blocks(blocks):
    def body(*refs):
        value = refs[0][...]
        for ref in refs[1:-1]:
            value = value + ref[...]
        refs[-1][...] = value

    return call(body, [shape(blocks[0].shape, F32)], [], blocks, size=738000, limit=4)[0]


def finish(total, moved, factor):
    tiles, rows, _ = total.shape
    taps = KS * KS

    def body(*refs):
        outs = refs[1 + len(moved) :]
        for tile in range(tiles):
            value = refs[0][tile]
            for other in refs[1 : 1 + len(moved)]:
                value = value + other[tile]
            value = value * factor
            outs[0][:, lane_tile(tile)] = value[:taps]
            for index in range(4):
                outs[1 + index][:, lane_tile(tile)] = value[taps + index : taps + index + 1]

    taps_sum, *vectors = call(
        body,
        [shape((taps, tiles * LANES), F32)] + [shape((1, tiles * LANES), F32)] * 4,
        [],
        [total, *moved],
        size=2214000,
        limit=4,
    )
    return [taps_sum] + [v.reshape(-1) for v in vectors]


def after(block, *others):
    return lax.optimization_barrier((block, *others))[0]


def pack_shard(rows_in, rows_out, bias):
    units, width = rows_in.shape
    row = jnp.pad(bias.reshape(1, units), ((0, BIAS_ROWS - 1), (0, width - units)))
    return jnp.concatenate([rows_in, rows_out, row])


def first_sends(field, rows_in, rows_out, bias, kernel, vectors, strip):
    pixels, width = field.shape
    units = rows_in.shape[0]
    taps, own = kernel.shape
    half = TAP_ROWS // 2

    def body(bias_ref, field_ref, in_ref, out_ref, kernel_ref, *refs):
        vector_refs, refs = refs[: len(vectors)], refs[len(vectors) :]
        joint, cross, pack, tap_stage, vector_stage, sems = refs
        row, _ = grid_place()
        start = pl.multiple_of((1 - row % 2) * (pixels - strip), 16)
        small = [pltpu.make_async_copy(kernel_ref, tap_stage, sems.at[0])]
        for index, ref in enumerate(vector_refs):
            small.append(pltpu.make_async_copy(ref, vector_stage.at[index], sems.at[1 + index]))
        at = 1 + len(vectors)
        large = [
            pltpu.make_async_copy(field_ref.at[pl.ds(start, strip)], cross.at[pl.ds(0, strip)], sems.at[at]),
            pltpu.make_async_copy(in_ref, joint.at[pl.ds(0, units)], sems.at[at + 1]),
            pltpu.make_async_copy(out_ref, joint.at[pl.ds(units, units)], sems.at[at + 2]),
        ]
        for copy in small + large:
            copy.start()
        line = jnp.concatenate([bias_ref[...].astype(F32), jnp.zeros((1, width - units), F32)], axis=1)
        line = jnp.broadcast_to(line, (BIAS_ROWS, width))
        places = lax.broadcasted_iota(jnp.int32, (BIAS_ROWS, width), 0)
        cross[strip + 2 * units :] = jnp.where(places == 0, line, 0.0).astype(BF16)
        for copy in small:
            copy.wait()
        for tile in range(own // LANES):
            pack[tile, TAP_ROWS - 8 :, :] = jnp.zeros((8, LANES), F32)
            pack[tile, :taps, :] = tap_stage[:, lane_tile(tile)]
            for index in range(len(vectors)):
                pack[tile, taps + index : taps + index + 1, :] = vector_stage[index, :, lane_tile(tile)]
        for part in range(2 * own // LANES):
            value = pack[part // 2, part % 2 * half : (part % 2 + 1) * half, :]
            value = jnp.concatenate([value, jnp.zeros((PARAM_ROWS - half, LANES), F32)])
            high = value.astype(BF16).astype(F32)
            for side, rest in enumerate((high, value - high)):
                lanes = lane_tile(2 * part + side)
                spread = jnp.broadcast_to(line[:1, lanes], (PARAM_ROWS, LANES))
                places = lax.broadcasted_iota(jnp.int32, (PARAM_ROWS, LANES), 0)
                joint[2 * units :, lanes] = jnp.where(places == half, spread, rest).astype(BF16)
        for copy in large:
            copy.wait()
        cross[strip : strip + 2 * units] = joint[: 2 * units]

    outs = [
        shape((2 * units + PARAM_ROWS, width), BF16),
        shape((strip + 2 * units + BIAS_ROWS, width), BF16),
        shape((own // LANES, TAP_ROWS, LANES), F32),
    ]
    args = [bias.reshape(1, units), field, rows_in, rows_out, kernel, *vectors]
    far = pl.BlockSpec(memory_space=pltpu.HBM)
    return pl.pallas_call(
        body,
        out_shape=outs,
        in_specs=[VMEM] + [far] * (len(args) - 1),
        out_specs=[VMEM] * len(outs),
        scratch_shapes=[
            pltpu.VMEM((taps, own), F32),
            pltpu.VMEM((len(vectors), 1, own), F32),
            pltpu.SemaphoreType.DMA((4 + len(vectors),)),
        ],
        compiler_params=pltpu.CompilerParams(vmem_limit_bytes=62 * 1024 * 1024),
        cost_estimate=pl.CostEstimate(flops=10000, bytes_accessed=1000000, transcendentals=0),
    )(*args)


def cut_rows(block, cuts):
    def body(ref, *outs):
        for (start, count), out in zip(cuts, outs):
            out[...] = ref[start : start + count]

    outs = [shape((count, block.shape[1]), block.dtype) for _, count in cuts]
    return call(body, outs, [], [block], size=738000, limit=4)


def row_sends(field, strip):
    row, _ = grid_place()
    starts = [(1 - (row + first) % 2) * (field.shape[0] - strip) for first in range(row_pairings())]
    return [lax.dynamic_slice_in_dim(field, start, strip, 0) for start in starts]


def gathered_shard(in_weight, out_weight, hidden_bias):
    units = in_weight.shape[0]
    groups, count = lax.axis_size("dp"), lax.axis_size("tile")
    place = lax.axis_index("tile")
    member = place % 4

    def mine(array):
        whole = lax.all_gather(array, ("dp", "tile"), axis=0, tiled=True)
        whole = whole.reshape((4, groups * count // 4 * units) + array.shape[1:])
        return lax.dynamic_index_in_dim(whole, member, 0, keepdims=False)

    rows_in, rows_out, bias = mine(in_weight), mine(out_weight), mine(hidden_bias)
    return pack_shard(rows_in, rows_out, bias)


def per_device(
    features,
    cotangent,
    in_weight,
    out_weight,
    hidden_bias,
    kernel,
    conv_bias,
    norm_gain,
    norm_bias,
    layer_scale,
    out_bias,
):
    image_count, _, rows, cols, width = features.shape
    groups, count = lax.axis_size("dp"), lax.axis_size("tile")
    units = in_weight.shape[0]
    pixels = rows * cols
    own = kernel.shape[1]
    strip = MARGIN * cols
    field = features.reshape(pixels, width)
    upstream = cotangent.reshape(pixels, width)

    by_permutes = units % 16 == 0 and groups == 4 and count == 8 and units < width and 4 * own == width
    vectors = [v.reshape(1, own) for v in (conv_bias, norm_gain, norm_bias, layer_scale, out_bias)]
    if by_permutes:
        held, cross, piece = first_sends(field, in_weight, out_weight, hidden_bias, kernel, vectors, strip)
        cross, far_upstream = tile_swap(cross, 4), tile_swap(upstream, 2)
        first, second, far = [across(held, bits) for bits in (1, 2, 3)]
        cross, far_upstream, first, second, far = lax.optimization_barrier(
            (cross, far_upstream, first, second, far)
        )
        params = place_params(piece, [first, second, far])
        bands = cut_rows(cross, [(0, strip)])
        (other,) = cut_rows(cross, [(strip, 2 * units + BIAS_ROWS)])
        other_first, other_second = across(other, 1), across(other, 2)
        (part_in,) = cut_rows(other_first, [(0, units)])
        (part_out,) = cut_rows(other_second, [(units, units + BIAS_ROWS)])
        far_in, far_out = across(part_in, 2), across(part_out, 1)
        after_params = 2 * units + TAP_ROWS // 2
        shards = [
            [(shard, 0, units), (shard, units, units), (shard, after_params, 1)]
            for shard in (held, first, second, far)
        ]
        whole = [(0, units), (units, units), (2 * units, BIAS_ROWS)]
        shards += [[(shard, *rows) for rows in whole] for shard in (other, other_first, other_second)]
        shards.append([(far_in, 0, units), (far_out, 0, units), (far_out, units, BIAS_ROWS)])
    else:
        bands = swap_rows(row_sends(field, strip))
        params = gather_params(kernel, vectors)
        far_upstream = tile_swap(upstream, 2)
        shards = [gathered_shard(in_weight, out_weight, hidden_bias)]
        units = shards[0].shape[0] // 2 - BIAS_ROWS // 2
        shards = [[(shards[0], 0, units), (shards[0], units, units), (shards[0], 2 * units, BIAS_ROWS)]]
    sides = swap_cols(border_columns(field, bands, rows, cols))
    padded, partial = forward_middle(field, bands, params, rows, cols)
    acts, standard, inverse = forward_end(partial, sides, params, rows, cols)
    padded = with_sides(padded, sides, rows, cols)
    near_acts, far_acts = tile_swap(acts, 1), tile_swap(acts, 2)
    near_upstream = tile_swap(upstream, 1)
    early = max(1, len(shards) - 1)
    if by_permutes:
        chip = [(upstream, 0), (near_upstream, 0)]
        near_hidden, near_sum = hidden_near([acts, near_acts], chip, params, shards[:early], units)
        far_acts = after(far_acts, far_in, far_out, padded, near_sum)
    else:
        half = units // 2
        cuts = [[(array, first + at, half) for array, first, _ in shards[0][:2]] for at in (0, half)]
        bias, row, _ = shards[0][2]
        lines = [jnp.pad(bias[row : row + 1, at : at + half], ((0, 0), (0, 0))) for at in (0, half)]
        shards = [[*cut, (line, 0, 1)] for cut, line in zip(cuts, lines)]
        units = half
        chip = [(upstream, 0), (near_upstream, 0)]
        near_hidden, near_sum = hidden_near([acts, near_acts], chip, params, shards[:early], units)
    normed = [acts, near_acts, far_acts, tile_swap(far_acts, 1)]
    upstreams = [*chip, (far_upstream, 0), (tile_swap(far_upstream, 1), 0)]
    late_hidden, late_sum = hidden_near(normed[:2], chip, params, shards[early:], units)
    far_hidden, back_own, back_send = hidden_far(
        normed[2:], upstreams[2:], params, shards, [near_sum, late_sum], units
    )
    hiddens = [near_hidden, late_hidden, far_hidden]

    def group_sum(mine, theirs, *others):
        peer = tile_swap(theirs, 1)
        return mine, peer, tile_swap(after(pair_sum(mine, peer), *others), 2)

    back_sums = group_sum(back_own, back_send)
    out_own, out_send, scale_part = project(hiddens, upstreams, shards, units)
    back_conv, wire, vector_parts, *back_sends = norm_backward(
        *back_sums, standard, inverse, params, upstream, rows, cols
    )
    parts = kernel_gradient(
        padded, back_conv, vector_parts, scale_part, rows, cols, groups if by_permutes else 1
    )
    back_bands = swap_rows([after(send, parts[0]) for send in back_sends])
    back_sides = swap_cols(border_columns(wire, back_bands, rows, cols))
    middle = gradient_middle(wire, back_bands, params, upstream, rows, cols)
    grad = gradient_end(middle, back_sides, params, rows, cols)
    factor = 1.0 / math.sqrt(image_count * groups * count * pixels)
    if by_permutes:
        total = add_blocks([parts[0]] + [across(parts[bits], bits) for bits in range(1, groups)])
        block = block_output(*group_sum(out_own, out_send, total), params, field)
        total = after(total, *back_bands)
        total = add_blocks([total, tile_swap(total, 1)])
        total = after(add_blocks([total, tile_swap(total, 4)]), middle, *back_sides)
        sums = finish(after(total, block, grad), [tile_swap(total, 2)], factor)
    else:
        block = block_output(*group_sum(out_own, out_send), params, field)
        sums = sum_params(parts[0], factor)
    return (block.reshape(features.shape), grad.reshape(features.shape), *sums)


def solution(mesh):
    placed = (
        P("dp", "tile", None, None, None),
        P("dp", "tile", None, None, None),
        P(("dp", "tile"), None),
        P(("dp", "tile"), None),
        P(("dp", "tile")),
        P(None, "dp"),
        P("dp"),
        P("dp"),
        P("dp"),
        P("dp"),
        P("dp"),
    )
    return jax.shard_map(
        per_device,
        mesh=mesh,
        in_specs=placed,
        out_specs=(
            P("dp", "tile", None, None, None),
            P("dp", "tile", None, None, None),
            P(None, "dp"),
            P("dp"),
            P("dp"),
            P("dp"),
            P("dp"),
        ),
        check_vma=False,
    )
```

```python
import math

import jax
import jax.numpy as jnp
from jax import lax
from jax.experimental import pallas as pl
from jax.experimental.pallas import tpu as pltpu
from jax.sharding import PartitionSpec as P

KS = 7
GX = 4
MARGIN = KS // 2
LANES = 128
PITCH = 32
INSET = 8
TAP_ROWS = 56
BIAS_ROWS = 8
PARAM_ROWS = 32
F32 = jnp.float32
BF16 = jnp.bfloat16

VMEM = pl.BlockSpec(memory_space=pltpu.VMEM)


def call(body, outs, scratch, args, flops=0, size=0, aliases=None, limit=32):
    return pl.pallas_call(
        body,
        out_shape=outs,
        in_specs=[VMEM] * len(args),
        out_specs=[VMEM] * len(outs),
        scratch_shapes=scratch,
        input_output_aliases=aliases or {},
        compiler_params=pltpu.CompilerParams(vmem_limit_bytes=limit * 1024 * 1024),
        cost_estimate=pl.CostEstimate(flops=flops, bytes_accessed=size, transcendentals=0),
    )(*args)


def shape(dims, kind):
    return jax.ShapeDtypeStruct(dims, kind)


def lane_tile(tile):
    return slice(tile * LANES, (tile + 1) * LANES)


def grid_place():
    place = lax.axis_index("tile")
    return place // GX, place % GX


def swap_rows(sends):
    count = lax.axis_size("tile")
    grid_rows = count // GX
    moved = []
    for first, block in enumerate(sends):
        route = []
        for place in range(count):
            row = place // GX
            if row % 2 == first and row + 1 < grid_rows:
                route += [(place, place + GX), (place + GX, place)]
        moved.append(lax.ppermute(block, "tile", route))
    return moved


def swap_cols(sends):
    count = lax.axis_size("tile")
    moved = []
    for first, block in enumerate(sends):
        route = []
        for place in range(count):
            col = place % GX
            if col % 2 == first:
                other = place - col + (col + 1) % GX
                route += [(place, other), (other, place)]
        moved.append(lax.ppermute(block, "tile", route))
    return moved


def row_pairings():
    return 1 if lax.axis_size("tile") // GX == 2 else 2


def above_below(bands, tile):
    row, _ = grid_place()
    even = row % 2 == 0
    first = bands[0][:, lane_tile(tile)].astype(F32)
    second = bands[1][:, lane_tile(tile)].astype(F32) if len(bands) > 1 else jnp.zeros_like(first)
    return jnp.where(even, second, first), jnp.where(even, first, second)


def border_columns(field, bands, rows, cols):
    width = field.shape[1]
    tall = rows + 2 * MARGIN
    packed = -(-tall * MARGIN // 16) * 16

    def body(field_ref, *refs):
        band_refs = refs[: len(bands)]
        outs, full, left, right = refs[len(bands) : -3], refs[-3], refs[-2], refs[-1]
        _, col = grid_place()
        even = col % 2 == 0
        left[...] = jnp.zeros_like(left)
        right[...] = jnp.zeros_like(right)
        for tile in range(width // LANES):
            above, below = above_below(band_refs, tile)
            full[: MARGIN * cols] = above
            full[MARGIN * cols : (MARGIN + rows) * cols] = field_ref[:, lane_tile(tile)].astype(F32)
            full[(MARGIN + rows) * cols :] = below
            for row in range(tall):
                here = pl.ds(row * MARGIN, MARGIN)
                left[here] = full[pl.ds(row * cols, MARGIN)]
                right[here] = full[pl.ds(row * cols + cols - MARGIN, MARGIN)]
            toward_left, toward_right = left[...], right[...]
            outs[0][:, lane_tile(tile)] = jnp.where(even, toward_right, toward_left).astype(BF16)
            outs[1][:, lane_tile(tile)] = jnp.where(even, toward_left, toward_right).astype(BF16)

    return call(
        body,
        [shape((packed, width), BF16)] * 2,
        [pltpu.VMEM((tall * cols, LANES), F32)] + [pltpu.VMEM((packed, LANES), F32)] * 2,
        [field, *bands],
        size=1107000,
        limit=8,
    )


def fill_middle(padded, field_ref, band_refs, rows, cols):
    width = field_ref.shape[1]
    for tile in range(width // LANES):
        above, below = above_below(band_refs, tile)
        for row in range(MARGIN):
            source = slice(row * cols, (row + 1) * cols)
            padded[tile, pl.ds(row * PITCH + INSET, cols)] = above[source]
            padded[tile, pl.ds((MARGIN + rows + row) * PITCH + INSET, cols)] = below[source]
        for row in range(rows):
            padded[tile, pl.ds((MARGIN + row) * PITCH + INSET, cols)] = field_ref[
                row * cols : (row + 1) * cols, lane_tile(tile)
            ].astype(F32)
        for row in range(rows + 2 * MARGIN):
            padded[tile, pl.ds(row * PITCH, INSET)] = jnp.zeros((INSET, LANES), F32)
            padded[tile, pl.ds(row * PITCH + INSET + cols, INSET)] = jnp.zeros((INSET, LANES), F32)


def left_right(edge, side_refs, lanes):
    _, col = grid_place()
    even = col % 2 == 0
    inner = (col > 0) & (col < GX - 1)
    first = side_refs[0][:, lanes].astype(F32)
    second = jnp.where(inner, side_refs[1][:, lanes].astype(F32), 0.0)
    edge[0] = jnp.where(even, second, first)
    edge[1] = jnp.where(even, first, second)


def side_sums(left, right, edge, taps, near, far, rows, cols, flipped):
    for row in range(rows + 2 * MARGIN):
        left[pl.ds(row * cols, MARGIN)] = edge[0, pl.ds(row * MARGIN, MARGIN)]
        start = row * cols + cols + MARGIN - 8
        right[pl.ds(start, MARGIN)] = edge[1, pl.ds(row * MARGIN, MARGIN)]
    for side, sums, shifts in ((left, near, range(MARGIN)), (right, far, range(KS - MARGIN, KS))):
        for b in shifts:
            for r in range(rows + 2 * MARGIN):
                pixels = side[pl.ds(r * cols + b, 8)]
                for a in range(KS):
                    if 0 <= r - a < rows:
                        index = (KS - 1 - a) * KS + KS - 1 - b if flipped else a * KS + b
                        sums[r - a] = sums[r - a] + taps[index] * pixels
    return near, far


def side_scratch(sides, rows, cols):
    tall = rows + 2 * MARGIN
    return [pltpu.VMEM((tall * cols + 8, LANES), F32)] * 2 + [pltpu.VMEM((2, sides[0].shape[0], LANES), F32)]


def window(padded, tile, row, shift, cols):
    return padded[tile, pl.ds(row * PITCH + INSET - MARGIN + shift, cols), :]


def tap_sums(padded, tile, taps, sums, rows, cols, flipped):
    for b in range(KS):
        for r in range(rows + 2 * MARGIN):
            pixels = window(padded, tile, r, b, cols)
            for a in range(KS):
                if 0 <= r - a < rows:
                    index = (KS - 1 - a) * KS + KS - 1 - b if flipped else a * KS + b
                    sums[r - a] = sums[r - a] + taps[index] * pixels
    return sums


def forward_middle(field, bands, params, rows, cols):
    pixels, width = field.shape
    tiles = width // LANES
    span = (rows + 2 * MARGIN) * PITCH

    def body(*refs):
        field_ref, band_refs, (params_ref, padded, out) = refs[0], refs[1:-3], refs[-3:]
        fill_middle(padded, field_ref, band_refs, rows, cols)

        @pl.loop(0, tiles)
        def _(tile):
            taps = [params_ref[tile, pl.ds(t, 1), :] for t in range(KS * KS)]
            start = jnp.broadcast_to(params_ref[tile, pl.ds(KS * KS, 1), :], (cols, LANES))
            sums = tap_sums(padded, tile, taps, [start] * rows, rows, cols, False)
            for row in range(rows):
                out[tile, pl.ds(row * cols, cols), :] = sums[row]

    return call(
        body,
        [shape((tiles, span, LANES), F32), shape((tiles, pixels, LANES), F32)],
        [],
        [field, *bands, params],
        size=8000000,
        limit=16,
    )


def forward_end(partial, sides, params, rows, cols):
    tiles, pixels, _ = partial.shape
    width = tiles * LANES

    def body(partial_ref, first_ref, second_ref, params_ref, acts, standard, inverse, left, right, edge):
        left[...] = jnp.zeros_like(left)
        right[...] = jnp.zeros_like(right)

        @pl.loop(0, tiles)
        def _(tile):
            left_right(edge, (first_ref, second_ref), pl.ds(pl.multiple_of(tile * LANES, LANES), LANES))
            taps = [params_ref[tile, pl.ds(t, 1), :] for t in range(KS * KS)]
            near = [partial_ref[tile, pl.ds(row * cols, 8), :] for row in range(rows)]
            far = [partial_ref[tile, pl.ds((row + 1) * cols - 8, 8), :] for row in range(rows)]
            if cols > 16:
                standard[tile] = partial_ref[tile]
            near, far = side_sums(left, right, edge, taps, near, far, rows, cols, False)
            for row in range(rows):
                standard[tile, pl.ds(row * cols, 8), :] = near[row]
                standard[tile, pl.ds((row + 1) * cols - 8, 8), :] = far[row]

        total = standard[0]
        for tile in range(1, tiles):
            total = total + standard[tile]
        average = jnp.sum(total, axis=1, keepdims=True) * (1.0 / width)
        total = jnp.zeros((pixels, LANES), F32)
        for tile in range(tiles):
            centered = standard[tile] - average
            total = total + centered * centered
        scale = lax.rsqrt(jnp.sum(total, axis=1, keepdims=True) * (1.0 / width) + 1e-06)
        inverse[...] = jnp.broadcast_to(scale, (pixels, LANES))
        for tile in range(tiles):
            value = (standard[tile] - average) * scale
            standard[tile] = value
            gain = params_ref[tile, KS * KS + 1 : KS * KS + 2, :]
            shift = params_ref[tile, KS * KS + 2 : KS * KS + 3, :]
            acts[:, lane_tile(tile)] = (value * gain + shift).astype(BF16)

    return call(
        body,
        [
            shape((pixels, width), BF16),
            shape((tiles, pixels, LANES), F32),
            shape((pixels, LANES), F32),
        ],
        side_scratch(sides, rows, cols),
        [partial, *sides, params],
        size=6000000,
        limit=8,
    )


def with_sides(padded, sides, rows, cols):
    tiles = padded.shape[0]

    def body(padded_ref, first_ref, second_ref, out, edge):
        for tile in range(tiles):
            out[tile] = padded_ref[tile]
            left_right(edge, (first_ref, second_ref), lane_tile(tile))
            for row in range(rows + 2 * MARGIN):
                here = pl.ds(row * MARGIN, MARGIN)
                out[tile, pl.ds(row * PITCH + INSET - MARGIN, MARGIN)] = edge[0, here]
                out[tile, pl.ds(row * PITCH + INSET + cols, MARGIN)] = edge[1, here]

    return call(
        body,
        [shape(padded.shape, F32)],
        [pltpu.VMEM((2, sides[0].shape[0], LANES), F32)],
        [padded, *sides],
        size=2000000,
        limit=8,
    )[0]


def arrays_of(shards):
    arrays, slots = [], []
    for shard in shards:
        places = []
        for array, start, _ in shard:
            known = [index for index, other in enumerate(arrays) if other is array]
            if not known:
                arrays.append(array)
            places.append((known[0] if known else len(arrays) - 1, start))
        slots.append(places)
    return arrays, slots


def hidden_scratch(rows, units, width):
    return [
        pltpu.VMEM((rows, width), BF16),
        pltpu.VMEM((rows, width), BF16),
        pltpu.VMEM((rows, units), F32),
        pltpu.VMEM((rows, units), F32),
        pltpu.VMEM((rows, units), BF16),
    ]


def weight_scratch(units, width):
    return [pltpu.VMEM((units, width), BF16), pltpu.VMEM((units, width), BF16)]


def place_rows(norm, back, normed_refs, up_refs, starts, params_ref):
    pixels = normed_refs[0].shape[0]
    for index, start in enumerate(starts):
        here = slice(index * pixels, (index + 1) * pixels)
        norm[here] = normed_refs[index][...]
        for tile in range(norm.shape[1] // LANES):
            lanes = lane_tile(tile)
            layer = params_ref[tile, KS * KS + 3 : KS * KS + 4, :]
            rows = up_refs[index][start : start + pixels, lanes]
            back[here, lanes] = (rows.astype(F32) * layer).astype(BF16)


def place_weights(win, wout, shard_refs, slots, units):
    for index, (rows_in, rows_out, _) in enumerate(slots):
        here = slice(index * units, (index + 1) * units)
        win[here] = shard_refs[rows_in[0]][rows_in[1] : rows_in[1] + units]
        wout[here] = shard_refs[rows_out[0]][rows_out[1] : rows_out[1] + units]
    lines = [shard_refs[bias[0]][bias[1] : bias[1] + 1, :units].astype(F32) for *_, bias in slots]
    return lines[0] if len(lines) == 1 else jnp.concatenate(lines, axis=1)


def hidden_block(norm, back, win, wout, line, hid, pre, slope, bpre):
    step = 16
    across = (((1,), (1,)), ((), ()))
    pre[...] = lax.dot_general(norm[...], win[...], across, preferred_element_type=F32) + line
    slope[...] = lax.dot_general(back[...], wout[...], across, preferred_element_type=F32)

    @pl.loop(0, norm.shape[0] // step)
    def _(part):
        here = pl.ds(pl.multiple_of(part * step, step), step)
        value = pre[here, :]
        half = 0.5 * (1.0 + lax.erf(value * 0.7071067811865476))
        hid[here, :] = (value * half).astype(BF16)
        bell = jnp.exp(-0.5 * value * value) * 0.3989422804014327
        bpre[here, :] = (slope[here, :] * (half + value * bell)).astype(BF16)

    return jnp.dot(bpre[...], win[...], preferred_element_type=F32)


def hidden_near(normed, upstream, params, shards, units):
    pixels, width = normed[0].shape
    arrays, slots = arrays_of(shards)
    members, count, every = len(normed), len(arrays), len(shards) * units
    rows = members * pixels

    def body(*refs):
        normed_refs, up_refs, params_ref = refs[:members], refs[members : 2 * members], refs[2 * members]
        shard_refs, rest = refs[2 * members + 1 : 2 * members + 1 + count], refs[2 * members + 1 + count :]
        hid, total, win, wout, norm, back, pre, slope, bpre = rest
        place_rows(norm, back, normed_refs, up_refs, [start for _, start in upstream], params_ref)
        line = place_weights(win, wout, shard_refs, slots, units)
        total[...] = hidden_block(norm, back, win, wout, line, hid, pre, slope, bpre)

    return call(
        body,
        [shape((rows, every), BF16), shape((rows, width), F32)],
        weight_scratch(every, width) + hidden_scratch(rows, every, width),
        [*normed, *[array for array, _ in upstream], params, *arrays],
        size=7000000,
        limit=20,
    )


def hidden_far(normed, upstream, params, shards, near_sums, units):
    pixels, width = normed[0].shape
    arrays, slots = arrays_of(shards)
    members, count, every = len(normed), len(arrays), len(shards) * units
    rows = members * pixels

    def body(*refs):
        normed_refs, up_refs, params_ref = refs[:members], refs[members : 2 * members], refs[2 * members]
        shard_refs, rest = refs[2 * members + 1 : 2 * members + 1 + count], refs[2 * members + 1 + count :]
        sum_refs, rest = rest[: len(near_sums)], rest[len(near_sums) :]
        hid, stay, send, win, wout, norm, back, pre, slope, bpre = rest
        place_rows(norm, back, normed_refs, up_refs, [start for _, start in upstream], params_ref)
        line = place_weights(win, wout, shard_refs, slots, units)
        far = hidden_block(norm, back, win, wout, line, hid, pre, slope, bpre)
        near = sum_refs[0][...]
        for ref in sum_refs[1:]:
            near = near + ref[...]
        stay[:pixels] = near[:pixels]
        stay[pixels:] = far[:pixels]
        send[:pixels] = near[pixels:].astype(BF16)
        send[pixels:] = far[pixels:].astype(BF16)

    return call(
        body,
        [shape((rows, every), BF16), shape((rows, width), F32), shape((rows, width), BF16)],
        weight_scratch(every, width) + hidden_scratch(rows, every, width),
        [*normed, *[array for array, _ in upstream], params, *arrays, *near_sums],
        size=8000000,
        limit=28,
    )


def project(hiddens, upstream, shards, units):
    pixels, width = upstream[0][0].shape[0], upstream[0][0].shape[1]
    arrays, slots = arrays_of([[rows_out] for _, rows_out, _ in shards])
    members, count, every = len(upstream), len(arrays), len(shards) * units
    half = members // 2 * pixels
    early, late, _ = hiddens

    def body(early_ref, late_ref, far_ref, *refs):
        up_refs, shard_refs = refs[:members], refs[members : members + count]
        stay, send, scale, wout, hid = refs[members + count :]
        for index, ((slot, start),) in enumerate(slots):
            wout[index * units : (index + 1) * units] = shard_refs[slot][start : start + units]
        hid[:half, : early.shape[1]] = early_ref[...]
        hid[:half, early.shape[1] :] = late_ref[...]
        hid[half:] = far_ref[...]
        projected = jnp.dot(hid[...], wout[...], preferred_element_type=F32)
        stay[:pixels] = projected[:pixels]
        stay[pixels:] = projected[half : half + pixels]
        send[:pixels] = projected[pixels:half].astype(BF16)
        send[pixels:] = projected[half + pixels :].astype(BF16)
        for tile in range(width // LANES):
            lanes = lane_tile(tile)
            sums = jnp.zeros((pixels, LANES), F32)
            for index in range(members):
                rows = projected[index * pixels : (index + 1) * pixels, lanes]
                start = upstream[index][1]
                sums = sums + up_refs[index][start : start + pixels, lanes].astype(F32) * rows
            scale[tile] = jnp.broadcast_to(jnp.sum(sums, axis=0, keepdims=True), (8, LANES))

    return call(
        body,
        [shape((half, width), F32), shape((half, width), BF16), shape((width // LANES, 8, LANES), F32)],
        [pltpu.VMEM((every, width), BF16), pltpu.VMEM((2 * half, every), BF16)],
        [*hiddens, *[array for array, _ in upstream], *arrays],
        size=3911400,
        limit=20,
    )


def pair_sum(mine, peer):
    rows, width = mine.shape
    half = rows // 2

    def body(mine_ref, peer_ref, out):
        out[...] = (mine_ref[half:, :] + peer_ref[half:, :].astype(F32)).astype(BF16)

    return call(body, [shape((half, width), BF16)], [], [mine, peer], size=738000, limit=4)[0]


def norm_backward(own, peer, far, standard, inverse, params, upstream, rows, cols):
    pixels, width = upstream.shape
    tiles = width // LANES
    strip = MARGIN * cols

    def body(own_ref, peer_ref, far_ref, std, inv, params_ref, up_ref, conv, wire, vectors, *sends):
        zero = jnp.zeros((pixels, LANES), F32)
        plain, mixed = zero, zero
        for tile in range(tiles):
            lanes = lane_tile(tile)
            normed = own_ref[:pixels, lanes] + peer_ref[:pixels, lanes].astype(F32) + far_ref[:, lanes].astype(F32)
            gain = params_ref[tile, KS * KS + 1 : KS * KS + 2, :]
            scaled = normed * gain
            product = normed * std[tile]
            conv[tile] = scaled
            plain = plain + scaled
            mixed = mixed + product * gain
            vectors[tile] = jnp.zeros((8, LANES), F32)
            vectors[tile, 1:2, :] = jnp.sum(product, axis=0, keepdims=True)
            vectors[tile, 2:3, :] = jnp.sum(normed, axis=0, keepdims=True)
            out_bias = params_ref[tile, KS * KS + 4 : KS * KS + 5, :]
            vectors[tile, 3:4, :] = jnp.sum(up_ref[:, lanes].astype(F32), axis=0, keepdims=True) * out_bias
        plain = jnp.sum(plain, axis=1, keepdims=True) * (1.0 / width)
        mixed = jnp.sum(mixed, axis=1, keepdims=True) * (1.0 / width)
        for tile in range(tiles):
            value = inv[...] * (conv[tile] - plain - std[tile] * mixed)
            conv[tile] = value
            wire[:, lane_tile(tile)] = value.astype(BF16)
            vectors[tile, 0:1, :] = jnp.sum(value, axis=0, keepdims=True)
        row, _ = grid_place()
        even = row % 2 == 0
        top, bottom = wire[:strip, :], wire[pixels - strip :, :]
        sends[0][...] = jnp.where(even, bottom, top)
        if len(sends) > 1:
            sends[1][...] = jnp.where(even, top, bottom)

    return call(
        body,
        [
            shape((tiles, pixels, LANES), F32),
            shape((pixels, width), BF16),
            shape((tiles, 8, LANES), F32),
        ]
        + [shape((strip, width), BF16)] * row_pairings(),
        [],
        [own, peer, far, standard, inverse, params, upstream],
        size=1845000,
        limit=16,
    )


def block_output(own, peer, far, params, field):
    pixels, width = field.shape

    def body(own_ref, peer_ref, far_ref, params_ref, field_ref, block):
        for tile in range(width // LANES):
            lanes = lane_tile(tile)
            out_bias = params_ref[tile, KS * KS + 4 : KS * KS + 5, :]
            layer = params_ref[tile, KS * KS + 3 : KS * KS + 4, :]
            projected = own_ref[:pixels, lanes] + peer_ref[:pixels, lanes].astype(F32) + far_ref[:, lanes].astype(F32)
            block[:, lanes] = (field_ref[:, lanes].astype(F32) + layer * (projected + out_bias)).astype(BF16)

    return call(
        body,
        [shape((pixels, width), BF16)],
        [],
        [own, peer, far, params, field],
        size=3210300,
        limit=8,
    )[0]


def kernel_gradient(padded, back_conv, vectors, scale_part, rows, cols, groups):
    tiles = back_conv.shape[0]
    share = tiles // groups

    def body(padded_ref, conv, vectors_ref, scale_ref, *refs):
        outs, out = refs[:-1], refs[-1]

        @pl.loop(0, tiles)
        def _(tile):
            grads = [conv[tile, pl.ds(row * cols, cols), :] for row in range(rows)]
            for b in range(KS):
                sums = [None] * KS
                for r in range(rows + 2 * MARGIN):
                    pixels = window(padded_ref, tile, r, b, cols)
                    for a in range(KS):
                        if 0 <= r - a < rows:
                            term = pixels * grads[r - a]
                            sums[a] = term if sums[a] is None else sums[a] + term
                for a in range(KS):
                    out[tile, pl.ds(a * KS + b, 1), :] = jnp.sum(sums[a], axis=0, keepdims=True)
            out[tile, pl.ds(KS * KS, TAP_ROWS - KS * KS), :] = vectors_ref[tile, : TAP_ROWS - KS * KS, :]
            out[tile, pl.ds(KS * KS + 3, 1), :] += scale_ref[tile, :1, :]

        if groups == 1:
            outs[0][...] = out[...]
        else:
            me = lax.axis_index("dp")
            for bits in range(groups):
                for part in range(share):
                    outs[bits][part] = out[(me ^ bits) * share + part]

    return call(
        body,
        [shape((share, TAP_ROWS, LANES), F32)] * groups,
        [pltpu.VMEM((tiles, TAP_ROWS, LANES), F32)],
        [padded, back_conv, vectors, scale_part],
        size=7380000,
        limit=8,
    )


def gradient_middle(wire, bands, params, upstream, rows, cols):
    pixels, width = wire.shape
    tiles = width // LANES
    span = (rows + 2 * MARGIN) * PITCH

    def body(*refs):
        wire_ref, band_refs, (params_ref, up_ref, out, padded) = refs[0], refs[1:-4], refs[-4:]
        fill_middle(padded, wire_ref, band_refs, rows, cols)

        @pl.loop(0, tiles)
        def _(tile):
            lanes = pl.ds(pl.multiple_of(tile * LANES, LANES), LANES)
            taps = [params_ref[tile, pl.ds(t, 1), :] for t in range(KS * KS)]
            start = [up_ref[pl.ds(row * cols, cols), lanes].astype(F32) for row in range(rows)]
            sums = tap_sums(padded, tile, taps, start, rows, cols, True)
            for row in range(rows):
                out[tile, pl.ds(row * cols, cols), :] = sums[row]

    return call(
        body,
        [shape((tiles, pixels, LANES), F32)],
        [pltpu.VMEM((tiles, span, LANES), F32)],
        [wire, *bands, params, upstream],
        size=8000000,
        limit=16,
    )[0]


def gradient_end(partial, sides, params, rows, cols):
    tiles, pixels, _ = partial.shape

    def body(partial_ref, first_ref, second_ref, params_ref, out, left, right, edge):
        left[...] = jnp.zeros_like(left)
        right[...] = jnp.zeros_like(right)

        @pl.loop(0, tiles)
        def _(tile):
            lanes = pl.ds(pl.multiple_of(tile * LANES, LANES), LANES)
            left_right(edge, (first_ref, second_ref), lanes)
            taps = [params_ref[tile, pl.ds(t, 1), :] for t in range(KS * KS)]
            near = [partial_ref[tile, pl.ds(row * cols, 8), :] for row in range(rows)]
            far = [partial_ref[tile, pl.ds((row + 1) * cols - 8, 8), :] for row in range(rows)]
            near, far = side_sums(left, right, edge, taps, near, far, rows, cols, True)
            for row in range(rows):
                middle = partial_ref[tile, pl.ds(row * cols + 8, cols - 16), :] if cols > 16 else None
                whole = [near[row]] + ([middle] if cols > 16 else []) + [far[row]]
                out[pl.ds(row * cols, cols), lanes] = jnp.concatenate(whole).astype(BF16)

    return call(
        body,
        [shape((pixels, tiles * LANES), BF16)],
        side_scratch(sides, rows, cols),
        [partial, *sides, params],
        size=5000000,
        limit=8,
    )[0]


def across(block, bits):
    groups = lax.axis_size("dp")
    return lax.ppermute(block, "dp", [(i, i ^ bits) for i in range(groups)])


def tile_swap(block, bits):
    return lax.ppermute(block, "tile", [(i, i ^ bits) for i in range(lax.axis_size("tile"))])


def place_params(own, joints):
    share, rows, _ = own.shape
    half = rows // 2

    def body(own_ref, *refs):
        joint_refs, out = refs[:-1], refs[-1]
        me = lax.axis_index("dp")
        for part in range(share):
            out[me * share + part] = own_ref[part]
        for bits, ref in enumerate(joint_refs, 1):
            start = ref.shape[0] - PARAM_ROWS
            for part in range(2 * share):
                high = ref[start:, lane_tile(2 * part)].astype(F32)
                value = high + ref[start:, lane_tile(2 * part + 1)].astype(F32)
                out[(me ^ bits) * share + part // 2, pl.ds(part % 2 * half, half), :] = value[:half]

    return call(
        body,
        [shape((4 * share, rows, LANES), F32)],
        [],
        [own, *joints],
        size=738000,
        limit=4,
    )[0]


def gather_params(kernel, vectors):
    own = kernel.shape[1]
    pack = jnp.concatenate([kernel, *vectors, jnp.zeros((TAP_ROWS - KS * KS - len(vectors), own), F32)])
    whole = lax.all_gather(pack, "dp", axis=1, tiled=True)
    return whole.reshape(TAP_ROWS, -1, LANES).transpose(1, 0, 2)


def sum_params(parts, factor):
    flat = parts.transpose(1, 0, 2).reshape(TAP_ROWS, -1)
    sums = lax.psum(lax.psum_scatter(flat, "dp", scatter_dimension=1, tiled=True), "tile") * factor
    taps = KS * KS
    return [sums[:taps]] + [sums[taps + index] for index in range(4)]


def add_blocks(blocks):
    def body(*refs):
        value = refs[0][...]
        for ref in refs[1:-1]:
            value = value + ref[...]
        refs[-1][...] = value

    return call(body, [shape(blocks[0].shape, F32)], [], blocks, size=738000, limit=4)[0]


def finish(total, moved, factor):
    tiles, rows, _ = total.shape
    taps = KS * KS

    def body(*refs):
        outs = refs[1 + len(moved) :]
        for tile in range(tiles):
            value = refs[0][tile]
            for other in refs[1 : 1 + len(moved)]:
                value = value + other[tile]
            value = value * factor
            outs[0][:, lane_tile(tile)] = value[:taps]
            for index in range(4):
                outs[1 + index][:, lane_tile(tile)] = value[taps + index : taps + index + 1]

    taps_sum, *vectors = call(
        body,
        [shape((taps, tiles * LANES), F32)] + [shape((1, tiles * LANES), F32)] * 4,
        [],
        [total, *moved],
        size=2214000,
        limit=4,
    )
    return [taps_sum] + [v.reshape(-1) for v in vectors]


def after(block, *others):
    return lax.optimization_barrier((block, *others))[0]


def pack_shard(rows_in, rows_out, bias):
    units, width = rows_in.shape
    row = jnp.pad(bias.reshape(1, units), ((0, BIAS_ROWS - 1), (0, width - units)))
    return jnp.concatenate([rows_in, rows_out, row])


def first_sends(field, rows_in, rows_out, bias, kernel, vectors, strip):
    pixels, width = field.shape
    units = rows_in.shape[0]
    taps, own = kernel.shape
    half = TAP_ROWS // 2

    def body(bias_ref, field_ref, in_ref, out_ref, kernel_ref, *refs):
        vector_refs, refs = refs[: len(vectors)], refs[len(vectors) :]
        joint, cross, pack, tap_stage, vector_stage, sems = refs
        row, _ = grid_place()
        start = pl.multiple_of((1 - row % 2) * (pixels - strip), 16)
        small = [pltpu.make_async_copy(kernel_ref, tap_stage, sems.at[0])]
        for index, ref in enumerate(vector_refs):
            small.append(pltpu.make_async_copy(ref, vector_stage.at[index], sems.at[1 + index]))
        at = 1 + len(vectors)
        large = [
            pltpu.make_async_copy(field_ref.at[pl.ds(start, strip)], cross.at[pl.ds(0, strip)], sems.at[at]),
            pltpu.make_async_copy(in_ref, joint.at[pl.ds(0, units)], sems.at[at + 1]),
            pltpu.make_async_copy(out_ref, joint.at[pl.ds(units, units)], sems.at[at + 2]),
        ]
        for copy in small + large:
            copy.start()
        line = jnp.concatenate([bias_ref[...].astype(F32), jnp.zeros((1, width - units), F32)], axis=1)
        line = jnp.broadcast_to(line, (BIAS_ROWS, width))
        places = lax.broadcasted_iota(jnp.int32, (BIAS_ROWS, width), 0)
        cross[strip + 2 * units :] = jnp.where(places == 0, line, 0.0).astype(BF16)
        for copy in small:
            copy.wait()
        for tile in range(own // LANES):
            pack[tile, TAP_ROWS - 8 :, :] = jnp.zeros((8, LANES), F32)
            pack[tile, :taps, :] = tap_stage[:, lane_tile(tile)]
            for index in range(len(vectors)):
                pack[tile, taps + index : taps + index + 1, :] = vector_stage[index, :, lane_tile(tile)]
        for part in range(2 * own // LANES):
            value = pack[part // 2, part % 2 * half : (part % 2 + 1) * half, :]
            value = jnp.concatenate([value, jnp.zeros((PARAM_ROWS - half, LANES), F32)])
            high = value.astype(BF16).astype(F32)
            for side, rest in enumerate((high, value - high)):
                lanes = lane_tile(2 * part + side)
                spread = jnp.broadcast_to(line[:1, lanes], (PARAM_ROWS, LANES))
                places = lax.broadcasted_iota(jnp.int32, (PARAM_ROWS, LANES), 0)
                joint[2 * units :, lanes] = jnp.where(places == half, spread, rest).astype(BF16)
        for copy in large:
            copy.wait()
        cross[strip : strip + 2 * units] = joint[: 2 * units]

    outs = [
        shape((2 * units + PARAM_ROWS, width), BF16),
        shape((strip + 2 * units + BIAS_ROWS, width), BF16),
        shape((own // LANES, TAP_ROWS, LANES), F32),
    ]
    args = [bias.reshape(1, units), field, rows_in, rows_out, kernel, *vectors]
    far = pl.BlockSpec(memory_space=pltpu.HBM)
    return pl.pallas_call(
        body,
        out_shape=outs,
        in_specs=[VMEM] + [far] * (len(args) - 1),
        out_specs=[VMEM] * len(outs),
        scratch_shapes=[
            pltpu.VMEM((taps, own), F32),
            pltpu.VMEM((len(vectors), 1, own), F32),
            pltpu.SemaphoreType.DMA((4 + len(vectors),)),
        ],
        compiler_params=pltpu.CompilerParams(vmem_limit_bytes=62 * 1024 * 1024),
        cost_estimate=pl.CostEstimate(flops=10000, bytes_accessed=1000000, transcendentals=0),
    )(*args)


def cut_rows(block, cuts):
    def body(ref, *outs):
        for (start, count), out in zip(cuts, outs):
            out[...] = ref[start : start + count]

    outs = [shape((count, block.shape[1]), block.dtype) for _, count in cuts]
    return call(body, outs, [], [block], size=738000, limit=4)


def row_sends(field, strip):
    row, _ = grid_place()
    starts = [(1 - (row + first) % 2) * (field.shape[0] - strip) for first in range(row_pairings())]
    return [lax.dynamic_slice_in_dim(field, start, strip, 0) for start in starts]


def gathered_shard(in_weight, out_weight, hidden_bias):
    units = in_weight.shape[0]
    groups, count = lax.axis_size("dp"), lax.axis_size("tile")
    place = lax.axis_index("tile")
    member = place % 4

    def mine(array):
        whole = lax.all_gather(array, ("dp", "tile"), axis=0, tiled=True)
        whole = whole.reshape((4, groups * count // 4 * units) + array.shape[1:])
        return lax.dynamic_index_in_dim(whole, member, 0, keepdims=False)

    rows_in, rows_out, bias = mine(in_weight), mine(out_weight), mine(hidden_bias)
    return pack_shard(rows_in, rows_out, bias)


def per_device(
    features,
    cotangent,
    in_weight,
    out_weight,
    hidden_bias,
    kernel,
    conv_bias,
    norm_gain,
    norm_bias,
    layer_scale,
    out_bias,
):
    image_count, _, rows, cols, width = features.shape
    groups, count = lax.axis_size("dp"), lax.axis_size("tile")
    units = in_weight.shape[0]
    pixels = rows * cols
    own = kernel.shape[1]
    strip = MARGIN * cols
    field = features.reshape(pixels, width)
    upstream = cotangent.reshape(pixels, width)

    by_permutes = units % 16 == 0 and groups == 4 and count == 8 and units < width and 4 * own == width
    vectors = [v.reshape(1, own) for v in (conv_bias, norm_gain, norm_bias, layer_scale, out_bias)]
    if by_permutes:
        held, cross, piece = first_sends(field, in_weight, out_weight, hidden_bias, kernel, vectors, strip)
        cross, far_upstream = tile_swap(cross, 4), tile_swap(upstream, 2)
        first, second, far = [across(held, bits) for bits in (1, 2, 3)]
        cross, far_upstream, first, second, far = lax.optimization_barrier(
            (cross, far_upstream, first, second, far)
        )
        params = place_params(piece, [first, second, far])
        bands = cut_rows(cross, [(0, strip)])
        (other,) = cut_rows(cross, [(strip, 2 * units + BIAS_ROWS)])
        other_first, other_second = across(other, 1), across(other, 2)
        (part_in,) = cut_rows(other_first, [(0, units)])
        (part_out,) = cut_rows(other_second, [(units, units + BIAS_ROWS)])
        far_in, far_out = across(part_in, 2), across(part_out, 1)
        after_params = 2 * units + TAP_ROWS // 2
        shards = [
            [(shard, 0, units), (shard, units, units), (shard, after_params, 1)]
            for shard in (held, first, second, far)
        ]
        whole = [(0, units), (units, units), (2 * units, BIAS_ROWS)]
        shards += [[(shard, *rows) for rows in whole] for shard in (other, other_first, other_second)]
        shards.append([(far_in, 0, units), (far_out, 0, units), (far_out, units, BIAS_ROWS)])
    else:
        bands = swap_rows(row_sends(field, strip))
        params = gather_params(kernel, vectors)
        far_upstream = tile_swap(upstream, 2)
        shards = [gathered_shard(in_weight, out_weight, hidden_bias)]
        units = shards[0].shape[0] // 2 - BIAS_ROWS // 2
        shards = [[(shards[0], 0, units), (shards[0], units, units), (shards[0], 2 * units, BIAS_ROWS)]]
    sides = swap_cols(border_columns(field, bands, rows, cols))
    padded, partial = forward_middle(field, bands, params, rows, cols)
    acts, standard, inverse = forward_end(partial, sides, params, rows, cols)
    padded = with_sides(padded, sides, rows, cols)
    near_acts, far_acts = tile_swap(acts, 1), tile_swap(acts, 2)
    near_upstream = tile_swap(upstream, 1)
    early = max(1, len(shards) - 1)
    if by_permutes:
        chip = [(upstream, 0), (near_upstream, 0)]
        near_hidden, near_sum = hidden_near([acts, near_acts], chip, params, shards[:early], units)
        far_acts = after(far_acts, far_in, far_out, padded, near_sum)
    else:
        half = units // 2
        cuts = [[(array, first + at, half) for array, first, _ in shards[0][:2]] for at in (0, half)]
        bias, row, _ = shards[0][2]
        lines = [jnp.pad(bias[row : row + 1, at : at + half], ((0, 0), (0, 0))) for at in (0, half)]
        shards = [[*cut, (line, 0, 1)] for cut, line in zip(cuts, lines)]
        units = half
        chip = [(upstream, 0), (near_upstream, 0)]
        near_hidden, near_sum = hidden_near([acts, near_acts], chip, params, shards[:early], units)
    normed = [acts, near_acts, far_acts, tile_swap(far_acts, 1)]
    upstreams = [*chip, (far_upstream, 0), (tile_swap(far_upstream, 1), 0)]
    late_hidden, late_sum = hidden_near(normed[:2], chip, params, shards[early:], units)
    far_hidden, back_own, back_send = hidden_far(
        normed[2:], upstreams[2:], params, shards, [near_sum, late_sum], units
    )
    hiddens = [near_hidden, late_hidden, far_hidden]

    def group_sum(mine, theirs, *others):
        peer = tile_swap(theirs, 1)
        return mine, peer, tile_swap(after(pair_sum(mine, peer), *others), 2)

    back_sums = group_sum(back_own, back_send)
    out_own, out_send, scale_part = project(hiddens, upstreams, shards, units)
    back_conv, wire, vector_parts, *back_sends = norm_backward(
        *back_sums, standard, inverse, params, upstream, rows, cols
    )
    parts = kernel_gradient(
        padded, back_conv, vector_parts, scale_part, rows, cols, groups if by_permutes else 1
    )
    back_bands = swap_rows([after(send, parts[0]) for send in back_sends])
    back_sides = swap_cols(border_columns(wire, back_bands, rows, cols))
    middle = gradient_middle(wire, back_bands, params, upstream, rows, cols)
    grad = gradient_end(middle, back_sides, params, rows, cols)
    factor = 1.0 / math.sqrt(image_count * groups * count * pixels)
    if by_permutes:
        total = add_blocks([parts[0]] + [across(parts[bits], bits) for bits in range(1, groups)])
        block = block_output(*group_sum(out_own, out_send, total), params, field)
        total = after(total, *back_bands)
        total = add_blocks([total, tile_swap(total, 1)])
        total = after(add_blocks([total, tile_swap(total, 4)]), middle, *back_sides)
        sums = finish(after(total, block, grad), [tile_swap(total, 2)], factor)
    else:
        block = block_output(*group_sum(out_own, out_send), params, field)
        sums = sum_params(parts[0], factor)
    return (block.reshape(features.shape), grad.reshape(features.shape), *sums)


def solution(mesh):
    placed = (
        P("dp", "tile", None, None, None),
        P("dp", "tile", None, None, None),
        P(("dp", "tile"), None),
        P(("dp", "tile"), None),
        P(("dp", "tile")),
        P(None, "dp"),
        P("dp"),
        P("dp"),
        P("dp"),
        P("dp"),
        P("dp"),
    )
    return jax.shard_map(
        per_device,
        mesh=mesh,
        in_specs=placed,
        out_specs=(
            P("dp", "tile", None, None, None),
            P("dp", "tile", None, None, None),
            P(None, "dp"),
            P("dp"),
            P("dp"),
            P("dp"),
            P("dp"),
        ),
        check_vma=False,
    )
```
